256 devices in a mesh: sec: 8 (over y, x_lo), ty: 4 (over x_hi, core), tx: 8 (over z).
Axes of the slice: x: 4 (x_hi: 2, x_lo: 2; x = x_hi * 2 + x_lo), y: 4, z: 8, core: 2. Of those that a mesh axis runs over, the one named last changes fastest.
Arguments:
- images: float32 [8, 1024, 4096], P('sec', 'ty', 'tx'), may hold values from -12 to 12
Outputs:
- relaxed: float32 [8, 2, 16, 64], P('sec', None, 'ty', 'tx')
- cumulative: float32 [8, 2, 16, 64], P('sec', None, 'ty', 'tx')
The draws below stay inside these ranges and needn't reach their ends.
All inputs are finite; a program needn't handle non-finite values.
Results may differ from the reference program's by a relative error of at most 0.0003.
Values sent between devices are 32-bit elements; how exact they have to be, the bound alone decides.
A program may use at most 64 MiB of HBM per device.

```python
import jax
import jax.numpy as jnp
from jax import lax

PATCH = 128
STRIDE = 64
SECTIONS = 8
NY = 1024
NX = 4096
NODES_Y = 16


def draw_images(key, part):
    shifts = jax.random.randint(jax.random.fold_in(key, 11), (SECTIONS, 2, 2), -20, 21)
    base = jax.random.normal(jax.random.fold_in(key, 12), (SECTIONS, NY, NX), jnp.float32)
    layers = [base[0]]
    for index in range(1, SECTIONS):
        previous = layers[-1]
        moved_one = jnp.roll(jnp.roll(previous, shifts[index, 0, 0], axis=0), shifts[index, 0, 1], axis=1)
        layers.append(0.03 * moved_one + 0.9995 * base[index])
    stacked = jnp.stack(layers)
    return jnp.clip(stacked, -12.0, 12.0).astype(jnp.float32)


def setup_inputs(seed: int = 0) -> dict:
    arg_keys = jax.random.split(jax.random.key(seed), 2)
    return {
        "images": draw_images(jax.random.fold_in(arg_keys[1], 71), 0),
    }


stiffness = 1.0
rate = 0.25


def soft_flow(corr):
    count = corr.shape[0]
    scores = corr / PATCH
    weights = jax.nn.softmax(scores.reshape(count, PATCH * PATCH), axis=-1).reshape(count, PATCH, PATCH)
    offsets = jnp.arange(PATCH)
    offsets = jnp.where(offsets < PATCH // 2, offsets, offsets - PATCH).astype(jnp.float32)
    flow_y = jnp.sum(weights * offsets[:, None], axis=(1, 2))
    flow_x = jnp.sum(weights * offsets[None, :], axis=(1, 2))
    return jnp.stack([flow_y, flow_x])


def band_patches(band):
    nodes = band.shape[1] // STRIDE - 1
    columns = band.reshape(PATCH, nodes + 1, STRIDE)
    pieces = jnp.concatenate([columns[:, :-1], columns[:, 1:]], axis=2)
    pieces = jnp.transpose(pieces, (1, 0, 2))
    return pieces - jnp.mean(pieces, axis=(1, 2), keepdims=True)


def section_flow(pair):
    first_img, second_img = pair
    half = STRIDE // 2
    first_pad = jnp.pad(first_img, half)
    second_pad = jnp.pad(second_img, half)

    def row_flow(row_index):
        start = (row_index * STRIDE).astype(jnp.int32)
        first_band = lax.dynamic_slice_in_dim(first_pad, start, PATCH, 0)
        second_band = lax.dynamic_slice_in_dim(second_pad, start, PATCH, 0)
        first_freq = jnp.fft.fft2(band_patches(first_band))
        second_freq = jnp.fft.fft2(band_patches(second_band))
        corr = jnp.real(jnp.fft.ifft2(jnp.conj(first_freq) * second_freq)).astype(jnp.float32)
        return soft_flow(corr)

    rows = lax.map(row_flow, jnp.arange(NODES_Y, dtype=jnp.int32))
    return jnp.transpose(rows, (1, 0, 2))


def relax_step(field, flow):
    padded = jnp.pad(field, ((0, 0), (0, 0), (1, 1), (1, 1)))
    lap = padded[:, :, :-2, 1:-1] + padded[:, :, 2:, 1:-1] + padded[:, :, 1:-1, :-2] + padded[:, :, 1:-1, 2:] - 4.0 * field
    return field + rate * (stiffness * lap + flow - field)


def reference(images):
    following = jnp.concatenate([images[1:], jnp.zeros_like(images[:1])], axis=0)
    flows = lax.map(section_flow, (images, following))
    keep = (jnp.arange(SECTIONS) < SECTIONS - 1).astype(jnp.float32)
    flows = flows * keep[:, None, None, None]
    relaxed = flows
    for step in range(2):
        relaxed = relax_step(relaxed, flows)
    totals = jnp.cumsum(relaxed, axis=0)
    cumulative = jnp.concatenate([jnp.zeros_like(relaxed[:1]), totals[:-1]], axis=0)
    return relaxed, cumulative
```

```python
import functools

import jax
import jax.numpy as jnp
import ml_dtypes
import numpy as np
from jax import lax
from jax.experimental import pallas as pl
from jax.experimental.pallas import tpu as pltpu
from jax.sharding import PartitionSpec as P

PATCH = 128
STRIDE = 64
HALF = 32
RATE = 0.25
GROUP = 4

MESH = pl.DeviceIdType.MESH
DIRECTIONS = [(dy, dx) for dy in (-1, 0, 1) for dx in (-1, 0, 1) if (dy, dx) != (0, 0)]
F32 = jnp.float32
BF16 = jnp.bfloat16


def split_table(table):
    high = table.astype(ml_dtypes.bfloat16)
    low = (table - high.astype(np.float64)).astype(ml_dtypes.bfloat16)
    return high, low


def tables():
    half = PATCH // 2
    point = np.arange(PATCH)
    angle = 2.0 * np.pi / PATCH
    packed = np.zeros((PATCH, PATCH))
    for k in range(half):
        packed[k] = np.cos(angle * (k * point % PATCH))
        packed[half + k] = np.sin(angle * (k * point % PATCH))
    packed[half] = np.cos(np.pi * point)
    weight = np.full(PATCH, 2.0)
    weight[0] = weight[half] = 1.0
    inverse = packed.T * weight[None, :] / PATCH

    def left(table):
        high, low = split_table(table)
        return np.block([[high, high], [low, low]])

    def right(table):
        high, low = split_table(table)
        return np.block([[high, low], [high, low]])

    scale = np.log2(np.e) / PATCH
    return np.stack(
        [right(packed.T), left(packed), left(inverse), right(inverse.T * scale)]
    ).astype(ml_dtypes.bfloat16)


def split(value):
    high = value.astype(BF16)
    low = (value - high.astype(F32)).astype(BF16)
    return high, low


def product(own, other):
    half = PATCH // 2
    lane = lax.broadcasted_iota(jnp.int32, (half, PATCH), 1)
    row = lax.broadcasted_iota(jnp.int32, (half, PATCH), 0)
    left = lane < half
    alone = (lane == 0) | (lane == half)
    plain = left | alone
    top_row = row == 0
    t, u = own[:half], own[half:]
    t2, u2 = other[:half], other[half:]
    rt2 = pltpu.roll(t2, half, 1)
    ru2 = pltpu.roll(u2, half, 1)
    uu, uru = u * u2, u * ru2
    g = t * t2 + jnp.where(top_row, 0.0, uu)
    h = t * rt2 + jnp.where(top_row, 0.0, uru)
    g2 = jnp.where(top_row, uu, t * u2 - u * t2)
    h2 = jnp.where(top_row, uru, t * ru2 - u * rt2)

    def joined(g, h):
        cross = pltpu.roll(jnp.where(left, h, g), half, 1)
        cross = jnp.where(alone, 0.0, cross)
        return jnp.where(plain, cross + g, cross - h)

    top = joined(g, h)
    top = jnp.where(top_row & (lane == 0), 0.0, top)
    return jnp.concatenate([top, joined(g2, h2)], axis=0)


def moments(scores):
    peak = jnp.max(jnp.max(scores, axis=0, keepdims=True), axis=1, keepdims=True)
    terms = jnp.exp2(scores - peak)
    total = None
    for g in range(PATCH // 8):
        part = terms[8 * g : 8 * g + 8]
        steps = float(g if g < PATCH // 16 else g - PATCH // 8)
        total = part if total is None else total + part
        first = part * steps if g == 0 else first + part * steps
    sub = lax.broadcasted_iota(jnp.int32, (8, PATCH), 0).astype(F32)
    lane = lax.broadcasted_iota(jnp.int32, (8, PATCH), 1)
    lag = jnp.where(lane < PATCH // 2, lane, lane - PATCH).astype(F32)
    return [
        jnp.sum(value, axis=0, keepdims=True)
        for value in (total, first * 8.0 + total * sub, total * lag)
    ]


def relax(flow, inside):
    def lap(value):
        return (
            pltpu.roll(value, 1, 0)
            + pltpu.roll(value, 7, 0)
            + pltpu.roll(value, 1, 1)
            + pltpu.roll(value, PATCH - 1, 1)
            - 4.0 * value
        )

    first = flow + RATE * (lap(flow) + flow - flow)
    first = jnp.where(inside, first, 0.0)
    return first + RATE * (lap(first) + flow - first)


def kernel(
    sizes, x_ref, tables_ref, out_ref, own, nxt, own_hi, own_lo, nxt_hi, nxt_lo, spec, table,
    stats, flows, around, meshes,
    local_sem, piece_send, piece_recv, own_send, own_recv, nxt_send, nxt_recv,
    flow_send, flow_recv, mesh_send, mesh_recv,
):
    n_sec, n_ty, n_tx = sizes
    rows, cols = x_ref.shape
    node_rows, node_cols = rows // STRIDE, cols // STRIDE
    wide = node_cols * PATCH
    sec, ty, tx = lax.axis_index("sec"), lax.axis_index("ty"), lax.axis_index("tx")

    def there(dy, dx):
        ok = jnp.bool_(True)
        if dy:
            ok = (ty + dy >= 0) & (ty + dy < n_ty)
        if dx:
            in_x = (tx + dx >= 0) & (tx + dx < n_tx)
            ok = ok & in_x if dy else in_x
        return ok

    has_next = sec < n_sec - 1
    has_before = sec > 0

    barrier = pltpu.get_barrier_semaphore()

    def greet(ok, s, y, x):
        @pl.when(ok)
        def _():
            pl.semaphore_signal(barrier, inc=1, device_id=(s, y, x), device_id_type=MESH)

    for dy, dx in DIRECTIONS:
        greet(there(dy, dx), sec, ty + dy, tx + dx)
    for d in range(1, n_sec):
        pl.semaphore_signal(
            barrier, inc=1, device_id=(lax.rem(sec + d, n_sec), ty, tx), device_id_type=MESH
        )

    tile = pltpu.make_async_copy(
        x_ref, own.at[pl.ds(HALF, rows), pl.ds(PATCH, cols)], local_sem.at[0]
    )
    tile.start()
    load = pltpu.make_async_copy(tables_ref, table, local_sem.at[1])
    load.start()

    for ref in (own, nxt):
        @pl.when(ty == 0)
        def _(ref=ref):
            ref[0:HALF, :] = jnp.zeros((HALF, cols + 2 * PATCH), F32)

        @pl.when(ty == n_ty - 1)
        def _(ref=ref):
            ref[HALF + rows : 2 * HALF + rows, :] = jnp.zeros((HALF, cols + 2 * PATCH), F32)

        @pl.when(tx == 0)
        def _(ref=ref):
            ref[:, 0:PATCH] = jnp.zeros((2 * HALF + rows, PATCH), F32)

        @pl.when(tx == n_tx - 1)
        def _(ref=ref):
            ref[:, PATCH + cols :] = jnp.zeros((2 * HALF + rows, PATCH), F32)

    for index, (dy, dx) in enumerate(DIRECTIONS):
        @pl.when(jnp.logical_not(there(-dy, -dx)))
        def _(index=index):
            around[index] = jnp.zeros((8, PATCH), F32)

    for t in range(n_sec):
        @pl.when(t >= sec)
        def _(t=t):
            meshes[t] = jnp.zeros((8, PATCH), F32)

    tall = 1 + (ty > 0).astype(jnp.int32) + (ty < n_ty - 1).astype(jnp.int32)
    broad = 1 + (tx > 0).astype(jnp.int32) + (tx < n_tx - 1).astype(jnp.int32)
    pl.semaphore_wait(barrier, n_sec - 1 + tall * broad - 1)

    inner_rows = rows - 2 * HALF
    mids = inner_rows // STRIDE
    pieces = [
        (0, HALF, 0, cols),
        (rows - HALF, HALF, 0, cols),
        (HALF, inner_rows, 0, PATCH),
        (HALF, inner_rows, cols - PATCH, PATCH),
    ]
    pieces += [(HALF + m * STRIDE, STRIDE, PATCH, cols - 2 * PATCH) for m in range(mids)]

    def piece_copy(p):
        r, nr, c, nc = pieces[p]
        return pltpu.make_async_remote_copy(
            src_ref=x_ref.at[pl.ds(r, nr), pl.ds(c, nc)],
            dst_ref=nxt.at[pl.ds(HALF + r, nr), pl.ds(PATCH + c, nc)],
            send_sem=piece_send.at[p],
            recv_sem=piece_recv.at[p],
            device_id=(sec - 1, ty, tx),
            device_id_type=MESH,
        )

    def border(axis_step, size, width):
        if axis_step == 0:
            return 0, size, 0
        if axis_step < 0:
            return 0, width, size
        return size - width, width, -width

    def border_copy(index, from_tile, target, send, recv):
        dy, dx = DIRECTIONS[index]
        r, nr, to_r = border(dy, rows, HALF)
        c, nc, to_c = border(dx, cols, PATCH)
        if from_tile:
            src = x_ref.at[pl.ds(r, nr), pl.ds(c, nc)]
        else:
            src = target.at[pl.ds(HALF + r, nr), pl.ds(PATCH + c, nc)]
        return pltpu.make_async_remote_copy(
            src_ref=src,
            dst_ref=target.at[pl.ds(HALF + to_r, nr), pl.ds(PATCH + to_c, nc)],
            send_sem=send.at[index],
            recv_sem=recv.at[index],
            device_id=(sec, ty + dy, tx + dx),
            device_id_type=MESH,
        )

    @pl.when(has_before)
    def _():
        for p in range(4):
            piece_copy(p).start()

    for index, (dy, dx) in enumerate(DIRECTIONS):
        @pl.when(there(dy, dx))
        def _(index=index):
            border_copy(index, True, own, own_send, own_recv).start()

    @pl.when(has_before)
    def _():
        for p in range(4, len(pieces)):
            piece_copy(p).start()

    lane = lax.broadcasted_iota(jnp.int32, (STRIDE, PATCH), 1)
    even, odd = lane < PATCH - HALF, lane >= HALF

    def right_chunk(source, high, low, b):
        at = pl.ds(pl.multiple_of(b * STRIDE, STRIDE), STRIDE)
        parts = []
        for j in range(node_cols):
            t = j // 2
            main = source[at, (t + 1) * PATCH : (t + 2) * PATCH]
            if j % 2 == 0:
                patch = jnp.where(even, main, source[at, t * PATCH : (t + 1) * PATCH])
            else:
                patch = jnp.where(odd, main, source[at, (t + 2) * PATCH : (t + 3) * PATCH])
            parts.append(jnp.concatenate(split(patch), axis=1))
        got = jnp.dot(jnp.concatenate(parts, axis=0), table[0], preferred_element_type=F32)
        got = got[:, :PATCH] + got[:, PATCH:]
        for j in range(node_cols):
            hi, lo = split(got[j * STRIDE : (j + 1) * STRIDE])
            high[at, j * PATCH : (j + 1) * PATCH] = hi
            low[at, j * PATCH : (j + 1) * PATCH] = lo

    def left_spectrum(high, low, i, columns):
        at = pl.ds(pl.multiple_of(i * STRIDE, STRIDE), PATCH)
        both = jnp.concatenate([high[at, columns], low[at, columns]], axis=0)
        got = jnp.dot(table[1], both, preferred_element_type=F32)
        return got[:PATCH] + got[PATCH:]

    tile.wait()
    load.wait()
    for index, (dy, dx) in enumerate(DIRECTIONS):
        @pl.when(there(-dy, -dx))
        def _(index=index):
            border_copy(index, True, own, own_send, own_recv).wait_recv()

    @pl.loop(0, node_rows + 1)
    def _(b):
        right_chunk(own, own_hi, own_lo, b)

    @pl.when(has_next)
    def _():
        for p in range(4):
            piece_copy(p).wait_recv()
        for index, (dy, dx) in enumerate(DIRECTIONS):
            @pl.when(there(dy, dx))
            def _(index=index):
                border_copy(index, False, nxt, nxt_send, nxt_recv).start()

    @pl.loop(0, node_rows)
    def _(i):
        for c in range(0, wide, 2 * PATCH):
            at = pl.ds(c, 2 * PATCH)
            spec[i, :, at] = left_spectrum(own_hi, own_lo, i, at)

    @pl.when(has_next)
    def _():
        for index, (dy, dx) in enumerate(DIRECTIONS):
            @pl.when(there(-dy, -dx))
            def _(index=index):
                border_copy(index, False, nxt, nxt_send, nxt_recv).wait_recv()

    right_chunk(nxt, nxt_hi, nxt_lo, 0)

    def mid_wait(m):
        at = pl.ds(pl.multiple_of(HALF + m * STRIDE, HALF), STRIDE)
        to = pl.ds(pl.multiple_of(2 * HALF + m * STRIDE, HALF), STRIDE)
        pltpu.make_async_remote_copy(
            src_ref=x_ref.at[at, pl.ds(PATCH, cols - 2 * PATCH)],
            dst_ref=nxt.at[to, pl.ds(2 * PATCH, cols - 2 * PATCH)],
            send_sem=piece_send.at[4 + m],
            recv_sem=piece_recv.at[4 + m],
            device_id=(sec - 1, ty, tx),
            device_id_type=MESH,
        ).wait_recv()

    @pl.loop(0, node_rows)
    def _(i):
        @pl.when(has_next & (i < mids))
        def _():
            mid_wait(i)

        right_chunk(nxt, nxt_hi, nxt_lo, i + 1)

        @pl.loop(0, node_cols // GROUP)
        def _(g):
            columns = pl.ds(pl.multiple_of(g * GROUP * PATCH, PATCH), GROUP * PATCH)
            other = left_spectrum(nxt_hi, nxt_lo, i, columns)
            mine = spec[i, :, columns]
            prods = jnp.concatenate(
                [
                    product(mine[:, n * PATCH : (n + 1) * PATCH], other[:, n * PATCH : (n + 1) * PATCH])
                    for n in range(GROUP)
                ],
                axis=1,
            )
            mixed = jnp.dot(
                table[2], jnp.concatenate(split(prods), axis=0), preferred_element_type=F32
            )
            hi, lo = split(mixed[:PATCH] + mixed[PATCH:])
            stacked = jnp.concatenate(
                [
                    jnp.concatenate(
                        [hi[:, n * PATCH : (n + 1) * PATCH], lo[:, n * PATCH : (n + 1) * PATCH]], axis=1
                    )
                    for n in range(GROUP)
                ],
                axis=0,
            )
            corr = jnp.dot(stacked, table[3], preferred_element_type=F32)
            corr = corr[:, :PATCH] + corr[:, PATCH:]
            found = [moments(corr[n * PATCH : (n + 1) * PATCH]) for n in range(GROUP)]
            for q in range(3):
                stats[q, i, pl.ds(g * GROUP, GROUP), :] = jnp.concatenate(
                    [f[q] for f in found], axis=0
                )

    lanes = lax.broadcasted_iota(jnp.int32, (8, PATCH), 1)
    columns = jnp.zeros((8, PATCH), F32)
    for i in range(node_rows):
        total, down, across = (jnp.sum(stats[q, i], axis=1, keepdims=True) for q in range(3))
        inv = 1.0 / total
        columns = jnp.where(lanes == i, down * inv, columns)
        columns = jnp.where(lanes == node_rows + i, across * inv, columns)
    columns = jnp.where(has_next, columns, 0.0)
    block = jnp.transpose(jnp.concatenate([columns] * 16, axis=0))[:8]
    flows[0] = block

    def flow_copy(index):
        dy, dx = DIRECTIONS[index]
        return pltpu.make_async_remote_copy(
            src_ref=flows.at[0],
            dst_ref=around.at[index],
            send_sem=flow_send.at[index],
            recv_sem=flow_recv.at[index],
            device_id=(sec, ty + dy, tx + dx),
            device_id_type=MESH,
        )

    for index, (dy, dx) in enumerate(DIRECTIONS):
        @pl.when(there(dy, dx))
        def _(index=index):
            flow_copy(index).start()
    for index, (dy, dx) in enumerate(DIRECTIONS):
        @pl.when(there(-dy, -dx))
        def _(index=index):
            flow_copy(index).wait_recv()

    lines = {}
    for dy in (-1, 0, 1):
        def from_(dx, dy=dy):
            return block if (dy, dx) == (0, 0) else around[DIRECTIONS.index((-dy, -dx))]

        line = jnp.where(lanes < 2 + node_cols, pltpu.roll(from_(0), 2, 1), pltpu.roll(from_(1), 2 + node_cols, 1))
        lines[dy] = jnp.where(lanes < 2, pltpu.roll(from_(-1), PATCH + 2 - node_cols, 1), line)

    subs = lax.broadcasted_iota(jnp.int32, (8, PATCH), 0)
    row_id = ty * node_rows + subs - 2
    col_id = tx * node_cols + lanes - 2
    inside = (
        (row_id >= 0) & (row_id < node_rows * n_ty) & (col_id >= 0) & (col_id < node_cols * n_tx)
    )
    done = []
    for c in range(2):
        base = c * node_rows
        above = pltpu.roll(lines[-1], (8 - (base + node_rows - 2)) % 8, 0)
        here = pltpu.roll(lines[0], (8 + 2 - base) % 8, 0)
        below = pltpu.roll(lines[1], (8 + 2 + node_rows - base) % 8, 0)
        flow = jnp.where(subs < 2, above, jnp.where(subs < 2 + node_rows, here, below))
        done.append(pltpu.roll(relax(flow, inside), PATCH - 2, 1))
    result = jnp.where(
        subs < node_rows, pltpu.roll(done[0], 6, 0), pltpu.roll(done[1], (8 + node_rows - 2) % 8, 0)
    )
    flows[1] = result

    def mesh_copy(d):
        return pltpu.make_async_remote_copy(
            src_ref=flows.at[1],
            dst_ref=meshes.at[sec],
            send_sem=mesh_send.at[d],
            recv_sem=mesh_recv.at[d],
            device_id=(sec + d, ty, tx),
            device_id_type=MESH,
        )

    def mesh_wait(d):
        pltpu.make_async_remote_copy(
            src_ref=flows.at[1],
            dst_ref=meshes.at[sec - d],
            send_sem=mesh_send.at[d],
            recv_sem=mesh_recv.at[d],
            device_id=(sec - d, ty, tx),
            device_id_type=MESH,
        ).wait_recv()

    for d in range(1, n_sec):
        @pl.when(sec + d < n_sec)
        def _(d=d):
            mesh_copy(d).start()
    for d in range(1, n_sec):
        @pl.when(sec - d >= 0)
        def _(d=d):
            mesh_wait(d)

    earlier = meshes[0]
    for t in range(1, n_sec):
        earlier = earlier + meshes[t]
    out_ref[0] = result
    out_ref[1] = earlier

    @pl.when(has_before)
    def _():
        for p in range(len(pieces)):
            piece_copy(p).wait_send()

    for index, (dy, dx) in enumerate(DIRECTIONS):
        @pl.when(there(dy, dx))
        def _(index=index):
            border_copy(index, True, own, own_send, own_recv).wait_send()
            flow_copy(index).wait_send()

            @pl.when(has_next)
            def _():
                border_copy(index, False, nxt, nxt_send, nxt_recv).wait_send()

    for d in range(1, n_sec):
        @pl.when(sec + d < n_sec)
        def _(d=d):
            mesh_copy(d).wait_send()


def solution(mesh):
    sizes = tuple(mesh.shape[axis] for axis in ("sec", "ty", "tx"))

    def on_device(images):
        image = images[0]
        rows, cols = image.shape
        node_rows, node_cols = rows // STRIDE, cols // STRIDE
        high = 2 * HALF + rows
        wide = node_cols * PATCH
        around = len(DIRECTIONS)
        n_pieces = 4 + (rows - 2 * HALF) // STRIDE
        dma = pltpu.SemaphoreType.DMA
        out = pl.pallas_call(
            functools.partial(kernel, sizes),
            out_shape=jax.ShapeDtypeStruct((2, 8, PATCH), F32),
            in_specs=[pl.BlockSpec(memory_space=pl.ANY)] * 2,
            out_specs=pl.BlockSpec(memory_space=pltpu.VMEM),
            scratch_shapes=[
                pltpu.VMEM((high, cols + 2 * PATCH), F32),
                pltpu.VMEM((high, cols + 2 * PATCH), F32),
                pltpu.VMEM((high, wide), BF16),
                pltpu.VMEM((high, wide), BF16),
                pltpu.VMEM((high, wide), BF16),
                pltpu.VMEM((high, wide), BF16),
                pltpu.VMEM((node_rows, PATCH, wide), F32),
                pltpu.VMEM((4, 2 * PATCH, 2 * PATCH), BF16),
                pltpu.VMEM((3, node_rows, node_cols, PATCH), F32),
                pltpu.VMEM((2, 8, PATCH), F32),
                pltpu.VMEM((around, 8, PATCH), F32),
                pltpu.VMEM((sizes[0], 8, PATCH), F32),
                dma((2,)),
                dma((n_pieces,)),
                dma((n_pieces,)),
                dma((around,)),
                dma((around,)),
                dma((around,)),
                dma((around,)),
                dma((around,)),
                dma((around,)),
                dma((sizes[0],)),
                dma((sizes[0],)),
            ],
            compiler_params=pltpu.CompilerParams(
                collective_id=0, has_side_effects=True, vmem_limit_bytes=40 * 1024 * 1024
            ),
        )(image, jnp.asarray(tables()))
        out = out[:, :, :node_cols].reshape(2, 1, 2, node_rows, node_cols)
        return out[0], out[1]

    return jax.shard_map(
        on_device,
        mesh=mesh,
        in_specs=(P("sec", "ty", "tx"),),
        out_specs=(P("sec", None, "ty", "tx"), P("sec", None, "ty", "tx")),
        check_vma=False,
    )
```

```python
import functools

import jax
import jax.numpy as jnp
import ml_dtypes
import numpy as np
from jax import lax
from jax.experimental import pallas as pl
from jax.experimental.pallas import tpu as pltpu
from jax.sharding import PartitionSpec as P

PATCH = 128
STRIDE = 64
HALF = 32
RATE = 0.25

MESH = pl.DeviceIdType.MESH
DIRECTIONS = [(dy, dx) for dy in (-1, 0, 1) for dx in (-1, 0, 1) if (dy, dx) != (0, 0)]
F32 = jnp.float32
BF16 = jnp.bfloat16


def split_table(table):
    high = table.astype(ml_dtypes.bfloat16)
    low = (table - high.astype(np.float64)).astype(ml_dtypes.bfloat16)
    return high, low


def tables():
    half = PATCH // 2
    point = np.arange(PATCH)
    angle = 2.0 * np.pi / PATCH
    packed = np.zeros((PATCH, PATCH))
    for k in range(half):
        packed[k] = np.cos(angle * (k * point % PATCH))
        packed[half + k] = np.sin(angle * (k * point % PATCH))
    packed[half] = np.cos(np.pi * point)
    weight = np.full(PATCH, 2.0)
    weight[0] = weight[half] = 1.0
    inverse = packed.T * weight[None, :] / PATCH

    def left(table):
        high, low = split_table(table)
        return np.block([[high, high], [low, low]])

    def right(table):
        high, low = split_table(table)
        return np.block([[high, low], [high, low]])

    scale = np.log2(np.e) / PATCH
    return np.stack(
        [right(packed.T), left(packed), left(inverse), right(inverse.T * scale)]
    ).astype(ml_dtypes.bfloat16)


def split(value):
    high = value.astype(BF16)
    low = (value - high.astype(F32)).astype(BF16)
    return high, low


def product(own, other):
    half = PATCH // 2
    lane = lax.broadcasted_iota(jnp.int32, (half, PATCH), 1)
    row = lax.broadcasted_iota(jnp.int32, (half, PATCH), 0)
    left = lane < half
    alone = (lane == 0) | (lane == half)
    plain = left | alone
    top_row = row == 0
    t, u = own[:half], own[half:]
    t2, u2 = other[:half], other[half:]
    rt2 = pltpu.roll(t2, half, 1)
    ru2 = pltpu.roll(u2, half, 1)
    uu, uru = u * u2, u * ru2
    g = t * t2 + jnp.where(top_row, 0.0, uu)
    h = t * rt2 + jnp.where(top_row, 0.0, uru)
    g2 = jnp.where(top_row, uu, t * u2 - u * t2)
    h2 = jnp.where(top_row, uru, t * ru2 - u * rt2)

    def joined(g, h):
        cross = pltpu.roll(jnp.where(left, h, g), half, 1)
        cross = jnp.where(alone, 0.0, cross)
        return jnp.where(plain, cross + g, cross - h)

    top = joined(g, h)
    top = jnp.where(top_row & (lane == 0), 0.0, top)
    return jnp.concatenate([top, joined(g2, h2)], axis=0)


def moments(scores):
    peak = jnp.max(jnp.max(scores, axis=0, keepdims=True), axis=1, keepdims=True)
    terms = jnp.exp2(scores - peak)
    total = None
    for g in range(PATCH // 8):
        part = terms[8 * g : 8 * g + 8]
        steps = float(g if g < PATCH // 16 else g - PATCH // 8)
        total = part if total is None else total + part
        first = part * steps if g == 0 else first + part * steps
    sub = lax.broadcasted_iota(jnp.int32, (8, PATCH), 0).astype(F32)
    lane = lax.broadcasted_iota(jnp.int32, (8, PATCH), 1)
    lag = jnp.where(lane < PATCH // 2, lane, lane - PATCH).astype(F32)
    return [
        jnp.sum(value, axis=0, keepdims=True)
        for value in (total, first * 8.0 + total * sub, total * lag)
    ]


def relax(flow, inside):
    def lap(value):
        return (
            pltpu.roll(value, 1, 0)
            + pltpu.roll(value, 7, 0)
            + pltpu.roll(value, 1, 1)
            + pltpu.roll(value, PATCH - 1, 1)
            - 4.0 * value
        )

    first = flow + RATE * (lap(flow) + flow - flow)
    first = jnp.where(inside, first, 0.0)
    return first + RATE * (lap(first) + flow - first)


def kernel(
    sizes, x_ref, tables_ref, out_ref, own, nxt, own_hi, own_lo, nxt_hi, nxt_lo, spec, table,
    stats, flows, around, meshes,
    own_pack, own_land, nxt_pack, nxt_land,
    local_sem, piece_send, piece_recv, own_send, own_recv, nxt_send, nxt_recv, straight_send,
    flow_send, flow_recv, mesh_send, mesh_recv,
):
    n_sec, n_ty, n_tx = sizes
    rows, cols = x_ref.shape
    node_rows, node_cols = rows // STRIDE, cols // STRIDE
    wide = node_cols * PATCH
    sec, ty, tx = lax.axis_index("sec"), lax.axis_index("ty"), lax.axis_index("tx")

    def there(dy, dx):
        ok = jnp.bool_(True)
        if dy:
            ok = (ty + dy >= 0) & (ty + dy < n_ty)
        if dx:
            in_x = (tx + dx >= 0) & (tx + dx < n_tx)
            ok = ok & in_x if dy else in_x
        return ok

    has_next = sec < n_sec - 1
    has_before = sec > 0

    def crosses(dy):
        return (ty % 2 == 1) if dy > 0 else (ty % 2 == 0)

    def straight(dy, dx):
        return crosses(dy) & there(dy, dx)

    barrier = pltpu.get_barrier_semaphore()

    def greet(ok, s, y, x):
        @pl.when(ok)
        def _():
            pl.semaphore_signal(barrier, inc=1, device_id=(s, y, x), device_id_type=MESH)

    for dy, dx in DIRECTIONS:
        greet(there(dy, dx), sec, ty + dy, tx + dx)
    for dy in (-1, 1):
        for dx in (-1, 0, 1):
            greet(has_before & straight(dy, dx), sec - 1, ty + dy, tx + dx)
            greet(has_next & straight(dy, dx), sec + 1, ty + dy, tx + dx)
    for d in range(1, n_sec):
        pl.semaphore_signal(
            barrier, inc=1, device_id=(lax.rem(sec + d, n_sec), ty, tx), device_id_type=MESH
        )

    tile = pltpu.make_async_copy(
        x_ref, own.at[pl.ds(HALF, rows), pl.ds(PATCH, cols)], local_sem.at[0]
    )
    tile.start()
    load = pltpu.make_async_copy(tables_ref, table, local_sem.at[1])
    load.start()

    for ref in (own, nxt):
        @pl.when(ty == 0)
        def _(ref=ref):
            ref[0:HALF, :] = jnp.zeros((HALF, cols + 2 * PATCH), F32)

        @pl.when(ty == n_ty - 1)
        def _(ref=ref):
            ref[HALF + rows : 2 * HALF + rows, :] = jnp.zeros((HALF, cols + 2 * PATCH), F32)

        @pl.when(tx == 0)
        def _(ref=ref):
            ref[:, 0:PATCH] = jnp.zeros((2 * HALF + rows, PATCH), F32)

        @pl.when(tx == n_tx - 1)
        def _(ref=ref):
            ref[:, PATCH + cols :] = jnp.zeros((2 * HALF + rows, PATCH), F32)

    for index, (dy, dx) in enumerate(DIRECTIONS):
        @pl.when(jnp.logical_not(there(-dy, -dx)))
        def _(index=index):
            around[index] = jnp.zeros((8, PATCH), F32)

    for t in range(n_sec):
        @pl.when(t >= sec)
        def _(t=t):
            meshes[t] = jnp.zeros((8, PATCH), F32)

    tall = 1 + (ty > 0).astype(jnp.int32) + (ty < n_ty - 1).astype(jnp.int32)
    broad = 1 + (tx > 0).astype(jnp.int32) + (tx < n_tx - 1).astype(jnp.int32)
    apart = (crosses(-1) & there(-1, 0)).astype(jnp.int32) + (crosses(1) & there(1, 0)).astype(jnp.int32)
    ends = has_before.astype(jnp.int32) + has_next.astype(jnp.int32)
    pl.semaphore_wait(barrier, n_sec - 1 + tall * broad - 1 + apart * broad * ends)

    inner_rows = rows - 2 * HALF
    mids = inner_rows // STRIDE
    pieces = [
        (0, HALF, 0, cols),
        (rows - HALF, HALF, 0, cols),
        (HALF, inner_rows, 0, PATCH),
        (HALF, inner_rows, cols - PATCH, PATCH),
    ]
    pieces += [(HALF + m * STRIDE, STRIDE, PATCH, cols - 2 * PATCH) for m in range(mids)]

    def piece_copy(p):
        r, nr, c, nc = pieces[p]
        return pltpu.make_async_remote_copy(
            src_ref=x_ref.at[pl.ds(r, nr), pl.ds(c, nc)],
            dst_ref=nxt.at[pl.ds(HALF + r, nr), pl.ds(PATCH + c, nc)],
            send_sem=piece_send.at[p],
            recv_sem=piece_recv.at[p],
            device_id=(sec - 1, ty, tx),
            device_id_type=MESH,
        )

    def border(axis_step, size, width):
        if axis_step == 0:
            return 0, size, 0
        if axis_step < 0:
            return 0, width, size
        return size - width, width, -width

    def border_copy(index, source, target, send, recv, to_sec, pack=None, land=None):
        dy, dx = DIRECTIONS[index]
        if dy == 0:
            side = (dx + 1) // 2
            src, dst = pack.at[side], land.at[side]
        else:
            r, nr, to_r = border(dy, rows, HALF)
            c, nc, to_c = border(dx, cols, PATCH)
            if source is None:
                src = x_ref.at[pl.ds(r, nr), pl.ds(c, nc)]
            else:
                src = source.at[pl.ds(HALF + r, nr), pl.ds(PATCH + c, nc)]
            dst = target.at[pl.ds(HALF + to_r, nr), pl.ds(PATCH + to_c, nc)]
        return pltpu.make_async_remote_copy(
            src_ref=src,
            dst_ref=dst,
            send_sem=send.at[index],
            recv_sem=recv.at[index],
            device_id=(to_sec, ty + dy, tx + dx),
            device_id_type=MESH,
        )

    def own_border(index):
        return border_copy(index, None, own, own_send, own_recv, sec, own_pack, own_land)

    def nxt_border(index):
        return border_copy(index, nxt, nxt, nxt_send, nxt_recv, sec, nxt_pack, nxt_land)

    def nxt_straight(index):
        return border_copy(index, None, nxt, straight_send, nxt_recv, sec - 1)

    UPDOWN = [k for k, (dy, dx) in enumerate(DIRECTIONS) if dy]
    SIDES = [k for k, (dy, dx) in enumerate(DIRECTIONS) if not dy]

    def each(indices, ok, do):
        for index in indices:
            @pl.when(ok(*DIRECTIONS[index]))
            def _(index=index):
                do(index)

    def from_there(dy, dx):
        return there(-dy, -dx)

    def handed_on(dy, dx):
        return jnp.logical_not(crosses(dy)) & there(dy, dx)

    span = rows // 4
    packed_lane = lax.broadcasted_iota(jnp.int32, (span, PATCH), 1)

    def pack_columns(source, into):
        for side, at in enumerate((PATCH, cols)):
            first = 0 if side == 0 else PATCH - HALF
            value = None
            for q in range(4):
                part = source[HALF + span * q : HALF + span * (q + 1), at : at + PATCH]
                part = pltpu.roll(part, (HALF * q - first) % PATCH, 1) if HALF * q != first else part
                value = part if q == 0 else jnp.where(packed_lane >= HALF * q, part, value)
            into[side] = value

    def unpack_columns(land, target):
        for side, at in enumerate((PATCH + cols, 0)):
            first = 0 if side == 0 else PATCH - HALF

            @pl.when(there(0, 1 - 2 * side))
            def _(side=side, at=at, first=first):
                for q in range(4):
                    part = land[side]
                    part = pltpu.roll(part, (first - HALF * q) % PATCH, 1) if HALF * q != first else part
                    target[HALF + span * q : HALF + span * (q + 1), at : at + PATCH] = part

    @pl.when(has_before)
    def _():
        for p in range(4):
            piece_copy(p).start()
        each(UPDOWN, straight, lambda k: nxt_straight(k).start())

    each(UPDOWN, there, lambda k: own_border(k).start())

    @pl.when(has_before)
    def _():
        for p in range(4, len(pieces)):
            piece_copy(p).start()

    tile.wait()
    pack_columns(own, own_pack)
    each(SIDES, there, lambda k: own_border(k).start())
    load.wait()

    lane = lax.broadcasted_iota(jnp.int32, (STRIDE, PATCH), 1)
    even, odd = lane < PATCH - HALF, lane >= HALF

    def right_chunk(source, high, low, b):
        at = pl.ds(pl.multiple_of(b * STRIDE, STRIDE), STRIDE)
        parts = []
        for j in range(node_cols):
            t = j // 2
            main = source[at, (t + 1) * PATCH : (t + 2) * PATCH]
            if j % 2 == 0:
                patch = jnp.where(even, main, source[at, t * PATCH : (t + 1) * PATCH])
            else:
                patch = jnp.where(odd, main, source[at, (t + 2) * PATCH : (t + 3) * PATCH])
            parts.append(jnp.concatenate(split(patch), axis=1))
        got = jnp.dot(jnp.concatenate(parts, axis=0), table[0], preferred_element_type=F32)
        got = got[:, :PATCH] + got[:, PATCH:]
        for j in range(node_cols):
            hi, lo = split(got[j * STRIDE : (j + 1) * STRIDE])
            high[at, j * PATCH : (j + 1) * PATCH] = hi
            low[at, j * PATCH : (j + 1) * PATCH] = lo

    def left_spectrum(high, low, i, columns):
        at = pl.ds(pl.multiple_of(i * STRIDE, STRIDE), PATCH)
        both = jnp.concatenate([high[at, columns], low[at, columns]], axis=0)
        got = jnp.dot(table[1], both, preferred_element_type=F32)
        return got[:PATCH] + got[PATCH:]

    each(range(len(DIRECTIONS)), from_there, lambda k: own_border(k).wait_recv())
    unpack_columns(own_land, own)

    @pl.loop(0, node_rows + 1)
    def _(b):
        right_chunk(own, own_hi, own_lo, b)

    @pl.when(has_next)
    def _():
        piece_copy(0).wait_recv()
        piece_copy(1).wait_recv()
        each(UPDOWN, handed_on, lambda k: nxt_border(k).start())

    @pl.loop(0, node_rows)
    def _(i):
        for c in range(0, wide, 2 * PATCH):
            at = pl.ds(c, 2 * PATCH)
            spec[i, :, at] = left_spectrum(own_hi, own_lo, i, at)

    @pl.when(has_next)
    def _():
        piece_copy(2).wait_recv()
        piece_copy(3).wait_recv()
        pack_columns(nxt, nxt_pack)
        each(SIDES, there, lambda k: nxt_border(k).start())
        each(range(len(DIRECTIONS)), from_there, lambda k: nxt_border(k).wait_recv())
        unpack_columns(nxt_land, nxt)

    right_chunk(nxt, nxt_hi, nxt_lo, 0)
    right_chunk(nxt, nxt_hi, nxt_lo, node_rows)

    def mid_wait(m):
        at = pl.ds(pl.multiple_of(HALF + m * STRIDE, HALF), STRIDE)
        to = pl.ds(pl.multiple_of(2 * HALF + m * STRIDE, HALF), STRIDE)
        pltpu.make_async_remote_copy(
            src_ref=x_ref.at[at, pl.ds(PATCH, cols - 2 * PATCH)],
            dst_ref=nxt.at[to, pl.ds(2 * PATCH, cols - 2 * PATCH)],
            send_sem=piece_send.at[4 + m],
            recv_sem=piece_recv.at[4 + m],
            device_id=(sec - 1, ty, tx),
            device_id_type=MESH,
        ).wait_recv()

    @pl.loop(0, node_rows)
    def _(i):
        @pl.when(i < mids)
        def _():
            @pl.when(has_next)
            def _():
                mid_wait(i)

            right_chunk(nxt, nxt_hi, nxt_lo, i + 1)

        nodes = [slice(n * PATCH, (n + 1) * PATCH) for n in range(node_cols)]
        other = left_spectrum(nxt_hi, nxt_lo, i, pl.ds(0, wide))
        mine = spec[i]
        prods = jnp.concatenate([product(mine[:, n], other[:, n]) for n in nodes], axis=1)
        mixed = jnp.dot(
            table[2], jnp.concatenate(split(prods), axis=0), preferred_element_type=F32
        )
        hi, lo = split(mixed[:PATCH] + mixed[PATCH:])
        stacked = jnp.concatenate(
            [jnp.concatenate([hi[:, n], lo[:, n]], axis=1) for n in nodes], axis=0
        )
        corr = jnp.dot(stacked, table[3], preferred_element_type=F32)
        corr = corr[:, :PATCH] + corr[:, PATCH:]
        found = [moments(corr[n]) for n in nodes]
        for q in range(3):
            stats[q, i] = jnp.concatenate([f[q] for f in found], axis=0)

    lanes = lax.broadcasted_iota(jnp.int32, (8, PATCH), 1)
    columns = jnp.zeros((8, PATCH), F32)
    for i in range(node_rows):
        total, down, across = (jnp.sum(stats[q, i], axis=1, keepdims=True) for q in range(3))
        inv = 1.0 / total
        columns = jnp.where(lanes == i, down * inv, columns)
        columns = jnp.where(lanes == node_rows + i, across * inv, columns)
    columns = jnp.where(has_next, columns, 0.0)
    block = jnp.transpose(jnp.concatenate([columns] * 16, axis=0))[:8]
    flows[0] = block

    def flow_copy(index):
        dy, dx = DIRECTIONS[index]
        return pltpu.make_async_remote_copy(
            src_ref=flows.at[0],
            dst_ref=around.at[index],
            send_sem=flow_send.at[index],
            recv_sem=flow_recv.at[index],
            device_id=(sec, ty + dy, tx + dx),
            device_id_type=MESH,
        )

    for index, (dy, dx) in enumerate(DIRECTIONS):
        @pl.when(there(dy, dx))
        def _(index=index):
            flow_copy(index).start()
    for index, (dy, dx) in enumerate(DIRECTIONS):
        @pl.when(there(-dy, -dx))
        def _(index=index):
            flow_copy(index).wait_recv()

    lines = {}
    for dy in (-1, 0, 1):
        def from_(dx, dy=dy):
            return block if (dy, dx) == (0, 0) else around[DIRECTIONS.index((-dy, -dx))]

        line = jnp.where(lanes < 2 + node_cols, pltpu.roll(from_(0), 2, 1), pltpu.roll(from_(1), 2 + node_cols, 1))
        lines[dy] = jnp.where(lanes < 2, pltpu.roll(from_(-1), PATCH + 2 - node_cols, 1), line)

    subs = lax.broadcasted_iota(jnp.int32, (8, PATCH), 0)
    row_id = ty * node_rows + subs - 2
    col_id = tx * node_cols + lanes - 2
    inside = (
        (row_id >= 0) & (row_id < node_rows * n_ty) & (col_id >= 0) & (col_id < node_cols * n_tx)
    )
    done = []
    for c in range(2):
        base = c * node_rows
        above = pltpu.roll(lines[-1], (8 - (base + node_rows - 2)) % 8, 0)
        here = pltpu.roll(lines[0], (8 + 2 - base) % 8, 0)
        below = pltpu.roll(lines[1], (8 + 2 + node_rows - base) % 8, 0)
        flow = jnp.where(subs < 2, above, jnp.where(subs < 2 + node_rows, here, below))
        done.append(pltpu.roll(relax(flow, inside), PATCH - 2, 1))
    result = jnp.where(
        subs < node_rows, pltpu.roll(done[0], 6, 0), pltpu.roll(done[1], (8 + node_rows - 2) % 8, 0)
    )
    flows[1] = result

    def mesh_copy(d):
        return pltpu.make_async_remote_copy(
            src_ref=flows.at[1],
            dst_ref=meshes.at[sec],
            send_sem=mesh_send.at[d],
            recv_sem=mesh_recv.at[d],
            device_id=(sec + d, ty, tx),
            device_id_type=MESH,
        )

    def mesh_wait(d):
        pltpu.make_async_remote_copy(
            src_ref=flows.at[1],
            dst_ref=meshes.at[sec - d],
            send_sem=mesh_send.at[d],
            recv_sem=mesh_recv.at[d],
            device_id=(sec - d, ty, tx),
            device_id_type=MESH,
        ).wait_recv()

    for d in range(1, n_sec):
        @pl.when(sec + d < n_sec)
        def _(d=d):
            mesh_copy(d).start()
    for d in range(1, n_sec):
        @pl.when(sec - d >= 0)
        def _(d=d):
            mesh_wait(d)

    earlier = meshes[0]
    for t in range(1, n_sec):
        earlier = earlier + meshes[t]
    out_ref[0] = result
    out_ref[1] = earlier

    @pl.when(has_before)
    def _():
        for p in range(len(pieces)):
            piece_copy(p).wait_send()

    every = range(len(DIRECTIONS))
    each(every, there, lambda k: own_border(k).wait_send())
    each(every, there, lambda k: flow_copy(k).wait_send())

    @pl.when(has_before)
    def _():
        each(UPDOWN, straight, lambda k: nxt_straight(k).wait_send())

    @pl.when(has_next)
    def _():
        each(UPDOWN, handed_on, lambda k: nxt_border(k).wait_send())
        each(SIDES, there, lambda k: nxt_border(k).wait_send())

    for d in range(1, n_sec):
        @pl.when(sec + d < n_sec)
        def _(d=d):
            mesh_copy(d).wait_send()


def solution(mesh):
    sizes = tuple(mesh.shape[axis] for axis in ("sec", "ty", "tx"))

    def on_device(images):
        image = images[0]
        rows, cols = image.shape
        node_rows, node_cols = rows // STRIDE, cols // STRIDE
        high = 2 * HALF + rows
        wide = node_cols * PATCH
        around = len(DIRECTIONS)
        n_pieces = 4 + (rows - 2 * HALF) // STRIDE
        dma = pltpu.SemaphoreType.DMA
        out = pl.pallas_call(
            functools.partial(kernel, sizes),
            out_shape=jax.ShapeDtypeStruct((2, 8, PATCH), F32),
            in_specs=[pl.BlockSpec(memory_space=pl.ANY)] * 2,
            out_specs=pl.BlockSpec(memory_space=pltpu.VMEM),
            scratch_shapes=[
                pltpu.VMEM((high, cols + 2 * PATCH), F32),
                pltpu.VMEM((high, cols + 2 * PATCH), F32),
                pltpu.VMEM((high, wide), BF16),
                pltpu.VMEM((high, wide), BF16),
                pltpu.VMEM((high, wide), BF16),
                pltpu.VMEM((high, wide), BF16),
                pltpu.VMEM((node_rows, PATCH, wide), F32),
                pltpu.VMEM((4, 2 * PATCH, 2 * PATCH), BF16),
                pltpu.VMEM((3, node_rows, node_cols, PATCH), F32),
                pltpu.VMEM((2, 8, PATCH), F32),
                pltpu.VMEM((around, 8, PATCH), F32),
                pltpu.VMEM((sizes[0], 8, PATCH), F32),
                pltpu.VMEM((2, rows // 4, PATCH), F32),
                pltpu.VMEM((2, rows // 4, PATCH), F32),
                pltpu.VMEM((2, rows // 4, PATCH), F32),
                pltpu.VMEM((2, rows // 4, PATCH), F32),
                dma((2,)),
                dma((n_pieces,)),
                dma((n_pieces,)),
                dma((around,)),
                dma((around,)),
                dma((around,)),
                dma((around,)),
                dma((around,)),
                dma((around,)),
                dma((around,)),
                dma((sizes[0],)),
                dma((sizes[0],)),
            ],
            compiler_params=pltpu.CompilerParams(
                collective_id=0, has_side_effects=True, vmem_limit_bytes=60 * 1024 * 1024
            ),
        )(image, jnp.asarray(tables()))
        out = out[:, :, :node_cols].reshape(2, 1, 2, node_rows, node_cols)
        return out[0], out[1]

    return jax.shard_map(
        on_device,
        mesh=mesh,
        in_specs=(P("sec", "ty", "tx"),),
        out_specs=(P("sec", None, "ty", "tx"), P("sec", None, "ty", "tx")),
        check_vma=False,
    )
```

```python
import functools

import jax
import jax.numpy as jnp
import ml_dtypes
import numpy as np
from jax import lax
from jax.experimental import pallas as pl
from jax.experimental.pallas import tpu as pltpu
from jax.sharding import PartitionSpec as P

PATCH = 128
STRIDE = 64
HALF = 32
RATE = 0.25

MESH = pl.DeviceIdType.MESH
DIRECTIONS = [(dy, dx) for dy in (-1, 0, 1) for dx in (-1, 0, 1) if (dy, dx) != (0, 0)]
F32 = jnp.float32
BF16 = jnp.bfloat16


def split_table(table):
    high = table.astype(ml_dtypes.bfloat16)
    low = (table - high.astype(np.float64)).astype(ml_dtypes.bfloat16)
    return high, low


def tables():
    half = PATCH // 2
    point = np.arange(PATCH)
    angle = 2.0 * np.pi / PATCH
    packed = np.zeros((PATCH, PATCH))
    for k in range(half):
        packed[k] = np.cos(angle * (k * point % PATCH))
        packed[half + k] = np.sin(angle * (k * point % PATCH))
    packed[half] = np.cos(np.pi * point)
    weight = np.full(PATCH, 2.0)
    weight[0] = weight[half] = 1.0
    inverse = packed.T * weight[None, :] / PATCH

    def left(table):
        high, low = split_table(table)
        return np.block([[high, high], [low, low]])

    def right(table):
        high, low = split_table(table)
        return np.block([[high, low], [high, low]])

    scale = np.log2(np.e) / PATCH
    return np.stack(
        [right(packed.T), left(packed), left(inverse), right(inverse.T * scale)]
    ).astype(ml_dtypes.bfloat16)


def split(value):
    high = value.astype(BF16)
    low = (value - high.astype(F32)).astype(BF16)
    return high, low


def product(own, other):
    half = PATCH // 2
    lane = lax.broadcasted_iota(jnp.int32, (half, PATCH), 1)
    row = lax.broadcasted_iota(jnp.int32, (half, PATCH), 0)
    left = lane < half
    alone = (lane == 0) | (lane == half)
    plain = left | alone
    top_row = row == 0
    t, u = own[:half], own[half:]
    t2, u2 = other[:half], other[half:]
    rt2 = pltpu.roll(t2, half, 1)
    ru2 = pltpu.roll(u2, half, 1)
    uu, uru = u * u2, u * ru2
    g = t * t2 + jnp.where(top_row, 0.0, uu)
    h = t * rt2 + jnp.where(top_row, 0.0, uru)
    g2 = jnp.where(top_row, uu, t * u2 - u * t2)
    h2 = jnp.where(top_row, uru, t * ru2 - u * rt2)

    def joined(g, h):
        cross = pltpu.roll(jnp.where(left, h, g), half, 1)
        cross = jnp.where(alone, 0.0, cross)
        return jnp.where(plain, cross + g, cross - h)

    top = joined(g, h)
    top = jnp.where(top_row & (lane == 0), 0.0, top)
    return jnp.concatenate([top, joined(g2, h2)], axis=0)


def moments(scores):
    peak = jnp.max(jnp.max(scores, axis=0, keepdims=True), axis=1, keepdims=True)
    terms = jnp.exp2(scores - peak)
    total = None
    for g in range(PATCH // 8):
        part = terms[8 * g : 8 * g + 8]
        steps = float(g if g < PATCH // 16 else g - PATCH // 8)
        total = part if total is None else total + part
        first = part * steps if g == 0 else first + part * steps
    sub = lax.broadcasted_iota(jnp.int32, (8, PATCH), 0).astype(F32)
    lane = lax.broadcasted_iota(jnp.int32, (8, PATCH), 1)
    lag = jnp.where(lane < PATCH // 2, lane, lane - PATCH).astype(F32)
    return [
        jnp.sum(value, axis=0, keepdims=True)
        for value in (total, first * 8.0 + total * sub, total * lag)
    ]


def relax(flow, inside):
    def lap(value):
        return (
            pltpu.roll(value, 1, 0)
            + pltpu.roll(value, 7, 0)
            + pltpu.roll(value, 1, 1)
            + pltpu.roll(value, PATCH - 1, 1)
            - 4.0 * value
        )

    first = flow + RATE * (lap(flow) + flow - flow)
    first = jnp.where(inside, first, 0.0)
    return first + RATE * (lap(first) + flow - first)


def kernel(
    sizes, x_ref, tables_ref, out_ref, own, nxt, own_hi, own_lo, nxt_hi, nxt_lo, spec, table,
    stats, flows, around, meshes,
    own_pack, own_land, nxt_pack, nxt_land,
    local_sem, piece_send, piece_recv, own_send, own_recv, nxt_send, nxt_recv, straight_send,
    flow_send, flow_recv, mesh_send, mesh_recv,
):
    n_sec, n_ty, n_tx = sizes
    rows, cols = x_ref.shape
    node_rows, node_cols = rows // STRIDE, cols // STRIDE
    wide = node_cols * PATCH
    sec, ty, tx = lax.axis_index("sec"), lax.axis_index("ty"), lax.axis_index("tx")

    def there(dy, dx):
        ok = jnp.bool_(True)
        if dy:
            ok = (ty + dy >= 0) & (ty + dy < n_ty)
        if dx:
            in_x = (tx + dx >= 0) & (tx + dx < n_tx)
            ok = ok & in_x if dy else in_x
        return ok

    has_next = sec < n_sec - 1
    has_before = sec > 0

    def crosses(dy):
        return (ty % 2 == 1) if dy > 0 else (ty % 2 == 0)

    def straight(dy):
        return crosses(dy) & there(dy, 0)

    barrier = pltpu.get_barrier_semaphore()

    def greet(ok, s, y, x):
        @pl.when(ok)
        def _():
            pl.semaphore_signal(barrier, inc=1, device_id=(s, y, x), device_id_type=MESH)

    for dy, dx in DIRECTIONS:
        greet(there(dy, dx), sec, ty + dy, tx + dx)
    for dy in (-1, 1):
        greet(has_before & straight(dy), sec - 1, ty + dy, tx)
        greet(has_next & straight(dy), sec + 1, ty + dy, tx)
    for d in range(1, n_sec):
        pl.semaphore_signal(
            barrier, inc=1, device_id=(lax.rem(sec + d, n_sec), ty, tx), device_id_type=MESH
        )

    tile = pltpu.make_async_copy(
        x_ref, own.at[pl.ds(HALF, rows), pl.ds(PATCH, cols)], local_sem.at[0]
    )
    tile.start()
    load = pltpu.make_async_copy(tables_ref, table, local_sem.at[1])
    load.start()

    for ref in (own, nxt):
        @pl.when(ty == 0)
        def _(ref=ref):
            ref[0:HALF, :] = jnp.zeros((HALF, cols + 2 * PATCH), F32)

        @pl.when(ty == n_ty - 1)
        def _(ref=ref):
            ref[HALF + rows : 2 * HALF + rows, :] = jnp.zeros((HALF, cols + 2 * PATCH), F32)

        @pl.when(tx == 0)
        def _(ref=ref):
            ref[:, 0:PATCH] = jnp.zeros((2 * HALF + rows, PATCH), F32)

        @pl.when(tx == n_tx - 1)
        def _(ref=ref):
            ref[:, PATCH + cols :] = jnp.zeros((2 * HALF + rows, PATCH), F32)

    for index, (dy, dx) in enumerate(DIRECTIONS):
        @pl.when(jnp.logical_not(there(-dy, -dx)))
        def _(index=index):
            around[index] = jnp.zeros((8, PATCH), F32)

    for t in range(n_sec):
        @pl.when(t >= sec)
        def _(t=t):
            meshes[t] = jnp.zeros((8, PATCH), F32)

    tall = 1 + (ty > 0).astype(jnp.int32) + (ty < n_ty - 1).astype(jnp.int32)
    broad = 1 + (tx > 0).astype(jnp.int32) + (tx < n_tx - 1).astype(jnp.int32)
    apart = (crosses(-1) & there(-1, 0)).astype(jnp.int32) + (crosses(1) & there(1, 0)).astype(jnp.int32)
    ends = has_before.astype(jnp.int32) + has_next.astype(jnp.int32)
    pl.semaphore_wait(barrier, n_sec - 1 + tall * broad - 1 + apart * ends)

    pieces = [(0, HALF), (rows - HALF, HALF), None]
    pieces += [(r, HALF) for r in range(HALF, rows - HALF, HALF)]
    inner = 3

    def piece_copy(p):
        if p == 2:
            src, dst = own_pack, nxt_pack
        else:
            r, nr = pieces[p]
            src = x_ref.at[pl.ds(r, nr)]
            dst = nxt.at[pl.ds(HALF + r, nr), pl.ds(PATCH, cols)]
        return pltpu.make_async_remote_copy(
            src_ref=src,
            dst_ref=dst,
            send_sem=piece_send.at[p],
            recv_sem=piece_recv.at[p],
            device_id=(sec - 1, ty, tx),
            device_id_type=MESH,
        )

    def advance(p):
        @pl.when(has_before)
        def _():
            piece_copy(p).wait_send()
            piece_copy(p + 2).start()

    def edge(dy):
        return (0, HALF + rows) if dy < 0 else (rows - HALF, 0)

    def row_copy(dy, through, target, send, recv, to_sec):
        r, to = edge(dy)
        if through is None:
            src = x_ref.at[pl.ds(r, HALF)]
        else:
            src = through.at[pl.ds(HALF + r, HALF), pl.ds(PATCH, cols)]
        side = (dy + 1) // 2
        return pltpu.make_async_remote_copy(
            src_ref=src,
            dst_ref=target.at[pl.ds(to, HALF), pl.ds(PATCH, cols)],
            send_sem=send.at[side],
            recv_sem=recv.at[side],
            device_id=(to_sec, ty + dy, tx),
            device_id_type=MESH,
        )

    def column_copy(dx, pack, land, send, recv):
        side = (dx + 1) // 2
        return pltpu.make_async_remote_copy(
            src_ref=pack.at[side],
            dst_ref=land.at[side],
            send_sem=send.at[2 + side],
            recv_sem=recv.at[2 + side],
            device_id=(sec, ty, tx + dx),
            device_id_type=MESH,
        )

    def own_rows(dy):
        return row_copy(dy, None, own, own_send, own_recv, sec)

    def own_columns(dx):
        return column_copy(dx, own_pack, own_land, own_send, own_recv)

    def nxt_rows(dy):
        return row_copy(dy, nxt, nxt, nxt_send, nxt_recv, sec)

    def nxt_straight(dy):
        return row_copy(dy, None, nxt, straight_send, nxt_recv, sec - 1)

    def nxt_columns(dx):
        return column_copy(dx, nxt_pack, nxt_land, nxt_send, nxt_recv)

    def up_down(ok, do):
        for dy in (-1, 1):
            @pl.when(ok(dy))
            def _(dy=dy):
                do(dy)

    def sides(sign, do):
        for dx in (-1, 1):
            @pl.when(there(0, sign * dx))
            def _(dx=dx):
                do(dx)

    def handed_on(dy):
        return jnp.logical_not(crosses(dy)) & there(dy, 0)

    span = (rows + 2 * HALF) // 4
    packed_lane = lax.broadcasted_iota(jnp.int32, (span, PATCH), 1)

    def pack_columns(source, into):
        for side, at in enumerate((PATCH, cols)):
            first = 0 if side == 0 else PATCH - HALF
            value = None
            for q in range(4):
                part = source[span * q : span * (q + 1), at : at + PATCH]
                part = pltpu.roll(part, (HALF * q - first) % PATCH, 1) if HALF * q != first else part
                value = part if q == 0 else jnp.where(packed_lane >= HALF * q, part, value)
            into[side] = value

    def unpack_columns(land, target):
        for side, at in enumerate((PATCH + cols, 0)):
            first = 0 if side == 0 else PATCH - HALF

            @pl.when(there(0, 1 - 2 * side))
            def _(side=side, at=at, first=first):
                for q in range(4):
                    part = land[side]
                    part = pltpu.roll(part, (first - HALF * q) % PATCH, 1) if HALF * q != first else part
                    target[span * q : span * (q + 1), at : at + PATCH] = part

    up_down(lambda dy: there(dy, 0), lambda dy: own_rows(dy).start())

    @pl.when(has_before)
    def _():
        piece_copy(0).start()
        piece_copy(1).start()
        up_down(straight, lambda dy: nxt_straight(dy).start())

    tile.wait()
    up_down(lambda dy: there(-dy, 0), lambda dy: own_rows(dy).wait_recv())
    pack_columns(own, own_pack)
    sides(1, lambda dx: own_columns(dx).start())
    advance(0)
    load.wait()

    lane = lax.broadcasted_iota(jnp.int32, (STRIDE, PATCH), 1)
    even, odd = lane < PATCH - HALF, lane >= HALF

    def right_chunk(source, high, low, b):
        at = pl.ds(pl.multiple_of(b * STRIDE, STRIDE), STRIDE)
        parts = []
        for j in range(node_cols):
            t = j // 2
            main = source[at, (t + 1) * PATCH : (t + 2) * PATCH]
            if j % 2 == 0:
                patch = jnp.where(even, main, source[at, t * PATCH : (t + 1) * PATCH])
            else:
                patch = jnp.where(odd, main, source[at, (t + 2) * PATCH : (t + 3) * PATCH])
            parts.append(jnp.concatenate(split(patch), axis=1))
        got = jnp.dot(jnp.concatenate(parts, axis=0), table[0], preferred_element_type=F32)
        got = got[:, :PATCH] + got[:, PATCH:]
        for j in range(node_cols):
            hi, lo = split(got[j * STRIDE : (j + 1) * STRIDE])
            high[at, j * PATCH : (j + 1) * PATCH] = hi
            low[at, j * PATCH : (j + 1) * PATCH] = lo

    def left_spectrum(high, low, i, columns):
        at = pl.ds(pl.multiple_of(i * STRIDE, STRIDE), PATCH)
        both = jnp.concatenate([high[at, columns], low[at, columns]], axis=0)
        got = jnp.dot(table[1], both, preferred_element_type=F32)
        return got[:PATCH] + got[PATCH:]

    advance(1)

    @pl.when(has_next)
    def _():
        piece_copy(0).wait_recv()
        piece_copy(1).wait_recv()
        up_down(handed_on, lambda dy: nxt_rows(dy).start())

    sides(-1, lambda dx: own_columns(dx).wait_recv())
    unpack_columns(own_land, own)

    @pl.loop(0, node_rows + 1)
    def _(b):
        right_chunk(own, own_hi, own_lo, b)

    advance(2)

    @pl.when(has_next)
    def _():
        piece_copy(2).wait_recv()
        sides(1, lambda dx: nxt_columns(dx).start())

    @pl.loop(0, node_rows)
    def _(i):
        for c in range(0, wide, 2 * PATCH):
            at = pl.ds(c, 2 * PATCH)
            spec[i, :, at] = left_spectrum(own_hi, own_lo, i, at)

    advance(3)

    @pl.when(has_next)
    def _():
        up_down(lambda dy: there(-dy, 0), lambda dy: nxt_rows(dy).wait_recv())
        sides(-1, lambda dx: nxt_columns(dx).wait_recv())
        unpack_columns(nxt_land, nxt)

    right_chunk(nxt, nxt_hi, nxt_lo, 0)
    right_chunk(nxt, nxt_hi, nxt_lo, node_rows)
    advance(4)

    def inner_wait(m):
        at = pl.ds(pl.multiple_of(HALF + m * HALF, HALF), HALF)
        to = pl.ds(pl.multiple_of(2 * HALF + m * HALF, HALF), HALF)
        pltpu.make_async_remote_copy(
            src_ref=x_ref.at[at],
            dst_ref=nxt.at[to, pl.ds(PATCH, cols)],
            send_sem=piece_send.at[inner + m],
            recv_sem=piece_recv.at[inner + m],
            device_id=(sec - 1, ty, tx),
            device_id_type=MESH,
        ).wait_recv()

    @pl.loop(0, node_rows)
    def _(i):
        @pl.when(i < node_rows - 1)
        def _():
            @pl.when(has_next)
            def _():
                inner_wait(2 * i)
                inner_wait(2 * i + 1)

            right_chunk(nxt, nxt_hi, nxt_lo, i + 1)

        nodes = [slice(n * PATCH, (n + 1) * PATCH) for n in range(node_cols)]
        other = left_spectrum(nxt_hi, nxt_lo, i, pl.ds(0, wide))
        mine = spec[i]
        prods = jnp.concatenate([product(mine[:, n], other[:, n]) for n in nodes], axis=1)
        mixed = jnp.dot(
            table[2], jnp.concatenate(split(prods), axis=0), preferred_element_type=F32
        )
        hi, lo = split(mixed[:PATCH] + mixed[PATCH:])
        stacked = jnp.concatenate(
            [jnp.concatenate([hi[:, n], lo[:, n]], axis=1) for n in nodes], axis=0
        )
        corr = jnp.dot(stacked, table[3], preferred_element_type=F32)
        corr = corr[:, :PATCH] + corr[:, PATCH:]
        found = [moments(corr[n]) for n in nodes]
        for q in range(3):
            stats[q, i] = jnp.concatenate([f[q] for f in found], axis=0)

        @pl.when(i == 0)
        def _():
            for p in range(5, len(pieces) - 2):
                advance(p)

    lanes = lax.broadcasted_iota(jnp.int32, (8, PATCH), 1)
    columns = jnp.zeros((8, PATCH), F32)
    for i in range(node_rows):
        total, down, across = (jnp.sum(stats[q, i], axis=1, keepdims=True) for q in range(3))
        inv = 1.0 / total
        columns = jnp.where(lanes == i, down * inv, columns)
        columns = jnp.where(lanes == node_rows + i, across * inv, columns)
    columns = jnp.where(has_next, columns, 0.0)
    block = jnp.transpose(jnp.concatenate([columns] * 16, axis=0))[:8]
    flows[0] = block

    def flow_copy(index):
        dy, dx = DIRECTIONS[index]
        return pltpu.make_async_remote_copy(
            src_ref=flows.at[0],
            dst_ref=around.at[index],
            send_sem=flow_send.at[index],
            recv_sem=flow_recv.at[index],
            device_id=(sec, ty + dy, tx + dx),
            device_id_type=MESH,
        )

    for index, (dy, dx) in enumerate(DIRECTIONS):
        @pl.when(there(dy, dx))
        def _(index=index):
            flow_copy(index).start()
    for index, (dy, dx) in enumerate(DIRECTIONS):
        @pl.when(there(-dy, -dx))
        def _(index=index):
            flow_copy(index).wait_recv()

    lines = {}
    for dy in (-1, 0, 1):
        def from_(dx, dy=dy):
            return block if (dy, dx) == (0, 0) else around[DIRECTIONS.index((-dy, -dx))]

        line = jnp.where(lanes < 2 + node_cols, pltpu.roll(from_(0), 2, 1), pltpu.roll(from_(1), 2 + node_cols, 1))
        lines[dy] = jnp.where(lanes < 2, pltpu.roll(from_(-1), PATCH + 2 - node_cols, 1), line)

    subs = lax.broadcasted_iota(jnp.int32, (8, PATCH), 0)
    row_id = ty * node_rows + subs - 2
    col_id = tx * node_cols + lanes - 2
    inside = (
        (row_id >= 0) & (row_id < node_rows * n_ty) & (col_id >= 0) & (col_id < node_cols * n_tx)
    )
    done = []
    for c in range(2):
        base = c * node_rows
        above = pltpu.roll(lines[-1], (8 - (base + node_rows - 2)) % 8, 0)
        here = pltpu.roll(lines[0], (8 + 2 - base) % 8, 0)
        below = pltpu.roll(lines[1], (8 + 2 + node_rows - base) % 8, 0)
        flow = jnp.where(subs < 2, above, jnp.where(subs < 2 + node_rows, here, below))
        done.append(pltpu.roll(relax(flow, inside), PATCH - 2, 1))
    result = jnp.where(
        subs < node_rows, pltpu.roll(done[0], 6, 0), pltpu.roll(done[1], (8 + node_rows - 2) % 8, 0)
    )
    flows[1] = result

    def mesh_copy(d):
        return pltpu.make_async_remote_copy(
            src_ref=flows.at[1],
            dst_ref=meshes.at[sec],
            send_sem=mesh_send.at[d],
            recv_sem=mesh_recv.at[d],
            device_id=(sec + d, ty, tx),
            device_id_type=MESH,
        )

    def mesh_wait(d):
        pltpu.make_async_remote_copy(
            src_ref=flows.at[1],
            dst_ref=meshes.at[sec - d],
            send_sem=mesh_send.at[d],
            recv_sem=mesh_recv.at[d],
            device_id=(sec - d, ty, tx),
            device_id_type=MESH,
        ).wait_recv()

    for d in range(1, n_sec):
        @pl.when(sec + d < n_sec)
        def _(d=d):
            mesh_copy(d).start()
    for d in range(1, n_sec):
        @pl.when(sec - d >= 0)
        def _(d=d):
            mesh_wait(d)

    earlier = meshes[0]
    for t in range(1, n_sec):
        earlier = earlier + meshes[t]
    out_ref[0] = result
    out_ref[1] = earlier

    for index, (dy, dx) in enumerate(DIRECTIONS):
        @pl.when(there(dy, dx))
        def _(index=index):
            flow_copy(index).wait_send()

    up_down(lambda dy: there(dy, 0), lambda dy: own_rows(dy).wait_send())
    sides(1, lambda dx: own_columns(dx).wait_send())

    @pl.when(has_before)
    def _():
        for p in range(len(pieces) - 2, len(pieces)):
            piece_copy(p).wait_send()
        up_down(straight, lambda dy: nxt_straight(dy).wait_send())

    @pl.when(has_next)
    def _():
        up_down(handed_on, lambda dy: nxt_rows(dy).wait_send())
        sides(1, lambda dx: nxt_columns(dx).wait_send())

    for d in range(1, n_sec):
        @pl.when(sec + d < n_sec)
        def _(d=d):
            mesh_copy(d).wait_send()


def solution(mesh):
    sizes = tuple(mesh.shape[axis] for axis in ("sec", "ty", "tx"))

    def on_device(images):
        image = images[0]
        rows, cols = image.shape
        node_rows, node_cols = rows // STRIDE, cols // STRIDE
        high = 2 * HALF + rows
        wide = node_cols * PATCH
        around = len(DIRECTIONS)
        n_pieces = 3 + (rows - 2 * HALF) // HALF
        dma = pltpu.SemaphoreType.DMA
        out = pl.pallas_call(
            functools.partial(kernel, sizes),
            out_shape=jax.ShapeDtypeStruct((2, 8, PATCH), F32),
            in_specs=[pl.BlockSpec(memory_space=pl.ANY)] * 2,
            out_specs=pl.BlockSpec(memory_space=pltpu.VMEM),
            scratch_shapes=[
                pltpu.VMEM((high, cols + 2 * PATCH), F32),
                pltpu.VMEM((high, cols + 2 * PATCH), F32),
                pltpu.VMEM((high, wide), BF16),
                pltpu.VMEM((high, wide), BF16),
                pltpu.VMEM((high, wide), BF16),
                pltpu.VMEM((high, wide), BF16),
                pltpu.VMEM((node_rows, PATCH, wide), F32),
                pltpu.VMEM((4, 2 * PATCH, 2 * PATCH), BF16),
                pltpu.VMEM((3, node_rows, node_cols, PATCH), F32),
                pltpu.VMEM((2, 8, PATCH), F32),
                pltpu.VMEM((around, 8, PATCH), F32),
                pltpu.VMEM((sizes[0], 8, PATCH), F32),
                pltpu.VMEM((2, high // 4, PATCH), F32),
                pltpu.VMEM((2, high // 4, PATCH), F32),
                pltpu.VMEM((2, high // 4, PATCH), F32),
                pltpu.VMEM((2, high // 4, PATCH), F32),
                dma((2,)),
                dma((n_pieces,)),
                dma((n_pieces,)),
                dma((4,)),
                dma((4,)),
                dma((4,)),
                dma((4,)),
                dma((2,)),
                dma((around,)),
                dma((around,)),
                dma((sizes[0],)),
                dma((sizes[0],)),
            ],
            compiler_params=pltpu.CompilerParams(
                collective_id=0, has_side_effects=True, vmem_limit_bytes=60 * 1024 * 1024
            ),
        )(image, jnp.asarray(tables()))
        out = out[:, :, :node_cols].reshape(2, 1, 2, node_rows, node_cols)
        return out[0], out[1]

    return jax.shard_map(
        on_device,
        mesh=mesh,
        in_specs=(P("sec", "ty", "tx"),),
        out_specs=(P("sec", None, "ty", "tx"), P("sec", None, "ty", "tx")),
        check_vma=False,
    )
```

```python
import functools

import jax
import jax.numpy as jnp
import ml_dtypes
import numpy as np
from jax import lax
from jax.experimental import pallas as pl
from jax.experimental.pallas import tpu as pltpu
from jax.sharding import PartitionSpec as P

PATCH = 128
STRIDE = 64
HALF = 32
RATE = 0.25

MESH = pl.DeviceIdType.MESH
DIRECTIONS = [(dy, dx) for dy in (-1, 0, 1) for dx in (-1, 0, 1) if (dy, dx) != (0, 0)]
F32 = jnp.float32
BF16 = jnp.bfloat16


def split_table(table):
    high = table.astype(ml_dtypes.bfloat16)
    low = (table - high.astype(np.float64)).astype(ml_dtypes.bfloat16)
    return high, low


def tables():
    half = PATCH // 2
    point = np.arange(PATCH)
    angle = 2.0 * np.pi / PATCH
    packed = np.zeros((PATCH, PATCH))
    for k in range(half):
        packed[k] = np.cos(angle * (k * point % PATCH))
        packed[half + k] = np.sin(angle * (k * point % PATCH))
    packed[half] = np.cos(np.pi * point)
    weight = np.full(PATCH, 2.0)
    weight[0] = weight[half] = 1.0
    inverse = packed.T * weight[None, :] / PATCH

    def left(table):
        high, low = split_table(table)
        return np.block([[high, high], [low, low]])

    def right(table):
        high, low = split_table(table)
        return np.block([[high, low], [high, low]])

    scale = np.log2(np.e) / PATCH
    return np.stack(
        [right(packed.T), left(packed), left(inverse), right(inverse.T * scale)]
    ).astype(ml_dtypes.bfloat16)


def split(value):
    high = value.astype(BF16)
    low = (value - high.astype(F32)).astype(BF16)
    return high, low


def product(own, other):
    half = PATCH // 2
    lane = lax.broadcasted_iota(jnp.int32, (half, PATCH), 1)
    row = lax.broadcasted_iota(jnp.int32, (half, PATCH), 0)
    left = lane < half
    alone = (lane == 0) | (lane == half)
    plain = left | alone
    top_row = row == 0
    t, u = own[:half], own[half:]
    t2, u2 = other[:half], other[half:]
    rt2 = pltpu.roll(t2, half, 1)
    ru2 = pltpu.roll(u2, half, 1)
    uu, uru = u * u2, u * ru2
    g = t * t2 + jnp.where(top_row, 0.0, uu)
    h = t * rt2 + jnp.where(top_row, 0.0, uru)
    g2 = jnp.where(top_row, uu, t * u2 - u * t2)
    h2 = jnp.where(top_row, uru, t * ru2 - u * rt2)

    def joined(g, h):
        cross = pltpu.roll(jnp.where(left, h, g), half, 1)
        cross = jnp.where(alone, 0.0, cross)
        return jnp.where(plain, cross + g, cross - h)

    top = joined(g, h)
    top = jnp.where(top_row & (lane == 0), 0.0, top)
    return jnp.concatenate([top, joined(g2, h2)], axis=0)


def moments(scores):
    peak = jnp.max(jnp.max(scores, axis=0, keepdims=True), axis=1, keepdims=True)
    terms = jnp.exp2(scores - peak)
    total = None
    for g in range(PATCH // 8):
        part = terms[8 * g : 8 * g + 8]
        steps = float(g if g < PATCH // 16 else g - PATCH // 8)
        total = part if total is None else total + part
        first = part * steps if g == 0 else first + part * steps
    sub = lax.broadcasted_iota(jnp.int32, (8, PATCH), 0).astype(F32)
    lane = lax.broadcasted_iota(jnp.int32, (8, PATCH), 1)
    lag = jnp.where(lane < PATCH // 2, lane, lane - PATCH).astype(F32)
    return [
        jnp.sum(value, axis=0, keepdims=True)
        for value in (total, first * 8.0 + total * sub, total * lag)
    ]


def relax(flow, inside):
    def lap(value):
        return (
            pltpu.roll(value, 1, 0)
            + pltpu.roll(value, 7, 0)
            + pltpu.roll(value, 1, 1)
            + pltpu.roll(value, PATCH - 1, 1)
            - 4.0 * value
        )

    first = flow + RATE * (lap(flow) + flow - flow)
    first = jnp.where(inside, first, 0.0)
    return first + RATE * (lap(first) + flow - first)


def kernel(
    sizes, x_ref, tables_ref, out_ref, own, nxt, own_hi, own_lo, nxt_hi, nxt_lo, spec, table,
    stats, flows, around, meshes,
    own_pack, own_land, nxt_pack, nxt_land,
    local_sem, piece_send, piece_recv, own_send, own_recv, nxt_send, nxt_recv, straight_send,
    flow_send, flow_recv, mesh_send, mesh_recv,
):
    n_sec, n_ty, n_tx = sizes
    rows, cols = x_ref.shape
    node_rows, node_cols = rows // STRIDE, cols // STRIDE
    wide = node_cols * PATCH
    sec, ty, tx = lax.axis_index("sec"), lax.axis_index("ty"), lax.axis_index("tx")

    def there(dy, dx):
        ok = jnp.bool_(True)
        if dy:
            ok = (ty + dy >= 0) & (ty + dy < n_ty)
        if dx:
            in_x = (tx + dx >= 0) & (tx + dx < n_tx)
            ok = ok & in_x if dy else in_x
        return ok

    has_next = sec < n_sec - 1
    has_before = sec > 0

    def crosses(dy):
        return (ty % 2 == 1) if dy > 0 else (ty % 2 == 0)

    def straight(dy):
        return crosses(dy) & there(dy, 0)

    barrier = pltpu.get_barrier_semaphore()

    def greet(ok, s, y, x):
        @pl.when(ok)
        def _():
            pl.semaphore_signal(barrier, inc=1, device_id=(s, y, x), device_id_type=MESH)

    for dy, dx in DIRECTIONS:
        greet(there(dy, dx), sec, ty + dy, tx + dx)
    for dy in (-1, 1):
        greet(has_before & straight(dy), sec - 1, ty + dy, tx)
        greet(has_next & straight(dy), sec + 1, ty + dy, tx)
    for d in range(1, n_sec):
        pl.semaphore_signal(
            barrier, inc=1, device_id=(lax.rem(sec + d, n_sec), ty, tx), device_id_type=MESH
        )

    tile = pltpu.make_async_copy(
        x_ref, own.at[pl.ds(HALF, rows), pl.ds(PATCH, cols)], local_sem.at[0]
    )
    tile.start()
    load = pltpu.make_async_copy(tables_ref, table, local_sem.at[1])
    load.start()

    for ref in (own, nxt):
        @pl.when(ty == 0)
        def _(ref=ref):
            ref[0:HALF, :] = jnp.zeros((HALF, cols + 2 * PATCH), F32)

        @pl.when(ty == n_ty - 1)
        def _(ref=ref):
            ref[HALF + rows : 2 * HALF + rows, :] = jnp.zeros((HALF, cols + 2 * PATCH), F32)

        @pl.when(tx == 0)
        def _(ref=ref):
            ref[:, 0:PATCH] = jnp.zeros((2 * HALF + rows, PATCH), F32)

        @pl.when(tx == n_tx - 1)
        def _(ref=ref):
            ref[:, PATCH + cols :] = jnp.zeros((2 * HALF + rows, PATCH), F32)

    for index, (dy, dx) in enumerate(DIRECTIONS):
        @pl.when(jnp.logical_not(there(-dy, -dx)))
        def _(index=index):
            around[index] = jnp.zeros((8, PATCH), F32)

    for t in range(n_sec):
        @pl.when(t >= sec)
        def _(t=t):
            meshes[t] = jnp.zeros((8, PATCH), F32)

    tall = 1 + (ty > 0).astype(jnp.int32) + (ty < n_ty - 1).astype(jnp.int32)
    broad = 1 + (tx > 0).astype(jnp.int32) + (tx < n_tx - 1).astype(jnp.int32)
    apart = (crosses(-1) & there(-1, 0)).astype(jnp.int32) + (crosses(1) & there(1, 0)).astype(jnp.int32)
    ends = has_before.astype(jnp.int32) + has_next.astype(jnp.int32)
    pl.semaphore_wait(barrier, n_sec - 1 + tall * broad - 1 + apart * ends)

    middle = rows // 2 - HALF
    pieces = [
        (0, HALF, 0, cols),
        (rows - HALF, HALF, 0, cols),
        None,
        (HALF, STRIDE, 0, cols),
        (rows - HALF - STRIDE, STRIDE, 0, cols),
        (middle, STRIDE, 0, 2 * PATCH),
        (middle, STRIDE, 3 * PATCH, PATCH),
        (middle, STRIDE, 2 * PATCH, PATCH),
    ]

    def piece_copy(p):
        if p == 2:
            src, dst = own_pack, nxt_pack
        else:
            r, nr, c, nc = pieces[p]
            src = x_ref.at[pl.ds(r, nr), pl.ds(c, nc)]
            dst = nxt.at[pl.ds(HALF + r, nr), pl.ds(PATCH + c, nc)]
        return pltpu.make_async_remote_copy(
            src_ref=src,
            dst_ref=dst,
            send_sem=piece_send.at[p],
            recv_sem=piece_recv.at[p],
            device_id=(sec - 1, ty, tx),
            device_id_type=MESH,
        )

    def arrived(*indices):
        @pl.when(has_next)
        def _():
            for p in indices:
                piece_copy(p).wait_recv()

    def edge(dy):
        return (0, HALF + rows) if dy < 0 else (rows - HALF, 0)

    def row_copy(dy, through, target, send, recv, to_sec):
        r, to = edge(dy)
        if through is None:
            src = x_ref.at[pl.ds(r, HALF)]
        else:
            src = through.at[pl.ds(HALF + r, HALF), pl.ds(PATCH, cols)]
        side = (dy + 1) // 2
        return pltpu.make_async_remote_copy(
            src_ref=src,
            dst_ref=target.at[pl.ds(to, HALF), pl.ds(PATCH, cols)],
            send_sem=send.at[side],
            recv_sem=recv.at[side],
            device_id=(to_sec, ty + dy, tx),
            device_id_type=MESH,
        )

    def column_copy(dx, pack, land, send, recv):
        side = (dx + 1) // 2
        return pltpu.make_async_remote_copy(
            src_ref=pack.at[side],
            dst_ref=land.at[side],
            send_sem=send.at[2 + side],
            recv_sem=recv.at[2 + side],
            device_id=(sec, ty, tx + dx),
            device_id_type=MESH,
        )

    def own_rows(dy):
        return row_copy(dy, None, own, own_send, own_recv, sec)

    def own_columns(dx):
        return column_copy(dx, own_pack, own_land, own_send, own_recv)

    def nxt_rows(dy):
        return row_copy(dy, nxt, nxt, nxt_send, nxt_recv, sec)

    def nxt_straight(dy):
        return row_copy(dy, None, nxt, straight_send, nxt_recv, sec - 1)

    def nxt_columns(dx):
        return column_copy(dx, nxt_pack, nxt_land, nxt_send, nxt_recv)

    def up_down(ok, do):
        for dy in (-1, 1):
            @pl.when(ok(dy))
            def _(dy=dy):
                do(dy)

    def sides(sign, do):
        for dx in (-1, 1):
            @pl.when(there(0, sign * dx))
            def _(dx=dx):
                do(dx)

    def handed_on(dy):
        return jnp.logical_not(crosses(dy)) & there(dy, 0)

    span = (rows + 2 * HALF) // 4
    packed_lane = lax.broadcasted_iota(jnp.int32, (span, PATCH), 1)

    def pack_columns(source, into):
        for side, at in enumerate((PATCH, cols)):
            first = 0 if side == 0 else PATCH - HALF
            value = None
            for q in range(4):
                part = source[span * q : span * (q + 1), at : at + PATCH]
                part = pltpu.roll(part, (HALF * q - first) % PATCH, 1) if HALF * q != first else part
                value = part if q == 0 else jnp.where(packed_lane >= HALF * q, part, value)
            into[side] = value

    def unpack_columns(land, target):
        for side, at in enumerate((PATCH + cols, 0)):
            first = 0 if side == 0 else PATCH - HALF

            @pl.when(there(0, 1 - 2 * side))
            def _(side=side, at=at, first=first):
                for q in range(4):
                    part = land[side]
                    part = pltpu.roll(part, (first - HALF * q) % PATCH, 1) if HALF * q != first else part
                    target[span * q : span * (q + 1), at : at + PATCH] = part

    up_down(lambda dy: there(dy, 0), lambda dy: own_rows(dy).start())

    @pl.when(has_before)
    def _():
        piece_copy(0).start()
        piece_copy(1).start()
        up_down(straight, lambda dy: nxt_straight(dy).start())

    tile.wait()
    up_down(lambda dy: there(-dy, 0), lambda dy: own_rows(dy).wait_recv())
    pack_columns(own, own_pack)
    sides(1, lambda dx: own_columns(dx).start())

    @pl.when(has_before)
    def _():
        for p in range(2, len(pieces)):
            piece_copy(p).start()

    load.wait()

    lane = lax.broadcasted_iota(jnp.int32, (STRIDE, PATCH), 1)
    even, odd = lane < PATCH - HALF, lane >= HALF

    order = [node_cols - 1, *range(node_cols - 1)]
    part_cols = node_cols // 2
    parts = (range(0, part_cols), range(part_cols, node_cols))
    every = range(node_cols)

    def right_chunk(source, high, low, b, places):
        at = pl.ds(b * STRIDE if isinstance(b, int) else pl.multiple_of(b * STRIDE, STRIDE), STRIDE)
        patches = []
        for j in (order[p] for p in places):
            t = j // 2
            main = source[at, (t + 1) * PATCH : (t + 2) * PATCH]
            if j % 2 == 0:
                patch = jnp.where(even, main, source[at, t * PATCH : (t + 1) * PATCH])
            else:
                patch = jnp.where(odd, main, source[at, (t + 2) * PATCH : (t + 3) * PATCH])
            patches.append(jnp.concatenate(split(patch), axis=1))
        got = jnp.dot(jnp.concatenate(patches, axis=0), table[0], preferred_element_type=F32)
        got = got[:, :PATCH] + got[:, PATCH:]
        for n, p in enumerate(places):
            hi, lo = split(got[n * STRIDE : (n + 1) * STRIDE])
            high[at, p * PATCH : (p + 1) * PATCH] = hi
            low[at, p * PATCH : (p + 1) * PATCH] = lo

    def left_spectrum(high, low, i, columns):
        at = pl.ds(pl.multiple_of(i * STRIDE, STRIDE), PATCH)
        both = jnp.concatenate([high[at, columns], low[at, columns]], axis=0)
        got = jnp.dot(table[1], both, preferred_element_type=F32)
        return got[:PATCH] + got[PATCH:]


    @pl.when(has_next)
    def _():
        piece_copy(0).wait_recv()
        piece_copy(1).wait_recv()
        up_down(handed_on, lambda dy: nxt_rows(dy).start())

    sides(-1, lambda dx: own_columns(dx).wait_recv())
    unpack_columns(own_land, own)

    @pl.loop(0, node_rows + 1)
    def _(b):
        right_chunk(own, own_hi, own_lo, b, every)


    @pl.when(has_next)
    def _():
        piece_copy(2).wait_recv()
        sides(1, lambda dx: nxt_columns(dx).start())

    @pl.loop(0, node_rows)
    def _(i):
        for c in range(0, wide, 2 * PATCH):
            at = pl.ds(c, 2 * PATCH)
            spec[i, :, at] = left_spectrum(own_hi, own_lo, i, at)


    @pl.when(has_next)
    def _():
        up_down(lambda dy: there(-dy, 0), lambda dy: nxt_rows(dy).wait_recv())
        sides(-1, lambda dx: nxt_columns(dx).wait_recv())
        unpack_columns(nxt_land, nxt)

    right_chunk(nxt, nxt_hi, nxt_lo, 0, every)
    right_chunk(nxt, nxt_hi, nxt_lo, node_rows, every)

    lanes = lax.broadcasted_iota(jnp.int32, (8, PATCH), 1)

    def flow_block(indices):
        columns = jnp.zeros((8, PATCH), F32)
        for i in indices:
            total, down, across = (jnp.sum(stats[q, i], axis=1, keepdims=True) for q in range(3))
            inv = 1.0 / total
            columns = jnp.where(lanes == i, down * inv, columns)
            columns = jnp.where(lanes == node_rows + i, across * inv, columns)
        columns = pltpu.roll(jnp.where(has_next, columns, 0.0), node_cols - 1, 0)
        return jnp.transpose(jnp.concatenate([columns] * 16, axis=0))[:8]

    def flow_copy(index):
        dy, dx = DIRECTIONS[index]
        return pltpu.make_async_remote_copy(
            src_ref=flows.at[1 if dy and dx else 0],
            dst_ref=around.at[index],
            send_sem=flow_send.at[index],
            recv_sem=flow_recv.at[index],
            device_id=(sec, ty + dy, tx + dx),
            device_id_type=MESH,
        )

    def flow_each(sign, corners, do):
        for index, (dy, dx) in enumerate(DIRECTIONS):
            if bool(dy and dx) in corners:
                @pl.when(there(sign * dy, sign * dx))
                def _(index=index):
                    do(index)

    last = node_rows - 1

    @pl.loop(0, 4)
    def _(step):
        @pl.when(step == 0)
        def _():
            arrived(3)
            right_chunk(nxt, nxt_hi, nxt_lo, 1, every)

        @pl.when(step == 1)
        def _():
            arrived(4)
            right_chunk(nxt, nxt_hi, nxt_lo, last, every)

        @pl.when(step == 2)
        def _():
            flows[1] = flow_block((0, last))
            flow_each(1, (True,), lambda k: flow_copy(k).start())
            arrived(5, 6)
            right_chunk(nxt, nxt_hi, nxt_lo, 2, parts[0])

        @pl.when(step == 3)
        def _():
            arrived(7)
            right_chunk(nxt, nxt_hi, nxt_lo, 2, parts[1])

        halves = [
            (jnp.where(step < 2, step * last, 1 + h), jnp.where(step < 2, h, step - 2)) for h in range(2)
        ]
        nodes = [slice(n * PATCH, (n + 1) * PATCH) for n in range(node_cols)]
        mine, other = [], []
        for i, g in halves:
            columns = pl.ds(pl.multiple_of(g * part_cols * PATCH, PATCH), part_cols * PATCH)
            other.append(left_spectrum(nxt_hi, nxt_lo, i, columns))
            mine.append(spec[i, :, columns])
        mine, other = (jnp.concatenate(value, axis=1) for value in (mine, other))
        prods = jnp.concatenate([product(mine[:, n], other[:, n]) for n in nodes], axis=1)
        mixed = jnp.dot(
            table[2], jnp.concatenate(split(prods), axis=0), preferred_element_type=F32
        )
        hi, lo = split(mixed[:PATCH] + mixed[PATCH:])
        stacked = jnp.concatenate(
            [jnp.concatenate([hi[:, n], lo[:, n]], axis=1) for n in nodes], axis=0
        )
        corr = jnp.dot(stacked, table[3], preferred_element_type=F32)
        corr = corr[:, :PATCH] + corr[:, PATCH:]
        found = [moments(corr[n]) for n in nodes]
        for h, (i, g) in enumerate(halves):
            for q in range(3):
                stats[q, i, pl.ds(g * part_cols, part_cols), :] = jnp.concatenate(
                    [f[q] for f in found[h * part_cols : (h + 1) * part_cols]], axis=0
                )

    block = flow_block(range(node_rows))
    flows[0] = block
    flow_each(1, (False,), lambda k: flow_copy(k).start())

    up_down(lambda dy: there(dy, 0), lambda dy: own_rows(dy).wait_send())
    sides(1, lambda dx: own_columns(dx).wait_send())

    @pl.when(has_before)
    def _():
        for p in range(len(pieces)):
            piece_copy(p).wait_send()
        up_down(straight, lambda dy: nxt_straight(dy).wait_send())

    @pl.when(has_next)
    def _():
        up_down(handed_on, lambda dy: nxt_rows(dy).wait_send())
        sides(1, lambda dx: nxt_columns(dx).wait_send())

    flow_each(-1, (True, False), lambda k: flow_copy(k).wait_recv())

    lines = {}
    for dy in (-1, 0, 1):
        def from_(dx, dy=dy):
            return block if (dy, dx) == (0, 0) else around[DIRECTIONS.index((-dy, -dx))]

        line = jnp.where(lanes < 2 + node_cols, pltpu.roll(from_(0), 2, 1), pltpu.roll(from_(1), 2 + node_cols, 1))
        lines[dy] = jnp.where(lanes < 2, pltpu.roll(from_(-1), PATCH + 2 - node_cols, 1), line)

    subs = lax.broadcasted_iota(jnp.int32, (8, PATCH), 0)
    row_id = ty * node_rows + subs - 2
    col_id = tx * node_cols + lanes - 2
    inside = (
        (row_id >= 0) & (row_id < node_rows * n_ty) & (col_id >= 0) & (col_id < node_cols * n_tx)
    )
    done = []
    for c in range(2):
        base = c * node_rows
        above = pltpu.roll(lines[-1], (8 - (base + node_rows - 2)) % 8, 0)
        here = pltpu.roll(lines[0], (8 + 2 - base) % 8, 0)
        below = pltpu.roll(lines[1], (8 + 2 + node_rows - base) % 8, 0)
        flow = jnp.where(subs < 2, above, jnp.where(subs < 2 + node_rows, here, below))
        done.append(pltpu.roll(relax(flow, inside), PATCH - 2, 1))
    result = jnp.where(
        subs < node_rows, pltpu.roll(done[0], 6, 0), pltpu.roll(done[1], (8 + node_rows - 2) % 8, 0)
    )
    flows[2] = result

    def mesh_copy(d):
        return pltpu.make_async_remote_copy(
            src_ref=flows.at[2],
            dst_ref=meshes.at[sec],
            send_sem=mesh_send.at[d],
            recv_sem=mesh_recv.at[d],
            device_id=(sec + d, ty, tx),
            device_id_type=MESH,
        )

    def mesh_wait(d):
        pltpu.make_async_remote_copy(
            src_ref=flows.at[2],
            dst_ref=meshes.at[sec - d],
            send_sem=mesh_send.at[d],
            recv_sem=mesh_recv.at[d],
            device_id=(sec - d, ty, tx),
            device_id_type=MESH,
        ).wait_recv()

    for d in range(1, n_sec):
        @pl.when(sec + d < n_sec)
        def _(d=d):
            mesh_copy(d).start()
    for d in range(1, n_sec):
        @pl.when(sec - d >= 0)
        def _(d=d):
            mesh_wait(d)

    earlier = meshes[0]
    for t in range(1, n_sec):
        earlier = earlier + meshes[t]
    out_ref[0] = result
    out_ref[1] = earlier

    flow_each(1, (True, False), lambda k: flow_copy(k).wait_send())
    for d in range(1, n_sec):
        @pl.when(sec + d < n_sec)
        def _(d=d):
            mesh_copy(d).wait_send()


def solution(mesh):
    sizes = tuple(mesh.shape[axis] for axis in ("sec", "ty", "tx"))

    def on_device(images):
        image = images[0]
        rows, cols = image.shape
        node_rows, node_cols = rows // STRIDE, cols // STRIDE
        high = 2 * HALF + rows
        wide = node_cols * PATCH
        around = len(DIRECTIONS)
        n_pieces = 8
        dma = pltpu.SemaphoreType.DMA
        out = pl.pallas_call(
            functools.partial(kernel, sizes),
            out_shape=jax.ShapeDtypeStruct((2, 8, PATCH), F32),
            in_specs=[pl.BlockSpec(memory_space=pl.ANY)] * 2,
            out_specs=pl.BlockSpec(memory_space=pltpu.VMEM),
            scratch_shapes=[
                pltpu.VMEM((high, cols + 2 * PATCH), F32),
                pltpu.VMEM((high, cols + 2 * PATCH), F32),
                pltpu.VMEM((high, wide), BF16),
                pltpu.VMEM((high, wide), BF16),
                pltpu.VMEM((high, wide), BF16),
                pltpu.VMEM((high, wide), BF16),
                pltpu.VMEM((node_rows, PATCH, wide), F32),
                pltpu.VMEM((4, 2 * PATCH, 2 * PATCH), BF16),
                pltpu.VMEM((3, node_rows, node_cols, PATCH), F32),
                pltpu.VMEM((3, 8, PATCH), F32),
                pltpu.VMEM((around, 8, PATCH), F32),
                pltpu.VMEM((sizes[0], 8, PATCH), F32),
                pltpu.VMEM((2, high // 4, PATCH), F32),
                pltpu.VMEM((2, high // 4, PATCH), F32),
                pltpu.VMEM((2, high // 4, PATCH), F32),
                pltpu.VMEM((2, high // 4, PATCH), F32),
                dma((2,)),
                dma((n_pieces,)),
                dma((n_pieces,)),
                dma((4,)),
                dma((4,)),
                dma((4,)),
                dma((4,)),
                dma((2,)),
                dma((around,)),
                dma((around,)),
                dma((sizes[0],)),
                dma((sizes[0],)),
            ],
            compiler_params=pltpu.CompilerParams(
                collective_id=0, has_side_effects=True, vmem_limit_bytes=60 * 1024 * 1024
            ),
        )(image, jnp.asarray(tables()))
        out = out[:, :, :node_cols].reshape(2, 1, 2, node_rows, node_cols)
        return out[0], out[1]

    return jax.shard_map(
        on_device,
        mesh=mesh,
        in_specs=(P("sec", "ty", "tx"),),
        out_specs=(P("sec", None, "ty", "tx"), P("sec", None, "ty", "tx")),
        check_vma=False,
    )
```

```python
import functools

import jax
import jax.numpy as jnp
import ml_dtypes
import numpy as np
from jax import lax
from jax.experimental import pallas as pl
from jax.experimental.pallas import tpu as pltpu
from jax.sharding import PartitionSpec as P

PATCH = 128
STRIDE = 64
HALF = 32
RATE = 0.25

MESH = pl.DeviceIdType.MESH
CORNERS = [(dy, dx) for dy in (-1, 1) for dx in (-1, 1)]
DIRECTIONS = [(dy, dx) for dy in (-1, 0, 1) for dx in (-1, 0, 1) if (dy, dx) != (0, 0)]
F32 = jnp.float32
BF16 = jnp.bfloat16


def split_table(table):
    high = table.astype(ml_dtypes.bfloat16)
    low = (table - high.astype(np.float64)).astype(ml_dtypes.bfloat16)
    return high, low


def tables():
    half = PATCH // 2
    point = np.arange(PATCH)
    angle = 2.0 * np.pi / PATCH
    packed = np.zeros((PATCH, PATCH))
    for k in range(half):
        packed[k] = np.cos(angle * (k * point % PATCH))
        packed[half + k] = np.sin(angle * (k * point % PATCH))
    packed[half] = np.cos(np.pi * point)
    weight = np.full(PATCH, 2.0)
    weight[0] = weight[half] = 1.0
    inverse = packed.T * weight[None, :] / PATCH

    def left(table):
        high, low = split_table(table)
        return np.block([[high, high], [low, low]])

    def right(table):
        high, low = split_table(table)
        return np.block([[high, low], [high, low]])

    scale = np.log2(np.e) / PATCH
    return np.stack(
        [right(packed.T), left(packed), left(inverse), right(inverse.T * scale)]
    ).astype(ml_dtypes.bfloat16)


def split(value):
    high = value.astype(BF16)
    low = (value - high.astype(F32)).astype(BF16)
    return high, low


def product(own, other):
    half = PATCH // 2
    lane = lax.broadcasted_iota(jnp.int32, (half, PATCH), 1)
    row = lax.broadcasted_iota(jnp.int32, (half, PATCH), 0)
    left = lane < half
    alone = (lane == 0) | (lane == half)
    plain = left | alone
    top_row = row == 0
    t, u = own[:half], own[half:]
    t2, u2 = other[:half], other[half:]
    rt2 = pltpu.roll(t2, half, 1)
    ru2 = pltpu.roll(u2, half, 1)
    uu, uru = u * u2, u * ru2
    g = t * t2 + jnp.where(top_row, 0.0, uu)
    h = t * rt2 + jnp.where(top_row, 0.0, uru)
    g2 = jnp.where(top_row, uu, t * u2 - u * t2)
    h2 = jnp.where(top_row, uru, t * ru2 - u * rt2)

    def joined(g, h):
        cross = pltpu.roll(jnp.where(left, h, g), half, 1)
        cross = jnp.where(alone, 0.0, cross)
        return jnp.where(plain, cross + g, cross - h)

    top = joined(g, h)
    top = jnp.where(top_row & (lane == 0), 0.0, top)
    return jnp.concatenate([top, joined(g2, h2)], axis=0)


def moments(scores):
    peak = jnp.max(jnp.max(scores, axis=0, keepdims=True), axis=1, keepdims=True)
    terms = jnp.exp2(scores - peak)
    total = None
    for g in range(PATCH // 8):
        part = terms[8 * g : 8 * g + 8]
        steps = float(g if g < PATCH // 16 else g - PATCH // 8)
        total = part if total is None else total + part
        first = part * steps if g == 0 else first + part * steps
    sub = lax.broadcasted_iota(jnp.int32, (8, PATCH), 0).astype(F32)
    lane = lax.broadcasted_iota(jnp.int32, (8, PATCH), 1)
    lag = jnp.where(lane < PATCH // 2, lane, lane - PATCH).astype(F32)
    return [
        jnp.sum(value, axis=0, keepdims=True)
        for value in (total, first * 8.0 + total * sub, total * lag)
    ]


def relax(flow, inside):
    def lap(value):
        return (
            pltpu.roll(value, 1, 0)
            + pltpu.roll(value, 7, 0)
            + pltpu.roll(value, 1, 1)
            + pltpu.roll(value, PATCH - 1, 1)
            - 4.0 * value
        )

    first = flow + RATE * (lap(flow) + flow - flow)
    first = jnp.where(inside, first, 0.0)
    return first + RATE * (lap(first) + flow - first)


def kernel(
    sizes, x_ref, tables_ref, out_ref, own, nxt, own_hi, own_lo, nxt_hi, nxt_lo, spec, table,
    stats, flows, around, meshes,
    own_pack, own_land, nxt_pack, nxt_land, own_rest, nxt_rest, tips, own_tips, nxt_tips,
    local_sem, piece_send, piece_recv, own_send, own_recv, nxt_send, nxt_recv, straight_send,
    tip_send, own_tip_recv, nxt_tip_recv,
    flow_send, flow_recv, mesh_send, mesh_recv,
):
    n_sec, n_ty, n_tx = sizes
    rows, cols = x_ref.shape
    node_rows, node_cols = rows // STRIDE, cols // STRIDE
    wide = node_cols * PATCH
    sec, ty, tx = lax.axis_index("sec"), lax.axis_index("ty"), lax.axis_index("tx")

    def there(dy, dx):
        ok = jnp.bool_(True)
        if dy:
            ok = (ty + dy >= 0) & (ty + dy < n_ty)
        if dx:
            in_x = (tx + dx >= 0) & (tx + dx < n_tx)
            ok = ok & in_x if dy else in_x
        return ok

    has_next = sec < n_sec - 1
    has_before = sec > 0

    def crosses(dy):
        return (ty % 2 == 1) if dy > 0 else (ty % 2 == 0)

    def straight(dy):
        return crosses(dy) & there(dy, 0)

    barrier = pltpu.get_barrier_semaphore()

    def greet(ok, s, y, x):
        @pl.when(ok)
        def _():
            pl.semaphore_signal(barrier, inc=1, device_id=(s, y, x), device_id_type=MESH)

    for dy, dx in DIRECTIONS:
        greet(there(dy, dx), sec, ty + dy, tx + dx)
    for dy in (-1, 1):
        greet(has_before & straight(dy), sec - 1, ty + dy, tx)
        greet(has_next & straight(dy), sec + 1, ty + dy, tx)
    for dy, dx in CORNERS:
        greet(has_before & there(dy, dx), sec - 1, ty + dy, tx + dx)
        greet(has_next & there(dy, dx), sec + 1, ty + dy, tx + dx)
    for d in range(1, n_sec):
        pl.semaphore_signal(
            barrier, inc=1, device_id=(lax.rem(sec + d, n_sec), ty, tx), device_id_type=MESH
        )

    tile = pltpu.make_async_copy(
        x_ref, own.at[pl.ds(HALF, rows), pl.ds(PATCH, cols)], local_sem.at[0]
    )
    tile.start()
    load = pltpu.make_async_copy(tables_ref, table, local_sem.at[1])
    load.start()

    for ref in (own, nxt):
        @pl.when(ty == 0)
        def _(ref=ref):
            ref[0:HALF, :] = jnp.zeros((HALF, cols + 2 * PATCH), F32)

        @pl.when(ty == n_ty - 1)
        def _(ref=ref):
            ref[HALF + rows : 2 * HALF + rows, :] = jnp.zeros((HALF, cols + 2 * PATCH), F32)

        @pl.when(tx == 0)
        def _(ref=ref):
            ref[:, 0:PATCH] = jnp.zeros((2 * HALF + rows, PATCH), F32)

        @pl.when(tx == n_tx - 1)
        def _(ref=ref):
            ref[:, PATCH + cols :] = jnp.zeros((2 * HALF + rows, PATCH), F32)

    for index, (dy, dx) in enumerate(DIRECTIONS):
        @pl.when(jnp.logical_not(there(-dy, -dx)))
        def _(index=index):
            around[index] = jnp.zeros((8, PATCH), F32)

    for t in range(n_sec):
        @pl.when(t >= sec)
        def _(t=t):
            meshes[t] = jnp.zeros((8, PATCH), F32)

    span = rows // 4
    spans = [(HALF + span * q, span) for q in range(4)]

    def turned(value, by):
        return pltpu.roll(value, by % PATCH, 1) if by % PATCH else value

    def packed(source, where, side):
        lane = lax.broadcasted_iota(jnp.int32, (where[0][1], PATCH), 1)
        at, first = ((PATCH, 0), (cols, PATCH - HALF))[side]
        value = None
        for q, (r, nr) in enumerate(where):
            part = turned(source[r : r + nr, at : at + PATCH], HALF * q - first)
            value = part if q == 0 else jnp.where(lane >= HALF * q, part, value)
        return value

    def unpack(value, target, where, side):
        at, first = ((PATCH + cols, 0), (0, PATCH - HALF))[side]
        for q, (r, nr) in enumerate(where):
            target[r : r + nr, at : at + PATCH] = turned(value, first - HALF * q)

    def unpack_columns(land, target):
        for side in range(2):
            @pl.when(there(0, 1 - 2 * side))
            def _(side=side):
                unpack(land[side], target, spans, side)

    def eighths(start):
        return [(start + 8 * q, 8) for q in range(4)]

    def unpack_tip(land, target, k):
        dy, dx = CORNERS[k]
        unpack(land[k], target, eighths(HALF + rows if dy < 0 else 0), (dx + 1) // 2)

    def pack_rest(m):
        lane = lax.broadcasted_iota(jnp.int32, (STRIDE, PATCH), 1)
        r = 2 * HALF + m * STRIDE
        left = own[r : r + STRIDE, PATCH : 2 * PATCH]
        right = own[r : r + STRIDE, cols : cols + PATCH]
        own_rest[m, 0:STRIDE] = jnp.where(lane < PATCH - HALF, right, left)
        own_rest[m, STRIDE : STRIDE + HALF] = jnp.where(
            lane[:HALF] < STRIDE, turned(left[:HALF], -HALF), turned(left[HALF:], HALF)
        )

    def unpack_rest(m):
        lane = lax.broadcasted_iota(jnp.int32, (HALF, PATCH), 1)
        for h in range(2):
            r = HALF + m * STRIDE + h * HALF
            q, start = r // span, r % span
            border = [nxt_pack[side, start : start + HALF] for side in range(2)]
            main = nxt_rest[m, h * HALF : (h + 1) * HALF]
            half = turned(nxt_rest[m, STRIDE : STRIDE + HALF], HALF if h == 0 else -HALF)
            left = jnp.where(lane < PATCH - HALF, half, main)
            left = jnp.where(lane < HALF, turned(border[0], -HALF * q), left)
            right = jnp.where(lane < PATCH - HALF, main, turned(border[1], PATCH - HALF - HALF * q))
            nxt[HALF + r : 2 * HALF + r, PATCH : 2 * PATCH] = left
            nxt[HALF + r : 2 * HALF + r, cols : cols + PATCH] = right

    tile.wait()
    for side in range(2):
        own_pack[side] = packed(own, spans, side)
    for k, (dy, dx) in enumerate(CORNERS):
        tips[k] = packed(own, eighths(HALF if dy < 0 else rows), (dx + 1) // 2)
    for m in range((rows - 2 * HALF) // STRIDE):
        pack_rest(m)

    tall = 1 + (ty > 0).astype(jnp.int32) + (ty < n_ty - 1).astype(jnp.int32)
    broad = 1 + (tx > 0).astype(jnp.int32) + (tx < n_tx - 1).astype(jnp.int32)
    apart = (crosses(-1) & there(-1, 0)).astype(jnp.int32) + (crosses(1) & there(1, 0)).astype(jnp.int32)
    ends = has_before.astype(jnp.int32) + has_next.astype(jnp.int32)
    pl.semaphore_wait(barrier, n_sec - 1 + tall * broad - 1 + (apart + (tall - 1) * (broad - 1)) * ends)

    bands = (rows - 2 * HALF) // STRIDE
    middle = bands // 2
    pieces = [
        (0, HALF, 0, cols),
        (rows - HALF, HALF, 0, cols),
        None,
        0,
        (HALF, STRIDE, PATCH, 2 * PATCH),
        bands - 1,
        (rows - HALF - STRIDE, STRIDE, PATCH, 2 * PATCH),
        middle,
        (HALF + middle * STRIDE, STRIDE, PATCH, PATCH),
        (HALF + middle * STRIDE, STRIDE, 2 * PATCH, PATCH),
    ]

    def piece_copy(p):
        piece = pieces[p]
        if piece is None:
            src, dst = own_pack, nxt_pack
        elif isinstance(piece, int):
            src, dst = own_rest.at[piece], nxt_rest.at[piece]
        else:
            r, nr, c, nc = piece
            src = x_ref.at[pl.ds(r, nr), pl.ds(c, nc)]
            dst = nxt.at[pl.ds(HALF + r, nr), pl.ds(PATCH + c, nc)]
        return pltpu.make_async_remote_copy(
            src_ref=src,
            dst_ref=dst,
            send_sem=piece_send.at[p],
            recv_sem=piece_recv.at[p],
            device_id=(sec - 1, ty, tx),
            device_id_type=MESH,
        )

    def arrived(*indices):
        @pl.when(has_next)
        def _():
            for p in indices:
                piece_copy(p).wait_recv()

    def edge(dy):
        return (0, HALF + rows) if dy < 0 else (rows - HALF, 0)

    def row_copy(dy, through, target, send, recv, to_sec):
        r, to = edge(dy)
        if through is None:
            src = x_ref.at[pl.ds(r, HALF)]
        else:
            src = through.at[pl.ds(HALF + r, HALF), pl.ds(PATCH, cols)]
        side = (dy + 1) // 2
        return pltpu.make_async_remote_copy(
            src_ref=src,
            dst_ref=target.at[pl.ds(to, HALF), pl.ds(PATCH, cols)],
            send_sem=send.at[side],
            recv_sem=recv.at[side],
            device_id=(to_sec, ty + dy, tx),
            device_id_type=MESH,
        )

    def column_copy(dx, pack, land, send, recv):
        side = (dx + 1) // 2
        return pltpu.make_async_remote_copy(
            src_ref=pack.at[side],
            dst_ref=land.at[side],
            send_sem=send.at[2 + side],
            recv_sem=recv.at[2 + side],
            device_id=(sec, ty, tx + dx),
            device_id_type=MESH,
        )

    def own_rows(dy):
        return row_copy(dy, None, own, own_send, own_recv, sec)

    def own_columns(dx):
        return column_copy(dx, own_pack, own_land, own_send, own_recv)

    def nxt_rows(dy):
        return row_copy(dy, nxt, nxt, nxt_send, nxt_recv, sec)

    def nxt_straight(dy):
        return row_copy(dy, None, nxt, straight_send, nxt_recv, sec - 1)

    def nxt_columns(dx):
        return column_copy(dx, nxt_pack, nxt_land, nxt_send, nxt_recv)

    def tip_copy(k, section):
        dy, dx = CORNERS[k]
        return pltpu.make_async_remote_copy(
            src_ref=tips.at[k],
            dst_ref=(own_tips, nxt_tips)[section].at[k],
            send_sem=tip_send.at[section, k],
            recv_sem=(own_tip_recv, nxt_tip_recv)[section].at[k],
            device_id=(sec - section, ty + dy, tx + dx),
            device_id_type=MESH,
        )

    def diagonals(sign, do):
        for k, (dy, dx) in enumerate(CORNERS):
            @pl.when(there(sign * dy, sign * dx))
            def _(k=k):
                do(k)

    def up_down(ok, do):
        for dy in (-1, 1):
            @pl.when(ok(dy))
            def _(dy=dy):
                do(dy)

    def sides(sign, do):
        for dx in (-1, 1):
            @pl.when(there(0, sign * dx))
            def _(dx=dx):
                do(dx)

    def handed_on(dy):
        return jnp.logical_not(crosses(dy)) & there(dy, 0)

    up_down(lambda dy: there(dy, 0), lambda dy: own_rows(dy).start())
    sides(1, lambda dx: own_columns(dx).start())
    diagonals(1, lambda k: tip_copy(k, 0).start())

    @pl.when(has_before)
    def _():
        diagonals(1, lambda k: tip_copy(k, 1).start())
        up_down(straight, lambda dy: nxt_straight(dy).start())

        @pl.when(crosses(-1))
        def _():
            piece_copy(1).start()

        @pl.when(jnp.logical_not(crosses(-1)))
        def _():
            piece_copy(0).start()

        piece_copy(2).start()

        @pl.when(crosses(-1))
        def _():
            piece_copy(0).start()

        @pl.when(jnp.logical_not(crosses(-1)))
        def _():
            piece_copy(1).start()

        piece_copy(3).start()

    load.wait()

    lane = lax.broadcasted_iota(jnp.int32, (STRIDE, PATCH), 1)
    even, odd = lane < PATCH - HALF, lane >= HALF

    order = [node_cols - 1, *range(node_cols - 1)]
    part_cols = node_cols // 2
    parts = (range(0, part_cols), range(part_cols, node_cols))
    every = range(node_cols)

    def right_chunk(source, high, low, b, places):
        at = pl.ds(b * STRIDE if isinstance(b, int) else pl.multiple_of(b * STRIDE, STRIDE), STRIDE)
        patches = []
        for j in (order[p] for p in places):
            t = j // 2
            main = source[at, (t + 1) * PATCH : (t + 2) * PATCH]
            if j % 2 == 0:
                patch = jnp.where(even, main, source[at, t * PATCH : (t + 1) * PATCH])
            else:
                patch = jnp.where(odd, main, source[at, (t + 2) * PATCH : (t + 3) * PATCH])
            patches.append(jnp.concatenate(split(patch), axis=1))
        got = jnp.dot(jnp.concatenate(patches, axis=0), table[0], preferred_element_type=F32)
        got = got[:, :PATCH] + got[:, PATCH:]
        for n, p in enumerate(places):
            hi, lo = split(got[n * STRIDE : (n + 1) * STRIDE])
            high[at, p * PATCH : (p + 1) * PATCH] = hi
            low[at, p * PATCH : (p + 1) * PATCH] = lo

    def left_spectrum(high, low, i, columns):
        at = pl.ds(pl.multiple_of(i * STRIDE, STRIDE), PATCH)
        both = jnp.concatenate([high[at, columns], low[at, columns]], axis=0)
        got = jnp.dot(table[1], both, preferred_element_type=F32)
        return got[:PATCH] + got[PATCH:]


    def hand_on(dy):
        piece_copy((dy + 1) // 2).wait_recv()
        nxt_rows(dy).start()

    up_down(lambda dy: there(-dy, 0), lambda dy: own_rows(dy).wait_recv())
    sides(-1, lambda dx: own_columns(dx).wait_recv())
    diagonals(-1, lambda k: tip_copy(k, 0).wait_recv())
    unpack_columns(own_land, own)
    diagonals(-1, lambda k: unpack_tip(own_tips, own, k))

    @pl.when(has_next)
    def _():
        up_down(handed_on, hand_on)

    @pl.loop(0, node_rows + 1)
    def _(b):
        right_chunk(own, own_hi, own_lo, b, every)

    @pl.when(has_next)
    def _():
        piece_copy(2).wait_recv()
        sides(1, lambda dx: nxt_columns(dx).start())

    @pl.when(has_before)
    def _():
        for p in range(4, len(pieces)):
            piece_copy(p).start()

    @pl.loop(0, node_rows)
    def _(i):
        for c in range(0, wide, 2 * PATCH):
            at = pl.ds(c, 2 * PATCH)
            spec[i, :, at] = left_spectrum(own_hi, own_lo, i, at)

    @pl.when(has_next)
    def _():
        for dy in (-1, 1):
            @pl.when(jnp.logical_not(handed_on(dy)))
            def _(dy=dy):
                piece_copy((dy + 1) // 2).wait_recv()

        up_down(lambda dy: there(-dy, 0), lambda dy: nxt_rows(dy).wait_recv())
        diagonals(-1, lambda k: tip_copy(k, 1).wait_recv())
        diagonals(-1, lambda k: unpack_tip(nxt_tips, nxt, k))
        sides(-1, lambda dx: nxt_columns(dx).wait_recv())
        unpack_columns(nxt_land, nxt)

    right_chunk(nxt, nxt_hi, nxt_lo, 0, every)
    right_chunk(nxt, nxt_hi, nxt_lo, node_rows, every)

    lanes = lax.broadcasted_iota(jnp.int32, (8, PATCH), 1)

    def flow_block(indices):
        columns = jnp.zeros((8, PATCH), F32)
        for i in indices:
            total, down, across = (jnp.sum(stats[q, i], axis=1, keepdims=True) for q in range(3))
            inv = 1.0 / total
            columns = jnp.where(lanes == i, down * inv, columns)
            columns = jnp.where(lanes == node_rows + i, across * inv, columns)
        columns = pltpu.roll(jnp.where(has_next, columns, 0.0), node_cols - 1, 0)
        return jnp.transpose(jnp.concatenate([columns] * 16, axis=0))[:8]

    def flow_copy(index):
        dy, dx = DIRECTIONS[index]
        return pltpu.make_async_remote_copy(
            src_ref=flows.at[1 if dy and dx else 0],
            dst_ref=around.at[index],
            send_sem=flow_send.at[index],
            recv_sem=flow_recv.at[index],
            device_id=(sec, ty + dy, tx + dx),
            device_id_type=MESH,
        )

    def flow_each(sign, corners, do):
        for index, (dy, dx) in enumerate(DIRECTIONS):
            if bool(dy and dx) in corners:
                @pl.when(there(sign * dy, sign * dx))
                def _(index=index):
                    do(index)

    last = node_rows - 1

    @pl.loop(0, 4)
    def _(step):
        @pl.when(step == 0)
        def _():
            arrived(3, 4)
            unpack_rest(0)
            right_chunk(nxt, nxt_hi, nxt_lo, 1, every)

        @pl.when(step == 1)
        def _():
            arrived(5, 6)
            unpack_rest(bands - 1)
            right_chunk(nxt, nxt_hi, nxt_lo, last, every)

        @pl.when(step == 2)
        def _():
            flows[1] = flow_block((0, last))
            flow_each(1, (True,), lambda k: flow_copy(k).start())
            arrived(7, 8)
            unpack_rest(middle)
            right_chunk(nxt, nxt_hi, nxt_lo, 2, parts[0])

        @pl.when(step == 3)
        def _():
            arrived(9)
            right_chunk(nxt, nxt_hi, nxt_lo, 2, parts[1])

        halves = [
            (jnp.where(step < 2, step * last, 1 + h), jnp.where(step < 2, h, step - 2)) for h in range(2)
        ]
        nodes = [slice(n * PATCH, (n + 1) * PATCH) for n in range(node_cols)]
        mine, other = [], []
        for i, g in halves:
            columns = pl.ds(pl.multiple_of(g * part_cols * PATCH, PATCH), part_cols * PATCH)
            other.append(left_spectrum(nxt_hi, nxt_lo, i, columns))
            mine.append(spec[i, :, columns])
        mine, other = (jnp.concatenate(value, axis=1) for value in (mine, other))
        prods = jnp.concatenate([product(mine[:, n], other[:, n]) for n in nodes], axis=1)
        mixed = jnp.dot(
            table[2], jnp.concatenate(split(prods), axis=0), preferred_element_type=F32
        )
        hi, lo = split(mixed[:PATCH] + mixed[PATCH:])
        stacked = jnp.concatenate(
            [jnp.concatenate([hi[:, n], lo[:, n]], axis=1) for n in nodes], axis=0
        )
        corr = jnp.dot(stacked, table[3], preferred_element_type=F32)
        corr = corr[:, :PATCH] + corr[:, PATCH:]
        found = [moments(corr[n]) for n in nodes]
        for h, (i, g) in enumerate(halves):
            for q in range(3):
                stats[q, i, pl.ds(g * part_cols, part_cols), :] = jnp.concatenate(
                    [f[q] for f in found[h * part_cols : (h + 1) * part_cols]], axis=0
                )

    block = flow_block(range(node_rows))
    flows[0] = block
    flow_each(1, (False,), lambda k: flow_copy(k).start())

    up_down(lambda dy: there(dy, 0), lambda dy: own_rows(dy).wait_send())
    sides(1, lambda dx: own_columns(dx).wait_send())
    diagonals(1, lambda k: tip_copy(k, 0).wait_send())

    @pl.when(has_before)
    def _():
        for p in range(len(pieces)):
            piece_copy(p).wait_send()
        up_down(straight, lambda dy: nxt_straight(dy).wait_send())
        diagonals(1, lambda k: tip_copy(k, 1).wait_send())

    @pl.when(has_next)
    def _():
        up_down(handed_on, lambda dy: nxt_rows(dy).wait_send())
        sides(1, lambda dx: nxt_columns(dx).wait_send())

    flow_each(-1, (True, False), lambda k: flow_copy(k).wait_recv())

    lines = {}
    for dy in (-1, 0, 1):
        def from_(dx, dy=dy):
            return block if (dy, dx) == (0, 0) else around[DIRECTIONS.index((-dy, -dx))]

        line = jnp.where(lanes < 2 + node_cols, pltpu.roll(from_(0), 2, 1), pltpu.roll(from_(1), 2 + node_cols, 1))
        lines[dy] = jnp.where(lanes < 2, pltpu.roll(from_(-1), PATCH + 2 - node_cols, 1), line)

    subs = lax.broadcasted_iota(jnp.int32, (8, PATCH), 0)
    row_id = ty * node_rows + subs - 2
    col_id = tx * node_cols + lanes - 2
    inside = (
        (row_id >= 0) & (row_id < node_rows * n_ty) & (col_id >= 0) & (col_id < node_cols * n_tx)
    )
    done = []
    for c in range(2):
        base = c * node_rows
        above = pltpu.roll(lines[-1], (8 - (base + node_rows - 2)) % 8, 0)
        here = pltpu.roll(lines[0], (8 + 2 - base) % 8, 0)
        below = pltpu.roll(lines[1], (8 + 2 + node_rows - base) % 8, 0)
        flow = jnp.where(subs < 2, above, jnp.where(subs < 2 + node_rows, here, below))
        done.append(pltpu.roll(relax(flow, inside), PATCH - 2, 1))
    result = jnp.where(
        subs < node_rows, pltpu.roll(done[0], 6, 0), pltpu.roll(done[1], (8 + node_rows - 2) % 8, 0)
    )
    flows[2] = result

    def mesh_copy(d):
        return pltpu.make_async_remote_copy(
            src_ref=flows.at[2],
            dst_ref=meshes.at[sec],
            send_sem=mesh_send.at[d],
            recv_sem=mesh_recv.at[d],
            device_id=(sec + d, ty, tx),
            device_id_type=MESH,
        )

    def mesh_wait(d):
        pltpu.make_async_remote_copy(
            src_ref=flows.at[2],
            dst_ref=meshes.at[sec - d],
            send_sem=mesh_send.at[d],
            recv_sem=mesh_recv.at[d],
            device_id=(sec - d, ty, tx),
            device_id_type=MESH,
        ).wait_recv()

    for d in range(1, n_sec):
        @pl.when(sec + d < n_sec)
        def _(d=d):
            mesh_copy(d).start()
    for d in range(1, n_sec):
        @pl.when(sec - d >= 0)
        def _(d=d):
            mesh_wait(d)

    earlier = meshes[0]
    for t in range(1, n_sec):
        earlier = earlier + meshes[t]
    out_ref[0] = result
    out_ref[1] = earlier

    flow_each(1, (True, False), lambda k: flow_copy(k).wait_send())
    for d in range(1, n_sec):
        @pl.when(sec + d < n_sec)
        def _(d=d):
            mesh_copy(d).wait_send()


def solution(mesh):
    sizes = tuple(mesh.shape[axis] for axis in ("sec", "ty", "tx"))

    def on_device(images):
        image = images[0]
        rows, cols = image.shape
        node_rows, node_cols = rows // STRIDE, cols // STRIDE
        high = 2 * HALF + rows
        wide = node_cols * PATCH
        around = len(DIRECTIONS)
        n_pieces = 10
        bands = (rows - 2 * HALF) // STRIDE
        dma = pltpu.SemaphoreType.DMA
        out = pl.pallas_call(
            functools.partial(kernel, sizes),
            out_shape=jax.ShapeDtypeStruct((2, 8, PATCH), F32),
            in_specs=[pl.BlockSpec(memory_space=pl.ANY)] * 2,
            out_specs=pl.BlockSpec(memory_space=pltpu.VMEM),
            scratch_shapes=[
                pltpu.VMEM((high, cols + 2 * PATCH), F32),
                pltpu.VMEM((high, cols + 2 * PATCH), F32),
                pltpu.VMEM((high, wide), BF16),
                pltpu.VMEM((high, wide), BF16),
                pltpu.VMEM((high, wide), BF16),
                pltpu.VMEM((high, wide), BF16),
                pltpu.VMEM((node_rows, PATCH, wide), F32),
                pltpu.VMEM((4, 2 * PATCH, 2 * PATCH), BF16),
                pltpu.VMEM((3, node_rows, node_cols, PATCH), F32),
                pltpu.VMEM((3, 8, PATCH), F32),
                pltpu.VMEM((around, 8, PATCH), F32),
                pltpu.VMEM((sizes[0], 8, PATCH), F32),
                pltpu.VMEM((2, rows // 4, PATCH), F32),
                pltpu.VMEM((2, rows // 4, PATCH), F32),
                pltpu.VMEM((2, rows // 4, PATCH), F32),
                pltpu.VMEM((2, rows // 4, PATCH), F32),
                pltpu.VMEM((bands, STRIDE + HALF, PATCH), F32),
                pltpu.VMEM((bands, STRIDE + HALF, PATCH), F32),
                pltpu.VMEM((len(CORNERS), 8, PATCH), F32),
                pltpu.VMEM((len(CORNERS), 8, PATCH), F32),
                pltpu.VMEM((len(CORNERS), 8, PATCH), F32),
                dma((2,)),
                dma((n_pieces,)),
                dma((n_pieces,)),
                dma((4,)),
                dma((4,)),
                dma((4,)),
                dma((4,)),
                dma((2,)),
                dma((2, len(CORNERS))),
                dma((len(CORNERS),)),
                dma((len(CORNERS),)),
                dma((around,)),
                dma((around,)),
                dma((sizes[0],)),
                dma((sizes[0],)),
            ],
            compiler_params=pltpu.CompilerParams(
                collective_id=0, has_side_effects=True, vmem_limit_bytes=60 * 1024 * 1024
            ),
        )(image, jnp.asarray(tables()))
        out = out[:, :, :node_cols].reshape(2, 1, 2, node_rows, node_cols)
        return out[0], out[1]

    return jax.shard_map(
        on_device,
        mesh=mesh,
        in_specs=(P("sec", "ty", "tx"),),
        out_specs=(P("sec", None, "ty", "tx"), P("sec", None, "ty", "tx")),
        check_vma=False,
    )
```

```python
import functools

import jax
import jax.numpy as jnp
import ml_dtypes
import numpy as np
from jax import lax
from jax.experimental import pallas as pl
from jax.experimental.pallas import tpu as pltpu
from jax.sharding import PartitionSpec as P

PATCH = 128
STRIDE = 64
HALF = 32
RATE = 0.25

MESH = pl.DeviceIdType.MESH
CORNERS = [(dy, dx) for dy in (-1, 1) for dx in (-1, 1)]
DIRECTIONS = [(dy, dx) for dy in (-1, 0, 1) for dx in (-1, 0, 1) if (dy, dx) != (0, 0)]
F32 = jnp.float32
BF16 = jnp.bfloat16


def split_table(table):
    high = table.astype(ml_dtypes.bfloat16)
    low = (table - high.astype(np.float64)).astype(ml_dtypes.bfloat16)
    return high, low


def tables():
    half = PATCH // 2
    point = np.arange(PATCH)
    angle = 2.0 * np.pi / PATCH
    packed = np.zeros((PATCH, PATCH))
    for k in range(half):
        packed[k] = np.cos(angle * (k * point % PATCH))
        packed[half + k] = np.sin(angle * (k * point % PATCH))
    packed[half] = np.cos(np.pi * point)
    weight = np.full(PATCH, 2.0)
    weight[0] = weight[half] = 1.0
    inverse = packed.T * weight[None, :] / PATCH

    def left(table):
        high, low = split_table(table)
        return np.block([[high, high], [low, low]])

    def right(table):
        high, low = split_table(table)
        return np.block([[high, low], [high, low]])

    scale = np.log2(np.e) / PATCH
    return np.stack(
        [right(packed.T), left(packed), left(inverse), right(inverse.T * scale)]
    ).astype(ml_dtypes.bfloat16)


def split(value):
    high = value.astype(BF16)
    low = (value - high.astype(F32)).astype(BF16)
    return high, low


def product(own, other):
    half = PATCH // 2
    lane = lax.broadcasted_iota(jnp.int32, (half, PATCH), 1)
    row = lax.broadcasted_iota(jnp.int32, (half, PATCH), 0)
    left = lane < half
    alone = (lane == 0) | (lane == half)
    plain = left | alone
    top_row = row == 0
    t, u = own[:half], own[half:]
    t2, u2 = other[:half], other[half:]
    rt2 = pltpu.roll(t2, half, 1)
    ru2 = pltpu.roll(u2, half, 1)
    uu, uru = u * u2, u * ru2
    g = t * t2 + jnp.where(top_row, 0.0, uu)
    h = t * rt2 + jnp.where(top_row, 0.0, uru)
    g2 = jnp.where(top_row, uu, t * u2 - u * t2)
    h2 = jnp.where(top_row, uru, t * ru2 - u * rt2)

    def joined(g, h):
        cross = pltpu.roll(jnp.where(left, h, g), half, 1)
        cross = jnp.where(alone, 0.0, cross)
        return jnp.where(plain, cross + g, cross - h)

    top = joined(g, h)
    top = jnp.where(top_row & (lane == 0), 0.0, top)
    return jnp.concatenate([top, joined(g2, h2)], axis=0)


def moments(scores):
    peak = jnp.max(jnp.max(scores, axis=0, keepdims=True), axis=1, keepdims=True)
    terms = jnp.exp2(scores - peak)
    total = None
    for g in range(PATCH // 8):
        part = terms[8 * g : 8 * g + 8]
        steps = float(g if g < PATCH // 16 else g - PATCH // 8)
        total = part if total is None else total + part
        first = part * steps if g == 0 else first + part * steps
    sub = lax.broadcasted_iota(jnp.int32, (8, PATCH), 0).astype(F32)
    lane = lax.broadcasted_iota(jnp.int32, (8, PATCH), 1)
    lag = jnp.where(lane < PATCH // 2, lane, lane - PATCH).astype(F32)
    return [
        jnp.sum(value, axis=0, keepdims=True)
        for value in (total, first * 8.0 + total * sub, total * lag)
    ]


def relax(flow, inside):
    def lap(value):
        return (
            pltpu.roll(value, 1, 0)
            + pltpu.roll(value, 7, 0)
            + pltpu.roll(value, 1, 1)
            + pltpu.roll(value, PATCH - 1, 1)
            - 4.0 * value
        )

    first = flow + RATE * (lap(flow) + flow - flow)
    first = jnp.where(inside, first, 0.0)
    return first + RATE * (lap(first) + flow - first)


def kernel(
    sizes, x_ref, tables_ref, out_ref, own, nxt, own_hi, own_lo, nxt_hi, nxt_lo, spec, table,
    stats, flows, around, meshes,
    own_pack, own_land, nxt_pack, nxt_land, own_rest, nxt_rest, edges, tips, own_tips, nxt_tips,
    local_sem, piece_send, piece_recv, own_send, own_recv, nxt_send, nxt_recv, straight_send,
    tip_send, own_tip_recv, nxt_tip_recv,
    flow_send, flow_recv, mesh_send, mesh_recv,
):
    n_sec, n_ty, n_tx = sizes
    rows, cols = x_ref.shape
    node_rows, node_cols = rows // STRIDE, cols // STRIDE
    wide = node_cols * PATCH
    sec, ty, tx = lax.axis_index("sec"), lax.axis_index("ty"), lax.axis_index("tx")

    def there(dy, dx):
        ok = jnp.bool_(True)
        if dy:
            ok = (ty + dy >= 0) & (ty + dy < n_ty)
        if dx:
            in_x = (tx + dx >= 0) & (tx + dx < n_tx)
            ok = ok & in_x if dy else in_x
        return ok

    has_next = sec < n_sec - 1
    has_before = sec > 0

    def crosses(dy):
        return (ty % 2 == 1) if dy > 0 else (ty % 2 == 0)

    bands = (rows - 2 * HALF) // STRIDE
    odd_core = ty % 2 == 1

    def mirrored(k, count=bands):
        return jnp.where(odd_core, count - 1 - k, k)

    def straight(dy):
        return crosses(dy) & there(dy, 0)

    barrier = pltpu.get_barrier_semaphore()

    def greet(ok, s, y, x):
        @pl.when(ok)
        def _():
            pl.semaphore_signal(barrier, inc=1, device_id=(s, y, x), device_id_type=MESH)

    for dy, dx in DIRECTIONS:
        greet(there(dy, dx), sec, ty + dy, tx + dx)
    for dy in (-1, 1):
        greet(has_before & straight(dy), sec - 1, ty + dy, tx)
        greet(has_next & straight(dy), sec + 1, ty + dy, tx)
    for dy, dx in CORNERS:
        greet(has_before & there(dy, dx), sec - 1, ty + dy, tx + dx)
        greet(has_next & there(dy, dx), sec + 1, ty + dy, tx + dx)
    for d in range(1, n_sec):
        pl.semaphore_signal(
            barrier, inc=1, device_id=(lax.rem(sec + d, n_sec), ty, tx), device_id_type=MESH
        )

    tile = pltpu.make_async_copy(
        x_ref, own.at[pl.ds(HALF, rows), pl.ds(PATCH, cols)], local_sem.at[0]
    )
    tile.start()
    load = pltpu.make_async_copy(tables_ref, table, local_sem.at[1])
    load.start()

    for ref in (own, nxt):
        @pl.when(ty == 0)
        def _(ref=ref):
            ref[0:HALF, :] = jnp.zeros((HALF, cols + 2 * PATCH), F32)

        @pl.when(ty == n_ty - 1)
        def _(ref=ref):
            ref[HALF + rows : 2 * HALF + rows, :] = jnp.zeros((HALF, cols + 2 * PATCH), F32)

        @pl.when(tx == 0)
        def _(ref=ref):
            ref[:, 0:PATCH] = jnp.zeros((2 * HALF + rows, PATCH), F32)

        @pl.when(tx == n_tx - 1)
        def _(ref=ref):
            ref[:, PATCH + cols :] = jnp.zeros((2 * HALF + rows, PATCH), F32)

    for index, (dy, dx) in enumerate(DIRECTIONS):
        @pl.when(jnp.logical_not(there(-dy, -dx)))
        def _(index=index):
            around[index] = jnp.zeros((8, PATCH), F32)

    for t in range(n_sec):
        @pl.when(t >= sec)
        def _(t=t):
            meshes[t] = jnp.zeros((8, PATCH), F32)

    span = rows // 4
    spans = [(HALF + span * q, span) for q in range(4)]

    def turned(value, by):
        return pltpu.roll(value, by % PATCH, 1) if by % PATCH else value

    def packed(source, where, side):
        lane = lax.broadcasted_iota(jnp.int32, (where[0][1], PATCH), 1)
        at, first = ((PATCH, 0), (cols, PATCH - HALF))[side]
        value = None
        for q, (r, nr) in enumerate(where):
            part = turned(source[r : r + nr, at : at + PATCH], HALF * q - first)
            value = part if q == 0 else jnp.where(lane >= HALF * q, part, value)
        return value

    def unpack(value, target, where, side):
        at, first = ((PATCH + cols, 0), (0, PATCH - HALF))[side]
        for q, (r, nr) in enumerate(where):
            target[r : r + nr, at : at + PATCH] = turned(value, first - HALF * q)

    def unpack_columns(land, target):
        for side in range(2):
            @pl.when(there(0, 1 - 2 * side))
            def _(side=side):
                unpack(land[side], target, spans, side)

    def eighths(start):
        return [(start + 8 * q, 8) for q in range(4)]

    def unpack_tip(land, target, k):
        dy, dx = CORNERS[k]
        unpack(land[k], target, eighths(HALF + rows if dy < 0 else 0), (dx + 1) // 2)

    def pack_rest(m):
        lane = lax.broadcasted_iota(jnp.int32, (STRIDE, PATCH), 1)
        r = 2 * HALF + m * STRIDE
        left = own[r : r + STRIDE, PATCH : 2 * PATCH]
        right = own[r : r + STRIDE, cols : cols + PATCH]
        own_rest[m, 0:STRIDE] = jnp.where(lane < PATCH - HALF, right, left)
        own_rest[m, STRIDE : STRIDE + HALF] = jnp.where(
            lane[:HALF] < STRIDE, turned(left[:HALF], -HALF), turned(left[HALF:], HALF)
        )
        left = own[r : r + STRIDE, 2 * PATCH : 3 * PATCH]
        right = own[r : r + STRIDE, 3 * PATCH : 4 * PATCH]
        lane = lane[:HALF]
        low = jnp.where(lane < HALF, left[:HALF], turned(left[HALF:], HALF))
        high = jnp.where(lane < PATCH - HALF, turned(right[:HALF], -HALF), right[HALF:])
        own_rest[m, STRIDE + HALF : STRIDE + 2 * HALF] = jnp.where(lane < STRIDE, low, high)

    def unpack_rest(m):
        lane = lax.broadcasted_iota(jnp.int32, (HALF, PATCH), 1)
        for h in range(2):
            r = HALF + m * STRIDE + h * HALF
            q, start = r // span, r % span
            border = [nxt_pack[side, start : start + HALF] for side in range(2)]
            main = nxt_rest[m, h * HALF : (h + 1) * HALF]
            half = turned(nxt_rest[m, STRIDE : STRIDE + HALF], HALF if h == 0 else -HALF)
            left = jnp.where(lane < PATCH - HALF, half, main)
            left = jnp.where(lane < HALF, turned(border[0], -HALF * q), left)
            right = jnp.where(lane < PATCH - HALF, main, turned(border[1], PATCH - HALF - HALF * q))
            nxt[HALF + r : 2 * HALF + r, PATCH : 2 * PATCH] = left
            nxt[HALF + r : 2 * HALF + r, cols : cols + PATCH] = right

    def unpack_edges(m):
        strip = nxt_rest[m, STRIDE + HALF : STRIDE + 2 * HALF]
        edges[0] = jnp.concatenate([strip, turned(strip, -HALF)], axis=0)
        edges[1] = jnp.concatenate([turned(strip, HALF), strip], axis=0)

    def at_band(k, do):
        for m in range(bands):
            @pl.when(mirrored(k) == m)
            def _(m=m):
                do(m)

    tile.wait()
    stats[...] = jnp.ones_like(stats)
    for side in range(2):
        own_pack[side] = packed(own, spans, side)
    for k, (dy, dx) in enumerate(CORNERS):
        tips[k] = packed(own, eighths(HALF if dy < 0 else rows), (dx + 1) // 2)
    for m in range(bands):
        pack_rest(m)

    tall = 1 + (ty > 0).astype(jnp.int32) + (ty < n_ty - 1).astype(jnp.int32)
    broad = 1 + (tx > 0).astype(jnp.int32) + (tx < n_tx - 1).astype(jnp.int32)
    apart = (crosses(-1) & there(-1, 0)).astype(jnp.int32) + (crosses(1) & there(1, 0)).astype(jnp.int32)
    ends = has_before.astype(jnp.int32) + has_next.astype(jnp.int32)
    pl.semaphore_wait(barrier, n_sec - 1 + tall * broad - 1 + (apart + (tall - 1) * (broad - 1)) * ends)

    banded = [mirrored(m) for m in range(bands)]

    def band_rest(m, last):
        return (banded[m], STRIDE + 2 * HALF if last else STRIDE + HALF)

    def band_inner(m):
        return (pl.multiple_of(HALF + banded[m] * STRIDE, HALF), STRIDE, PATCH, 2 * PATCH)

    pieces = [(0, HALF, 0, cols), (rows - HALF, HALF, 0, cols), None]
    for m in range(bands):
        pieces += [band_rest(m, m == bands - 1), band_inner(m)]

    def piece_copy(p):
        piece = pieces[p]
        if piece is None:
            src, dst = own_pack, nxt_pack
        elif len(piece) == 2:
            m, nr = piece
            src, dst = own_rest.at[m, pl.ds(0, nr)], nxt_rest.at[m, pl.ds(0, nr)]
        else:
            r, nr, c, nc = piece
            src = x_ref.at[pl.ds(r, nr), pl.ds(c, nc)]
            to = HALF + r if isinstance(r, int) else pl.multiple_of(HALF + r, HALF)
            dst = nxt.at[pl.ds(to, nr), pl.ds(PATCH + c, nc)]
        return pltpu.make_async_remote_copy(
            src_ref=src,
            dst_ref=dst,
            send_sem=piece_send.at[p],
            recv_sem=piece_recv.at[p],
            device_id=(sec - 1, ty, tx),
            device_id_type=MESH,
        )

    def arrived(*indices):
        @pl.when(has_next)
        def _():
            for p in indices:
                piece_copy(p).wait_recv()

    def edge(dy):
        return (0, HALF + rows) if dy < 0 else (rows - HALF, 0)

    def row_copy(dy, through, target, send, recv, to_sec):
        r, to = edge(dy)
        if through is None:
            src = x_ref.at[pl.ds(r, HALF)]
        else:
            src = through.at[pl.ds(HALF + r, HALF), pl.ds(PATCH, cols)]
        side = (dy + 1) // 2
        return pltpu.make_async_remote_copy(
            src_ref=src,
            dst_ref=target.at[pl.ds(to, HALF), pl.ds(PATCH, cols)],
            send_sem=send.at[side],
            recv_sem=recv.at[side],
            device_id=(to_sec, ty + dy, tx),
            device_id_type=MESH,
        )

    def column_copy(dx, pack, land, send, recv):
        side = (dx + 1) // 2
        return pltpu.make_async_remote_copy(
            src_ref=pack.at[side],
            dst_ref=land.at[side],
            send_sem=send.at[2 + side],
            recv_sem=recv.at[2 + side],
            device_id=(sec, ty, tx + dx),
            device_id_type=MESH,
        )

    def own_rows(dy):
        return row_copy(dy, None, own, own_send, own_recv, sec)

    def own_columns(dx):
        return column_copy(dx, own_pack, own_land, own_send, own_recv)

    def nxt_rows(dy):
        return row_copy(dy, nxt, nxt, nxt_send, nxt_recv, sec)

    def nxt_straight(dy):
        return row_copy(dy, None, nxt, straight_send, nxt_recv, sec - 1)

    def nxt_columns(dx):
        return column_copy(dx, nxt_pack, nxt_land, nxt_send, nxt_recv)

    def tip_copy(k, section):
        dy, dx = CORNERS[k]
        return pltpu.make_async_remote_copy(
            src_ref=tips.at[k],
            dst_ref=(own_tips, nxt_tips)[section].at[k],
            send_sem=tip_send.at[section, k],
            recv_sem=(own_tip_recv, nxt_tip_recv)[section].at[k],
            device_id=(sec - section, ty + dy, tx + dx),
            device_id_type=MESH,
        )

    def diagonals(sign, do):
        for k, (dy, dx) in enumerate(CORNERS):
            @pl.when(there(sign * dy, sign * dx))
            def _(k=k):
                do(k)

    def up_down(ok, do):
        for dy in (-1, 1):
            @pl.when(ok(dy))
            def _(dy=dy):
                do(dy)

    def sides(sign, do):
        for dx in (-1, 1):
            @pl.when(there(0, sign * dx))
            def _(dx=dx):
                do(dx)

    def handed_on(dy):
        return jnp.logical_not(crosses(dy)) & there(dy, 0)

    up_down(lambda dy: there(dy, 0), lambda dy: own_rows(dy).start())
    sides(1, lambda dx: own_columns(dx).start())
    diagonals(1, lambda k: tip_copy(k, 0).start())

    @pl.when(has_before)
    def _():
        diagonals(1, lambda k: tip_copy(k, 1).start())
        up_down(straight, lambda dy: nxt_straight(dy).start())

        @pl.when(crosses(-1))
        def _():
            piece_copy(1).start()

        @pl.when(jnp.logical_not(crosses(-1)))
        def _():
            piece_copy(0).start()

        piece_copy(2).start()

        @pl.when(crosses(-1))
        def _():
            piece_copy(0).start()

        @pl.when(jnp.logical_not(crosses(-1)))
        def _():
            piece_copy(1).start()

        piece_copy(3).start()

    load.wait()

    lane = lax.broadcasted_iota(jnp.int32, (STRIDE, PATCH), 1)
    even, odd = lane < PATCH - HALF, lane >= HALF

    order = [node_cols - 2, node_cols - 1, *range(node_cols - 2)]
    part_cols = node_cols // 2
    parts = (range(0, part_cols), range(part_cols, node_cols))
    every = range(node_cols)

    def right_chunk(source, high, low, b, places, ahead=False):
        at = pl.ds(b * STRIDE if isinstance(b, int) else pl.multiple_of(b * STRIDE, STRIDE), STRIDE)
        patches = []
        for j in (order[p] for p in places):
            t = j // 2
            main = source[at, (t + 1) * PATCH : (t + 2) * PATCH]
            beside = t if j % 2 == 0 else t + 2
            if ahead and j in (1, node_cols - 2):
                part = edges[0 if j == 1 else 1]
            else:
                part = source[at, beside * PATCH : (beside + 1) * PATCH]
            patch = jnp.where(even if j % 2 == 0 else odd, main, part)
            patches.append(jnp.concatenate(split(patch), axis=1))
        got = jnp.dot(jnp.concatenate(patches, axis=0), table[0], preferred_element_type=F32)
        got = got[:, :PATCH] + got[:, PATCH:]
        for n, p in enumerate(places):
            hi, lo = split(got[n * STRIDE : (n + 1) * STRIDE])
            high[at, p * PATCH : (p + 1) * PATCH] = hi
            low[at, p * PATCH : (p + 1) * PATCH] = lo

    def left_spectrum(high, low, i, columns):
        at = pl.ds(pl.multiple_of(i * STRIDE, STRIDE), PATCH)
        both = jnp.concatenate([high[at, columns], low[at, columns]], axis=0)
        got = jnp.dot(table[1], both, preferred_element_type=F32)
        return got[:PATCH] + got[PATCH:]


    def hand_on(dy):
        piece_copy((dy + 1) // 2).wait_recv()
        nxt_rows(dy).start()

    up_down(lambda dy: there(-dy, 0), lambda dy: own_rows(dy).wait_recv())
    sides(-1, lambda dx: own_columns(dx).wait_recv())
    diagonals(-1, lambda k: tip_copy(k, 0).wait_recv())
    unpack_columns(own_land, own)
    diagonals(-1, lambda k: unpack_tip(own_tips, own, k))

    @pl.when(has_next)
    def _():
        up_down(handed_on, hand_on)

    @pl.loop(0, node_rows + 1)
    def _(b):
        right_chunk(own, own_hi, own_lo, b, every)

    @pl.when(has_next)
    def _():
        piece_copy(2).wait_recv()
        sides(1, lambda dx: nxt_columns(dx).start())

    @pl.when(has_before)
    def _():
        for p in range(4, len(pieces)):
            piece_copy(p).start()

    @pl.loop(0, node_rows)
    def _(i):
        for c in range(0, wide, 2 * PATCH):
            at = pl.ds(c, 2 * PATCH)
            spec[i, :, at] = left_spectrum(own_hi, own_lo, i, at)

    @pl.when(has_next)
    def _():
        for dy in (-1, 1):
            @pl.when(jnp.logical_not(handed_on(dy)))
            def _(dy=dy):
                piece_copy((dy + 1) // 2).wait_recv()

        up_down(lambda dy: there(-dy, 0), lambda dy: nxt_rows(dy).wait_recv())
        diagonals(-1, lambda k: tip_copy(k, 1).wait_recv())
        diagonals(-1, lambda k: unpack_tip(nxt_tips, nxt, k))
        sides(-1, lambda dx: nxt_columns(dx).wait_recv())
        unpack_columns(nxt_land, nxt)

    right_chunk(nxt, nxt_hi, nxt_lo, 0, every)
    right_chunk(nxt, nxt_hi, nxt_lo, node_rows, every)

    lanes = lax.broadcasted_iota(jnp.int32, (8, PATCH), 1)

    def flow_block(indices):
        columns = jnp.zeros((8, PATCH), F32)
        for i in indices:
            total, down, across = (jnp.sum(stats[q, i], axis=1, keepdims=True) for q in range(3))
            inv = 1.0 / total
            columns = jnp.where(lanes == i, down * inv, columns)
            columns = jnp.where(lanes == node_rows + i, across * inv, columns)
        columns = pltpu.roll(jnp.where(has_next, columns, 0.0), node_cols - 2, 0)
        return jnp.transpose(jnp.concatenate([columns] * 16, axis=0))[:8]

    def flow_stage(dy, dx):
        if dy == 0:
            return 2
        return jnp.where(crosses(dy), 1, 0 if dx == 0 else 2)

    def flow_copy(index):
        dy, dx = DIRECTIONS[index]
        return pltpu.make_async_remote_copy(
            src_ref=flows.at[flow_stage(dy, dx)],
            dst_ref=around.at[index],
            send_sem=flow_send.at[index],
            recv_sem=flow_recv.at[index],
            device_id=(sec, ty + dy, tx + dx),
            device_id_type=MESH,
        )

    def flow_each(sign, do, stage=None):
        for index, (dy, dx) in enumerate(DIRECTIONS):
            ok = there(sign * dy, sign * dx)
            if stage is not None:
                ok = ok & (flow_stage(dy, dx) == stage)

            @pl.when(ok)
            def _(index=index):
                do(index)

    def flow_send_stage(stage):
        flows[stage] = flow_block(range(node_rows))
        flow_each(1, lambda k: flow_copy(k).start(), stage)

    @pl.loop(0, 4)
    def _(step):
        @pl.when(step == 0)
        def _():
            arrived(3, 4)
            at_band(0, unpack_rest)

        @pl.when(step == 1)
        def _():
            arrived(5, 6)
            at_band(1, unpack_rest)

        @pl.when(step < 2)
        def _():
            right_chunk(nxt, nxt_hi, nxt_lo, 1 + mirrored(step), every)

        @pl.when(step == 2)
        def _():
            flow_send_stage(1)
            arrived(7)
            at_band(2, unpack_rest)
            at_band(2, unpack_edges)
            right_chunk(nxt, nxt_hi, nxt_lo, 1 + mirrored(2), parts[0], True)

        @pl.when(step == 3)
        def _():
            flow_send_stage(2)
            arrived(8)
            right_chunk(nxt, nxt_hi, nxt_lo, 1 + mirrored(2), parts[1])

        halves = [
            (mirrored(jnp.where(step < 2, step, 2 + h), node_rows), jnp.where(step < 2, h, step - 2))
            for h in range(2)
        ]
        nodes = [slice(n * PATCH, (n + 1) * PATCH) for n in range(node_cols)]
        mine, other = [], []
        for i, g in halves:
            columns = pl.ds(pl.multiple_of(g * part_cols * PATCH, PATCH), part_cols * PATCH)
            other.append(left_spectrum(nxt_hi, nxt_lo, i, columns))
            mine.append(spec[i, :, columns])
        mine, other = (jnp.concatenate(value, axis=1) for value in (mine, other))
        prods = jnp.concatenate([product(mine[:, n], other[:, n]) for n in nodes], axis=1)
        mixed = jnp.dot(
            table[2], jnp.concatenate(split(prods), axis=0), preferred_element_type=F32
        )
        hi, lo = split(mixed[:PATCH] + mixed[PATCH:])
        stacked = jnp.concatenate(
            [jnp.concatenate([hi[:, n], lo[:, n]], axis=1) for n in nodes], axis=0
        )
        corr = jnp.dot(stacked, table[3], preferred_element_type=F32)
        corr = corr[:, :PATCH] + corr[:, PATCH:]
        found = [moments(corr[n]) for n in nodes]
        for h, (i, g) in enumerate(halves):
            for q in range(3):
                stats[q, i, pl.ds(g * part_cols, part_cols), :] = jnp.concatenate(
                    [f[q] for f in found[h * part_cols : (h + 1) * part_cols]], axis=0
                )

    block = flow_block(range(node_rows))
    flows[0] = block
    flow_each(1, lambda k: flow_copy(k).start(), 0)

    up_down(lambda dy: there(dy, 0), lambda dy: own_rows(dy).wait_send())
    sides(1, lambda dx: own_columns(dx).wait_send())
    diagonals(1, lambda k: tip_copy(k, 0).wait_send())

    @pl.when(has_before)
    def _():
        for p in range(len(pieces)):
            piece_copy(p).wait_send()
        up_down(straight, lambda dy: nxt_straight(dy).wait_send())
        diagonals(1, lambda k: tip_copy(k, 1).wait_send())

    @pl.when(has_next)
    def _():
        up_down(handed_on, lambda dy: nxt_rows(dy).wait_send())
        sides(1, lambda dx: nxt_columns(dx).wait_send())

    flow_each(-1, lambda k: flow_copy(k).wait_recv())

    lines = {}
    for dy in (-1, 0, 1):
        def from_(dx, dy=dy):
            return block if (dy, dx) == (0, 0) else around[DIRECTIONS.index((-dy, -dx))]

        line = jnp.where(lanes < 2 + node_cols, pltpu.roll(from_(0), 2, 1), pltpu.roll(from_(1), 2 + node_cols, 1))
        lines[dy] = jnp.where(lanes < 2, pltpu.roll(from_(-1), PATCH + 2 - node_cols, 1), line)

    subs = lax.broadcasted_iota(jnp.int32, (8, PATCH), 0)
    row_id = ty * node_rows + subs - 2
    col_id = tx * node_cols + lanes - 2
    inside = (
        (row_id >= 0) & (row_id < node_rows * n_ty) & (col_id >= 0) & (col_id < node_cols * n_tx)
    )
    done = []
    for c in range(2):
        base = c * node_rows
        above = pltpu.roll(lines[-1], (8 - (base + node_rows - 2)) % 8, 0)
        here = pltpu.roll(lines[0], (8 + 2 - base) % 8, 0)
        below = pltpu.roll(lines[1], (8 + 2 + node_rows - base) % 8, 0)
        flow = jnp.where(subs < 2, above, jnp.where(subs < 2 + node_rows, here, below))
        done.append(pltpu.roll(relax(flow, inside), PATCH - 2, 1))
    result = jnp.where(
        subs < node_rows, pltpu.roll(done[0], 6, 0), pltpu.roll(done[1], (8 + node_rows - 2) % 8, 0)
    )
    flows[3] = result

    def mesh_copy(d):
        return pltpu.make_async_remote_copy(
            src_ref=flows.at[3],
            dst_ref=meshes.at[sec],
            send_sem=mesh_send.at[d],
            recv_sem=mesh_recv.at[d],
            device_id=(sec + d, ty, tx),
            device_id_type=MESH,
        )

    def mesh_wait(d):
        pltpu.make_async_remote_copy(
            src_ref=flows.at[3],
            dst_ref=meshes.at[sec - d],
            send_sem=mesh_send.at[d],
            recv_sem=mesh_recv.at[d],
            device_id=(sec - d, ty, tx),
            device_id_type=MESH,
        ).wait_recv()

    for d in range(1, n_sec):
        @pl.when(sec + d < n_sec)
        def _(d=d):
            mesh_copy(d).start()
    for d in range(1, n_sec):
        @pl.when(sec - d >= 0)
        def _(d=d):
            mesh_wait(d)

    earlier = meshes[0]
    for t in range(1, n_sec):
        earlier = earlier + meshes[t]
    out_ref[0] = result
    out_ref[1] = earlier

    flow_each(1, lambda k: flow_copy(k).wait_send())
    for d in range(1, n_sec):
        @pl.when(sec + d < n_sec)
        def _(d=d):
            mesh_copy(d).wait_send()


def solution(mesh):
    sizes = tuple(mesh.shape[axis] for axis in ("sec", "ty", "tx"))

    def on_device(images):
        image = images[0]
        rows, cols = image.shape
        node_rows, node_cols = rows // STRIDE, cols // STRIDE
        high = 2 * HALF + rows
        wide = node_cols * PATCH
        around = len(DIRECTIONS)
        bands = (rows - 2 * HALF) // STRIDE
        n_pieces = 3 + 2 * bands
        dma = pltpu.SemaphoreType.DMA
        out = pl.pallas_call(
            functools.partial(kernel, sizes),
            out_shape=jax.ShapeDtypeStruct((2, 8, PATCH), F32),
            in_specs=[pl.BlockSpec(memory_space=pl.ANY)] * 2,
            out_specs=pl.BlockSpec(memory_space=pltpu.VMEM),
            scratch_shapes=[
                pltpu.VMEM((high, cols + 2 * PATCH), F32),
                pltpu.VMEM((high, cols + 2 * PATCH), F32),
                pltpu.VMEM((high, wide), BF16),
                pltpu.VMEM((high, wide), BF16),
                pltpu.VMEM((high, wide), BF16),
                pltpu.VMEM((high, wide), BF16),
                pltpu.VMEM((node_rows, PATCH, wide), F32),
                pltpu.VMEM((4, 2 * PATCH, 2 * PATCH), BF16),
                pltpu.VMEM((3, node_rows, node_cols, PATCH), F32),
                pltpu.VMEM((4, 8, PATCH), F32),
                pltpu.VMEM((around, 8, PATCH), F32),
                pltpu.VMEM((sizes[0], 8, PATCH), F32),
                pltpu.VMEM((2, rows // 4, PATCH), F32),
                pltpu.VMEM((2, rows // 4, PATCH), F32),
                pltpu.VMEM((2, rows // 4, PATCH), F32),
                pltpu.VMEM((2, rows // 4, PATCH), F32),
                pltpu.VMEM((bands, STRIDE + 2 * HALF, PATCH), F32),
                pltpu.VMEM((bands, STRIDE + 2 * HALF, PATCH), F32),
                pltpu.VMEM((2, STRIDE, PATCH), F32),
                pltpu.VMEM((len(CORNERS), 8, PATCH), F32),
                pltpu.VMEM((len(CORNERS), 8, PATCH), F32),
                pltpu.VMEM((len(CORNERS), 8, PATCH), F32),
                dma((2,)),
                dma((n_pieces,)),
                dma((n_pieces,)),
                dma((4,)),
                dma((4,)),
                dma((4,)),
                dma((4,)),
                dma((2,)),
                dma((2, len(CORNERS))),
                dma((len(CORNERS),)),
                dma((len(CORNERS),)),
                dma((around,)),
                dma((around,)),
                dma((sizes[0],)),
                dma((sizes[0],)),
            ],
            compiler_params=pltpu.CompilerParams(
                collective_id=0, has_side_effects=True, vmem_limit_bytes=60 * 1024 * 1024
            ),
        )(image, jnp.asarray(tables()))
        out = out[:, :, :node_cols].reshape(2, 1, 2, node_rows, node_cols)
        return out[0], out[1]

    return jax.shard_map(
        on_device,
        mesh=mesh,
        in_specs=(P("sec", "ty", "tx"),),
        out_specs=(P("sec", None, "ty", "tx"), P("sec", None, "ty", "tx")),
        check_vma=False,
    )
```

```python
import functools

import jax
import jax.numpy as jnp
import ml_dtypes
import numpy as np
from jax import lax
from jax.experimental import pallas as pl
from jax.experimental.pallas import tpu as pltpu
from jax.sharding import PartitionSpec as P

PATCH = 128
STRIDE = 64
HALF = 32
RATE = 0.25

MESH = pl.DeviceIdType.MESH
CORNERS = [(dy, dx) for dy in (-1, 1) for dx in (-1, 1)]
DIRECTIONS = [(dy, dx) for dy in (-1, 0, 1) for dx in (-1, 0, 1) if (dy, dx) != (0, 0)]
F32 = jnp.float32
BF16 = jnp.bfloat16


def split_table(table):
    high = table.astype(ml_dtypes.bfloat16)
    low = (table - high.astype(np.float64)).astype(ml_dtypes.bfloat16)
    return high, low


def tables():
    half = PATCH // 2
    point = np.arange(PATCH)
    angle = 2.0 * np.pi / PATCH
    packed = np.zeros((PATCH, PATCH))
    for k in range(half):
        packed[k] = np.cos(angle * (k * point % PATCH))
        packed[half + k] = np.sin(angle * (k * point % PATCH))
    packed[half] = np.cos(np.pi * point)
    weight = np.full(PATCH, 2.0)
    weight[0] = weight[half] = 1.0
    inverse = packed.T * weight[None, :] / PATCH

    def left(table):
        high, low = split_table(table)
        return np.block([[high, high], [low, low]])

    def right(table):
        high, low = split_table(table)
        return np.block([[high, low], [high, low]])

    scale = np.log2(np.e) / PATCH
    return np.stack(
        [right(packed.T), left(packed), left(inverse), right(inverse.T * scale)]
    ).astype(ml_dtypes.bfloat16)


def split(value):
    high = value.astype(BF16)
    low = (value - high.astype(F32)).astype(BF16)
    return high, low


def product(own, other):
    half = PATCH // 2
    lane = lax.broadcasted_iota(jnp.int32, (half, PATCH), 1)
    row = lax.broadcasted_iota(jnp.int32, (half, PATCH), 0)
    left = lane < half
    alone = (lane == 0) | (lane == half)
    plain = left | alone
    top_row = row == 0
    t, u = own[:half], own[half:]
    t2, u2 = other[:half], other[half:]
    rt2 = pltpu.roll(t2, half, 1)
    ru2 = pltpu.roll(u2, half, 1)
    uu, uru = u * u2, u * ru2
    g = t * t2 + jnp.where(top_row, 0.0, uu)
    h = t * rt2 + jnp.where(top_row, 0.0, uru)
    g2 = jnp.where(top_row, uu, t * u2 - u * t2)
    h2 = jnp.where(top_row, uru, t * ru2 - u * rt2)

    def joined(g, h):
        cross = pltpu.roll(jnp.where(left, h, g), half, 1)
        cross = jnp.where(alone, 0.0, cross)
        return jnp.where(plain, cross + g, cross - h)

    top = joined(g, h)
    top = jnp.where(top_row & (lane == 0), 0.0, top)
    return jnp.concatenate([top, joined(g2, h2)], axis=0)


def moments(scores):
    peak = jnp.max(jnp.max(scores, axis=0, keepdims=True), axis=1, keepdims=True)
    terms = jnp.exp2(scores - peak)
    total = None
    for g in range(PATCH // 8):
        part = terms[8 * g : 8 * g + 8]
        steps = float(g if g < PATCH // 16 else g - PATCH // 8)
        total = part if total is None else total + part
        first = part * steps if g == 0 else first + part * steps
    sub = lax.broadcasted_iota(jnp.int32, (8, PATCH), 0).astype(F32)
    lane = lax.broadcasted_iota(jnp.int32, (8, PATCH), 1)
    lag = jnp.where(lane < PATCH // 2, lane, lane - PATCH).astype(F32)
    return [
        jnp.sum(value, axis=0, keepdims=True)
        for value in (total, first * 8.0 + total * sub, total * lag)
    ]


def relax(flow, inside):
    def lap(value):
        return (
            pltpu.roll(value, 1, 0)
            + pltpu.roll(value, 7, 0)
            + pltpu.roll(value, 1, 1)
            + pltpu.roll(value, PATCH - 1, 1)
            - 4.0 * value
        )

    first = flow + RATE * (lap(flow) + flow - flow)
    first = jnp.where(inside, first, 0.0)
    return first + RATE * (lap(first) + flow - first)


def kernel(
    sizes, x_ref, tables_ref, out_ref, own, nxt, own_hi, own_lo, nxt_hi, nxt_lo, spec, table,
    stats, flows, around, meshes,
    own_pack, own_land, nxt_pack, nxt_land, own_rest, nxt_rest, edges, tips, own_tips, nxt_tips,
    local_sem, piece_send, piece_recv, own_send, own_recv, nxt_send, nxt_recv, straight_send,
    tip_send, own_tip_recv, nxt_tip_recv,
    flow_send, flow_recv, mesh_send, mesh_recv,
):
    n_sec, n_ty, n_tx = sizes
    rows, cols = x_ref.shape
    node_rows, node_cols = rows // STRIDE, cols // STRIDE
    wide = node_cols * PATCH
    sec, ty, tx = lax.axis_index("sec"), lax.axis_index("ty"), lax.axis_index("tx")

    def there(dy, dx):
        ok = jnp.bool_(True)
        if dy:
            ok = (ty + dy >= 0) & (ty + dy < n_ty)
        if dx:
            in_x = (tx + dx >= 0) & (tx + dx < n_tx)
            ok = ok & in_x if dy else in_x
        return ok

    has_next = sec < n_sec - 1
    has_before = sec > 0

    def crosses(dy):
        return (ty % 2 == 1) if dy > 0 else (ty % 2 == 0)

    bands = (rows - 2 * HALF) // STRIDE
    odd_core = ty % 2 == 1

    def mirrored(k, count=bands):
        return jnp.where(odd_core, count - 1 - k, k)

    def straight(dy):
        return crosses(dy) & there(dy, 0)

    barrier = pltpu.get_barrier_semaphore()

    def greet(ok, s, y, x):
        @pl.when(ok)
        def _():
            pl.semaphore_signal(barrier, inc=1, device_id=(s, y, x), device_id_type=MESH)

    for dy, dx in DIRECTIONS:
        greet(there(dy, dx), sec, ty + dy, tx + dx)
    for dy in (-1, 1):
        greet(has_next & straight(dy), sec + 1, ty + dy, tx)
    for dy, dx in CORNERS:
        greet(has_next & there(dy, dx), sec + 1, ty + dy, tx + dx)
    greet(has_next, sec + 1, ty, tx)
    for d in range(1, n_sec):
        greet(sec - d >= 0, sec - d, ty, tx)

    tile = pltpu.make_async_copy(
        x_ref, own.at[pl.ds(HALF, rows), pl.ds(PATCH, cols)], local_sem.at[0]
    )
    tile.start()
    load = pltpu.make_async_copy(tables_ref, table, local_sem.at[1])
    load.start()

    for ref in (own, nxt):
        @pl.when(ty == 0)
        def _(ref=ref):
            ref[0:HALF, :] = jnp.zeros((HALF, cols + 2 * PATCH), F32)

        @pl.when(ty == n_ty - 1)
        def _(ref=ref):
            ref[HALF + rows : 2 * HALF + rows, :] = jnp.zeros((HALF, cols + 2 * PATCH), F32)

        @pl.when(tx == 0)
        def _(ref=ref):
            ref[:, 0:PATCH] = jnp.zeros((2 * HALF + rows, PATCH), F32)

        @pl.when(tx == n_tx - 1)
        def _(ref=ref):
            ref[:, PATCH + cols :] = jnp.zeros((2 * HALF + rows, PATCH), F32)

    for index, (dy, dx) in enumerate(DIRECTIONS):
        @pl.when(jnp.logical_not(there(-dy, -dx)))
        def _(index=index):
            around[index] = jnp.zeros((8, PATCH), F32)

    for t in range(n_sec):
        @pl.when(t >= sec)
        def _(t=t):
            meshes[t] = jnp.zeros((8, PATCH), F32)

    span = rows // 4
    spans = [(HALF + span * q, span) for q in range(4)]

    def turned(value, by):
        return pltpu.roll(value, by % PATCH, 1) if by % PATCH else value

    def packed(source, where, side):
        lane = lax.broadcasted_iota(jnp.int32, (where[0][1], PATCH), 1)
        at, first = ((PATCH, 0), (cols, PATCH - HALF))[side]
        value = None
        for q, (r, nr) in enumerate(where):
            part = turned(source[r : r + nr, at : at + PATCH], HALF * q - first)
            value = part if q == 0 else jnp.where(lane >= HALF * q, part, value)
        return value

    def unpack(value, target, where, side):
        at, first = ((PATCH + cols, 0), (0, PATCH - HALF))[side]
        for q, (r, nr) in enumerate(where):
            target[r : r + nr, at : at + PATCH] = turned(value, first - HALF * q)

    def unpack_columns(land, target):
        for side in range(2):
            @pl.when(there(0, 1 - 2 * side))
            def _(side=side):
                unpack(land[side], target, spans, side)

    def eighths(start):
        return [(start + 8 * q, 8) for q in range(4)]

    def unpack_tip(land, target, k):
        dy, dx = CORNERS[k]
        unpack(land[k], target, eighths(HALF + rows if dy < 0 else 0), (dx + 1) // 2)

    def pack_rest(m):
        lane = lax.broadcasted_iota(jnp.int32, (STRIDE, PATCH), 1)
        r = 2 * HALF + m * STRIDE
        left = own[r : r + STRIDE, PATCH : 2 * PATCH]
        right = own[r : r + STRIDE, cols : cols + PATCH]
        own_rest[m, 0:STRIDE] = jnp.where(lane < PATCH - HALF, right, left)
        own_rest[m, STRIDE : STRIDE + HALF] = jnp.where(
            lane[:HALF] < STRIDE, turned(left[:HALF], -HALF), turned(left[HALF:], HALF)
        )
        left = own[r : r + STRIDE, 2 * PATCH : 3 * PATCH]
        right = own[r : r + STRIDE, 3 * PATCH : 4 * PATCH]
        lane = lane[:HALF]
        low = jnp.where(lane < HALF, left[:HALF], turned(left[HALF:], HALF))
        high = jnp.where(lane < PATCH - HALF, turned(right[:HALF], -HALF), right[HALF:])
        own_rest[m, STRIDE + HALF : STRIDE + 2 * HALF] = jnp.where(lane < STRIDE, low, high)

    def unpack_rest(m):
        lane = lax.broadcasted_iota(jnp.int32, (HALF, PATCH), 1)
        for h in range(2):
            r = HALF + m * STRIDE + h * HALF
            q, start = r // span, r % span
            border = [nxt_pack[side, start : start + HALF] for side in range(2)]
            main = nxt_rest[m, h * HALF : (h + 1) * HALF]
            half = turned(nxt_rest[m, STRIDE : STRIDE + HALF], HALF if h == 0 else -HALF)
            left = jnp.where(lane < PATCH - HALF, half, main)
            left = jnp.where(lane < HALF, turned(border[0], -HALF * q), left)
            right = jnp.where(lane < PATCH - HALF, main, turned(border[1], PATCH - HALF - HALF * q))
            nxt[HALF + r : 2 * HALF + r, PATCH : 2 * PATCH] = left
            nxt[HALF + r : 2 * HALF + r, cols : cols + PATCH] = right

    def unpack_edges(m):
        strip = nxt_rest[m, STRIDE + HALF : STRIDE + 2 * HALF]
        edges[0] = jnp.concatenate([strip, turned(strip, -HALF)], axis=0)
        edges[1] = jnp.concatenate([turned(strip, HALF), strip], axis=0)

    def at_band(k, do):
        for m in range(bands):
            @pl.when(mirrored(k) == m)
            def _(m=m):
                do(m)

    tile.wait()
    stats[...] = jnp.ones_like(stats)
    for side in range(2):
        own_pack[side] = packed(own, spans, side)
    for k, (dy, dx) in enumerate(CORNERS):
        tips[k] = packed(own, eighths(HALF if dy < 0 else rows), (dx + 1) // 2)
    for m in range(bands):
        pack_rest(m)

    tall = 1 + (ty > 0).astype(jnp.int32) + (ty < n_ty - 1).astype(jnp.int32)
    broad = 1 + (tx > 0).astype(jnp.int32) + (tx < n_tx - 1).astype(jnp.int32)
    apart = (crosses(-1) & there(-1, 0)).astype(jnp.int32) + (crosses(1) & there(1, 0)).astype(jnp.int32)
    back = has_before.astype(jnp.int32) * (1 + apart + (tall - 1) * (broad - 1))
    pl.semaphore_wait(barrier, tall * broad - 1 + back + n_sec - 1 - sec)

    banded = [mirrored(m) for m in range(bands)]

    def band_rest(m, last):
        return (banded[m], STRIDE + 2 * HALF if last else STRIDE + HALF)

    def band_inner(m):
        return (pl.multiple_of(HALF + banded[m] * STRIDE, HALF), STRIDE, PATCH, 2 * PATCH)

    pieces = [(0, HALF, 0, cols), (rows - HALF, HALF, 0, cols), None]
    for m in range(bands):
        pieces += [band_rest(m, m == bands - 1), band_inner(m)]

    def piece_copy(p):
        piece = pieces[p]
        if piece is None:
            src, dst = own_pack, nxt_pack
        elif len(piece) == 2:
            m, nr = piece
            src, dst = own_rest.at[m, pl.ds(0, nr)], nxt_rest.at[m, pl.ds(0, nr)]
        else:
            r, nr, c, nc = piece
            src = x_ref.at[pl.ds(r, nr), pl.ds(c, nc)]
            to = HALF + r if isinstance(r, int) else pl.multiple_of(HALF + r, HALF)
            dst = nxt.at[pl.ds(to, nr), pl.ds(PATCH + c, nc)]
        return pltpu.make_async_remote_copy(
            src_ref=src,
            dst_ref=dst,
            send_sem=piece_send.at[p],
            recv_sem=piece_recv.at[p],
            device_id=(sec - 1, ty, tx),
            device_id_type=MESH,
        )

    def arrived(*indices):
        @pl.when(has_next)
        def _():
            for p in indices:
                piece_copy(p).wait_recv()

    def edge(dy):
        return (0, HALF + rows) if dy < 0 else (rows - HALF, 0)

    def row_copy(dy, through, target, send, recv, to_sec):
        r, to = edge(dy)
        if through is None:
            src = x_ref.at[pl.ds(r, HALF)]
        else:
            src = through.at[pl.ds(HALF + r, HALF), pl.ds(PATCH, cols)]
        side = (dy + 1) // 2
        return pltpu.make_async_remote_copy(
            src_ref=src,
            dst_ref=target.at[pl.ds(to, HALF), pl.ds(PATCH, cols)],
            send_sem=send.at[side],
            recv_sem=recv.at[side],
            device_id=(to_sec, ty + dy, tx),
            device_id_type=MESH,
        )

    def column_copy(dx, pack, land, send, recv):
        side = (dx + 1) // 2
        return pltpu.make_async_remote_copy(
            src_ref=pack.at[side],
            dst_ref=land.at[side],
            send_sem=send.at[2 + side],
            recv_sem=recv.at[2 + side],
            device_id=(sec, ty, tx + dx),
            device_id_type=MESH,
        )

    def own_rows(dy):
        return row_copy(dy, None, own, own_send, own_recv, sec)

    def own_columns(dx):
        return column_copy(dx, own_pack, own_land, own_send, own_recv)

    def nxt_rows(dy):
        return row_copy(dy, nxt, nxt, nxt_send, nxt_recv, sec)

    def nxt_straight(dy):
        return row_copy(dy, None, nxt, straight_send, nxt_recv, sec - 1)

    def nxt_columns(dx):
        return column_copy(dx, nxt_pack, nxt_land, nxt_send, nxt_recv)

    def tip_copy(k, section):
        dy, dx = CORNERS[k]
        return pltpu.make_async_remote_copy(
            src_ref=tips.at[k],
            dst_ref=(own_tips, nxt_tips)[section].at[k],
            send_sem=tip_send.at[section, k],
            recv_sem=(own_tip_recv, nxt_tip_recv)[section].at[k],
            device_id=(sec - section, ty + dy, tx + dx),
            device_id_type=MESH,
        )

    def diagonals(sign, do):
        for k, (dy, dx) in enumerate(CORNERS):
            @pl.when(there(sign * dy, sign * dx))
            def _(k=k):
                do(k)

    def up_down(ok, do):
        for dy in (-1, 1):
            @pl.when(ok(dy))
            def _(dy=dy):
                do(dy)

    def sides(sign, do):
        for dx in (-1, 1):
            @pl.when(there(0, sign * dx))
            def _(dx=dx):
                do(dx)

    def handed_on(dy):
        return jnp.logical_not(crosses(dy)) & there(dy, 0)

    up_down(lambda dy: there(dy, 0), lambda dy: own_rows(dy).start())
    sides(1, lambda dx: own_columns(dx).start())
    diagonals(1, lambda k: tip_copy(k, 0).start())

    @pl.when(has_before)
    def _():
        diagonals(1, lambda k: tip_copy(k, 1).start())
        up_down(straight, lambda dy: nxt_straight(dy).start())

        @pl.when(crosses(-1))
        def _():
            piece_copy(1).start()

        @pl.when(jnp.logical_not(crosses(-1)))
        def _():
            piece_copy(0).start()

        piece_copy(2).start()

        @pl.when(crosses(-1))
        def _():
            piece_copy(0).start()

        @pl.when(jnp.logical_not(crosses(-1)))
        def _():
            piece_copy(1).start()

        for p in range(3, len(pieces)):
            piece_copy(p).start()

    load.wait()

    lane = lax.broadcasted_iota(jnp.int32, (STRIDE, PATCH), 1)
    even, odd = lane < PATCH - HALF, lane >= HALF

    order = [node_cols - 2, node_cols - 1, *range(node_cols - 2)]
    part_cols = node_cols // 2
    parts = (range(0, part_cols), range(part_cols, node_cols))
    every = range(node_cols)

    def right_chunk(source, high, low, b, places, ahead=False):
        at = pl.ds(b * STRIDE if isinstance(b, int) else pl.multiple_of(b * STRIDE, STRIDE), STRIDE)
        patches = []
        for j in (order[p] for p in places):
            t = j // 2
            main = source[at, (t + 1) * PATCH : (t + 2) * PATCH]
            beside = t if j % 2 == 0 else t + 2
            if ahead and j in (1, node_cols - 2):
                part = edges[0 if j == 1 else 1]
            else:
                part = source[at, beside * PATCH : (beside + 1) * PATCH]
            patch = jnp.where(even if j % 2 == 0 else odd, main, part)
            patches.append(jnp.concatenate(split(patch), axis=1))
        got = jnp.dot(jnp.concatenate(patches, axis=0), table[0], preferred_element_type=F32)
        got = got[:, :PATCH] + got[:, PATCH:]
        for n, p in enumerate(places):
            hi, lo = split(got[n * STRIDE : (n + 1) * STRIDE])
            high[at, p * PATCH : (p + 1) * PATCH] = hi
            low[at, p * PATCH : (p + 1) * PATCH] = lo

    def left_spectrum(high, low, i, columns):
        at = pl.ds(pl.multiple_of(i * STRIDE, STRIDE), PATCH)
        both = jnp.concatenate([high[at, columns], low[at, columns]], axis=0)
        got = jnp.dot(table[1], both, preferred_element_type=F32)
        return got[:PATCH] + got[PATCH:]


    def hand_on(dy):
        piece_copy((dy + 1) // 2).wait_recv()
        nxt_rows(dy).start()

    up_down(lambda dy: there(-dy, 0), lambda dy: own_rows(dy).wait_recv())
    sides(-1, lambda dx: own_columns(dx).wait_recv())
    diagonals(-1, lambda k: tip_copy(k, 0).wait_recv())
    unpack_columns(own_land, own)
    diagonals(-1, lambda k: unpack_tip(own_tips, own, k))

    @pl.when(has_next)
    def _():
        up_down(handed_on, hand_on)

    @pl.loop(0, node_rows + 1)
    def _(b):
        right_chunk(own, own_hi, own_lo, b, every)

    @pl.when(has_next)
    def _():
        piece_copy(2).wait_recv()
        sides(1, lambda dx: nxt_columns(dx).start())

    @pl.loop(0, node_rows)
    def _(i):
        for c in range(0, wide, 2 * PATCH):
            at = pl.ds(c, 2 * PATCH)
            spec[i, :, at] = left_spectrum(own_hi, own_lo, i, at)

    @pl.when(has_next)
    def _():
        for dy in (-1, 1):
            @pl.when(jnp.logical_not(handed_on(dy)))
            def _(dy=dy):
                piece_copy((dy + 1) // 2).wait_recv()

        up_down(lambda dy: there(-dy, 0), lambda dy: nxt_rows(dy).wait_recv())
        diagonals(-1, lambda k: tip_copy(k, 1).wait_recv())
        diagonals(-1, lambda k: unpack_tip(nxt_tips, nxt, k))
        sides(-1, lambda dx: nxt_columns(dx).wait_recv())
        unpack_columns(nxt_land, nxt)

    right_chunk(nxt, nxt_hi, nxt_lo, 0, every)
    right_chunk(nxt, nxt_hi, nxt_lo, node_rows, every)

    lanes = lax.broadcasted_iota(jnp.int32, (8, PATCH), 1)

    def flow_block(indices):
        columns = jnp.zeros((8, PATCH), F32)
        for i in indices:
            total, down, across = (jnp.sum(stats[q, i], axis=1, keepdims=True) for q in range(3))
            inv = 1.0 / total
            columns = jnp.where(lanes == i, down * inv, columns)
            columns = jnp.where(lanes == node_rows + i, across * inv, columns)
        columns = pltpu.roll(jnp.where(has_next, columns, 0.0), node_cols - 2, 0)
        return jnp.transpose(jnp.concatenate([columns] * 16, axis=0))[:8]

    def flow_stage(dy, dx):
        if dy == 0:
            return 2
        return jnp.where(crosses(dy), 1, 0 if dx == 0 else 2)

    def flow_copy(index):
        dy, dx = DIRECTIONS[index]
        return pltpu.make_async_remote_copy(
            src_ref=flows.at[flow_stage(dy, dx)],
            dst_ref=around.at[index],
            send_sem=flow_send.at[index],
            recv_sem=flow_recv.at[index],
            device_id=(sec, ty + dy, tx + dx),
            device_id_type=MESH,
        )

    def flow_each(sign, do, stage=None):
        for index, (dy, dx) in enumerate(DIRECTIONS):
            ok = there(sign * dy, sign * dx)
            if stage is not None:
                ok = ok & (flow_stage(dy, dx) == stage)

            @pl.when(ok)
            def _(index=index):
                do(index)

    def flow_send_stage(stage):
        flows[stage] = flow_block(range(node_rows))
        flow_each(1, lambda k: flow_copy(k).start(), stage)

    @pl.loop(0, 4)
    def _(step):
        @pl.when(step == 0)
        def _():
            arrived(3, 4)
            at_band(0, unpack_rest)

        @pl.when(step == 1)
        def _():
            arrived(5, 6)
            at_band(1, unpack_rest)

        @pl.when(step < 2)
        def _():
            right_chunk(nxt, nxt_hi, nxt_lo, 1 + mirrored(step), every)

        @pl.when(step == 2)
        def _():
            flow_send_stage(1)
            arrived(7)
            at_band(2, unpack_rest)
            at_band(2, unpack_edges)
            right_chunk(nxt, nxt_hi, nxt_lo, 1 + mirrored(2), parts[0], True)

        @pl.when(step == 3)
        def _():
            flow_send_stage(2)
            arrived(8)
            right_chunk(nxt, nxt_hi, nxt_lo, 1 + mirrored(2), parts[1])

        halves = [
            (mirrored(jnp.where(step < 2, step, 2 + h), node_rows), jnp.where(step < 2, h, step - 2))
            for h in range(2)
        ]
        nodes = [slice(n * PATCH, (n + 1) * PATCH) for n in range(node_cols)]
        mine, other = [], []
        for i, g in halves:
            columns = pl.ds(pl.multiple_of(g * part_cols * PATCH, PATCH), part_cols * PATCH)
            other.append(left_spectrum(nxt_hi, nxt_lo, i, columns))
            mine.append(spec[i, :, columns])
        mine, other = (jnp.concatenate(value, axis=1) for value in (mine, other))
        prods = jnp.concatenate([product(mine[:, n], other[:, n]) for n in nodes], axis=1)
        mixed = jnp.dot(
            table[2], jnp.concatenate(split(prods), axis=0), preferred_element_type=F32
        )
        hi, lo = split(mixed[:PATCH] + mixed[PATCH:])
        stacked = jnp.concatenate(
            [jnp.concatenate([hi[:, n], lo[:, n]], axis=1) for n in nodes], axis=0
        )
        corr = jnp.dot(stacked, table[3], preferred_element_type=F32)
        corr = corr[:, :PATCH] + corr[:, PATCH:]
        found = [moments(corr[n]) for n in nodes]
        for h, (i, g) in enumerate(halves):
            for q in range(3):
                stats[q, i, pl.ds(g * part_cols, part_cols), :] = jnp.concatenate(
                    [f[q] for f in found[h * part_cols : (h + 1) * part_cols]], axis=0
                )

    block = flow_block(range(node_rows))
    flows[0] = block
    flow_each(1, lambda k: flow_copy(k).start(), 0)

    up_down(lambda dy: there(dy, 0), lambda dy: own_rows(dy).wait_send())
    sides(1, lambda dx: own_columns(dx).wait_send())
    diagonals(1, lambda k: tip_copy(k, 0).wait_send())

    @pl.when(has_before)
    def _():
        for p in range(len(pieces)):
            piece_copy(p).wait_send()
        up_down(straight, lambda dy: nxt_straight(dy).wait_send())
        diagonals(1, lambda k: tip_copy(k, 1).wait_send())

    @pl.when(has_next)
    def _():
        up_down(handed_on, lambda dy: nxt_rows(dy).wait_send())
        sides(1, lambda dx: nxt_columns(dx).wait_send())

    flow_each(-1, lambda k: flow_copy(k).wait_recv())

    lines = {}
    for dy in (-1, 0, 1):
        def from_(dx, dy=dy):
            return block if (dy, dx) == (0, 0) else around[DIRECTIONS.index((-dy, -dx))]

        line = jnp.where(lanes < 2 + node_cols, pltpu.roll(from_(0), 2, 1), pltpu.roll(from_(1), 2 + node_cols, 1))
        lines[dy] = jnp.where(lanes < 2, pltpu.roll(from_(-1), PATCH + 2 - node_cols, 1), line)

    subs = lax.broadcasted_iota(jnp.int32, (8, PATCH), 0)
    row_id = ty * node_rows + subs - 2
    col_id = tx * node_cols + lanes - 2
    inside = (
        (row_id >= 0) & (row_id < node_rows * n_ty) & (col_id >= 0) & (col_id < node_cols * n_tx)
    )
    done = []
    for c in range(2):
        base = c * node_rows
        above = pltpu.roll(lines[-1], (8 - (base + node_rows - 2)) % 8, 0)
        here = pltpu.roll(lines[0], (8 + 2 - base) % 8, 0)
        below = pltpu.roll(lines[1], (8 + 2 + node_rows - base) % 8, 0)
        flow = jnp.where(subs < 2, above, jnp.where(subs < 2 + node_rows, here, below))
        done.append(pltpu.roll(relax(flow, inside), PATCH - 2, 1))
    result = jnp.where(
        subs < node_rows, pltpu.roll(done[0], 6, 0), pltpu.roll(done[1], (8 + node_rows - 2) % 8, 0)
    )
    flows[3] = result

    def mesh_copy(d):
        return pltpu.make_async_remote_copy(
            src_ref=flows.at[3],
            dst_ref=meshes.at[sec],
            send_sem=mesh_send.at[d],
            recv_sem=mesh_recv.at[d],
            device_id=(sec + d, ty, tx),
            device_id_type=MESH,
        )

    def mesh_wait(d):
        pltpu.make_async_remote_copy(
            src_ref=flows.at[3],
            dst_ref=meshes.at[sec - d],
            send_sem=mesh_send.at[d],
            recv_sem=mesh_recv.at[d],
            device_id=(sec - d, ty, tx),
            device_id_type=MESH,
        ).wait_recv()

    for d in range(1, n_sec):
        @pl.when(sec + d < n_sec)
        def _(d=d):
            mesh_copy(d).start()
    for d in range(1, n_sec):
        @pl.when(sec - d >= 0)
        def _(d=d):
            mesh_wait(d)

    earlier = meshes[0]
    for t in range(1, n_sec):
        earlier = earlier + meshes[t]
    out_ref[0] = result
    out_ref[1] = earlier

    flow_each(1, lambda k: flow_copy(k).wait_send())
    for d in range(1, n_sec):
        @pl.when(sec + d < n_sec)
        def _(d=d):
            mesh_copy(d).wait_send()


def solution(mesh):
    sizes = tuple(mesh.shape[axis] for axis in ("sec", "ty", "tx"))

    def on_device(images):
        image = images[0]
        rows, cols = image.shape
        node_rows, node_cols = rows // STRIDE, cols // STRIDE
        high = 2 * HALF + rows
        wide = node_cols * PATCH
        around = len(DIRECTIONS)
        bands = (rows - 2 * HALF) // STRIDE
        n_pieces = 3 + 2 * bands
        dma = pltpu.SemaphoreType.DMA
        out = pl.pallas_call(
            functools.partial(kernel, sizes),
            out_shape=jax.ShapeDtypeStruct((2, 8, PATCH), F32),
            in_specs=[pl.BlockSpec(memory_space=pl.ANY)] * 2,
            out_specs=pl.BlockSpec(memory_space=pltpu.VMEM),
            scratch_shapes=[
                pltpu.VMEM((high, cols + 2 * PATCH), F32),
                pltpu.VMEM((high, cols + 2 * PATCH), F32),
                pltpu.VMEM((high, wide), BF16),
                pltpu.VMEM((high, wide), BF16),
                pltpu.VMEM((high, wide), BF16),
                pltpu.VMEM((high, wide), BF16),
                pltpu.VMEM((node_rows, PATCH, wide), F32),
                pltpu.VMEM((4, 2 * PATCH, 2 * PATCH), BF16),
                pltpu.VMEM((3, node_rows, node_cols, PATCH), F32),
                pltpu.VMEM((4, 8, PATCH), F32),
                pltpu.VMEM((around, 8, PATCH), F32),
                pltpu.VMEM((sizes[0], 8, PATCH), F32),
                pltpu.VMEM((2, rows // 4, PATCH), F32),
                pltpu.VMEM((2, rows // 4, PATCH), F32),
                pltpu.VMEM((2, rows // 4, PATCH), F32),
                pltpu.VMEM((2, rows // 4, PATCH), F32),
                pltpu.VMEM((bands, STRIDE + 2 * HALF, PATCH), F32),
                pltpu.VMEM((bands, STRIDE + 2 * HALF, PATCH), F32),
                pltpu.VMEM((2, STRIDE, PATCH), F32),
                pltpu.VMEM((len(CORNERS), 8, PATCH), F32),
                pltpu.VMEM((len(CORNERS), 8, PATCH), F32),
                pltpu.VMEM((len(CORNERS), 8, PATCH), F32),
                dma((2,)),
                dma((n_pieces,)),
                dma((n_pieces,)),
                dma((4,)),
                dma((4,)),
                dma((4,)),
                dma((4,)),
                dma((2,)),
                dma((2, len(CORNERS))),
                dma((len(CORNERS),)),
                dma((len(CORNERS),)),
                dma((around,)),
                dma((around,)),
                dma((sizes[0],)),
                dma((sizes[0],)),
            ],
            compiler_params=pltpu.CompilerParams(
                collective_id=0, has_side_effects=True, vmem_limit_bytes=60 * 1024 * 1024
            ),
        )(image, jnp.asarray(tables()))
        out = out[:, :, :node_cols].reshape(2, 1, 2, node_rows, node_cols)
        return out[0], out[1]

    return jax.shard_map(
        on_device,
        mesh=mesh,
        in_specs=(P("sec", "ty", "tx"),),
        out_specs=(P("sec", None, "ty", "tx"), P("sec", None, "ty", "tx")),
        check_vma=False,
    )
```

```python
import functools

import jax
import jax.numpy as jnp
import ml_dtypes
import numpy as np
from jax import lax
from jax.experimental import pallas as pl
from jax.experimental.pallas import tpu as pltpu
from jax.sharding import PartitionSpec as P

PATCH = 128
STRIDE = 64
HALF = 32
RATE = 0.25

MESH = pl.DeviceIdType.MESH
CORNERS = [(dy, dx) for dy in (-1, 1) for dx in (-1, 1)]
DIRECTIONS = [(dy, dx) for dy in (-1, 0, 1) for dx in (-1, 0, 1) if (dy, dx) != (0, 0)]
F32 = jnp.float32
BF16 = jnp.bfloat16


def split_table(table):
    high = table.astype(ml_dtypes.bfloat16)
    low = (table - high.astype(np.float64)).astype(ml_dtypes.bfloat16)
    return high, low


def tables():
    half = PATCH // 2
    point = np.arange(PATCH)
    angle = 2.0 * np.pi / PATCH
    packed = np.zeros((PATCH, PATCH))
    for k in range(half):
        packed[k] = np.cos(angle * (k * point % PATCH))
        packed[half + k] = np.sin(angle * (k * point % PATCH))
    packed[half] = np.cos(np.pi * point)
    weight = np.full(PATCH, 2.0)
    weight[0] = weight[half] = 1.0
    inverse = packed.T * weight[None, :] / PATCH

    def left(table):
        high, low = split_table(table)
        return np.block([[high, high], [low, low]])

    def right(table):
        high, low = split_table(table)
        return np.block([[high, low], [high, low]])

    scale = np.log2(np.e) / PATCH
    return np.stack(
        [right(packed.T), left(packed), left(inverse), right(inverse.T * scale)]
    ).astype(ml_dtypes.bfloat16)


def split(value):
    high = value.astype(BF16)
    low = (value - high.astype(F32)).astype(BF16)
    return high, low


def product(own, turned, other):
    half = PATCH // 2
    lane = lax.broadcasted_iota(jnp.int32, (half, PATCH), 1)
    row = lax.broadcasted_iota(jnp.int32, (half, PATCH), 0)
    left = lane < half
    alone = (lane == 0) | (lane == half)
    plain = left | alone
    top_row = row == 0
    t, u = own[:half], own[half:]
    t2, u2 = other[:half], other[half:]
    rt, ru = turned[:half], turned[half:]
    uu, uru = u * u2, ru * u2
    g = t * t2 + jnp.where(top_row, 0.0, uu)
    h = rt * t2 + jnp.where(top_row, 0.0, uru)
    g2 = jnp.where(top_row, uu, t * u2 - u * t2)
    h2 = jnp.where(top_row, uru, rt * u2 - ru * t2)

    def joined(g, h):
        cross = pltpu.roll(jnp.where(left, h, g), half, 1)
        cross = jnp.where(alone, 0.0, cross)
        return jnp.where(plain, g + cross, h - cross)

    top = joined(g, h)
    top = jnp.where(top_row & (lane == 0), 0.0, top)
    return jnp.concatenate([top, joined(g2, h2)], axis=0)


def moments(scores):
    peak = jnp.max(jnp.max(scores, axis=0, keepdims=True), axis=1, keepdims=True)
    terms = jnp.exp2(scores - peak)
    total = None
    for g in range(PATCH // 8):
        part = terms[8 * g : 8 * g + 8]
        steps = float(g if g < PATCH // 16 else g - PATCH // 8)
        total = part if total is None else total + part
        first = part * steps if g == 0 else first + part * steps
    sub = lax.broadcasted_iota(jnp.int32, (8, PATCH), 0).astype(F32)
    lane = lax.broadcasted_iota(jnp.int32, (8, PATCH), 1)
    lag = jnp.where(lane < PATCH // 2, lane, lane - PATCH).astype(F32)
    return [
        jnp.sum(value, axis=0, keepdims=True)
        for value in (total, first * 8.0 + total * sub, total * lag)
    ]


def relax(flow, inside):
    def lap(value):
        return (
            pltpu.roll(value, 1, 0)
            + pltpu.roll(value, 7, 0)
            + pltpu.roll(value, 1, 1)
            + pltpu.roll(value, PATCH - 1, 1)
            - 4.0 * value
        )

    first = flow + RATE * (lap(flow) + flow - flow)
    first = jnp.where(inside, first, 0.0)
    return first + RATE * (lap(first) + flow - first)


def kernel(
    sizes, x_ref, tables_ref, out_ref, own, nxt, own_hi, own_lo, nxt_hi, nxt_lo, spec, table,
    stats, flows, around, meshes,
    own_pack, own_land, nxt_pack, nxt_land, own_rest, nxt_rest, edges, tips, own_tips, nxt_tips,
    local_sem, piece_send, piece_recv, own_send, own_recv, nxt_send, nxt_recv, straight_send,
    tip_send, own_tip_recv, nxt_tip_recv,
    flow_send, flow_recv, mesh_send, mesh_recv,
):
    n_sec, n_ty, n_tx = sizes
    rows, cols = x_ref.shape
    node_rows, node_cols = rows // STRIDE, cols // STRIDE
    wide = node_cols * PATCH
    sec, ty, tx = lax.axis_index("sec"), lax.axis_index("ty"), lax.axis_index("tx")

    def there(dy, dx):
        ok = jnp.bool_(True)
        if dy:
            ok = (ty + dy >= 0) & (ty + dy < n_ty)
        if dx:
            in_x = (tx + dx >= 0) & (tx + dx < n_tx)
            ok = ok & in_x if dy else in_x
        return ok

    has_next = sec < n_sec - 1
    has_before = sec > 0

    def crosses(dy):
        return (ty % 2 == 1) if dy > 0 else (ty % 2 == 0)

    bands = (rows - 2 * HALF) // STRIDE
    odd_core = ty % 2 == 1

    def mirrored(k, count=bands):
        return jnp.where(odd_core, count - 1 - k, k)

    def straight(dy):
        return crosses(dy) & there(dy, 0)

    barrier = pltpu.get_barrier_semaphore()

    def greet(ok, s, y, x):
        @pl.when(ok)
        def _():
            pl.semaphore_signal(barrier, inc=1, device_id=(s, y, x), device_id_type=MESH)

    for dy, dx in DIRECTIONS:
        greet(there(dy, dx), sec, ty + dy, tx + dx)
    for dy in (-1, 1):
        greet(has_next & straight(dy), sec + 1, ty + dy, tx)
    for dy, dx in CORNERS:
        greet(has_next & there(dy, dx), sec + 1, ty + dy, tx + dx)
    greet(has_next, sec + 1, ty, tx)
    for d in range(1, n_sec):
        greet(sec - d >= 0, sec - d, ty, tx)

    tile = pltpu.make_async_copy(
        x_ref, own.at[pl.ds(HALF, rows), pl.ds(PATCH, cols)], local_sem.at[0]
    )
    tile.start()
    load = pltpu.make_async_copy(tables_ref, table, local_sem.at[1])
    load.start()

    for ref in (own, nxt):
        @pl.when(ty == 0)
        def _(ref=ref):
            ref[0:HALF, :] = jnp.zeros((HALF, cols + 2 * PATCH), F32)

        @pl.when(ty == n_ty - 1)
        def _(ref=ref):
            ref[HALF + rows : 2 * HALF + rows, :] = jnp.zeros((HALF, cols + 2 * PATCH), F32)

        @pl.when(tx == 0)
        def _(ref=ref):
            ref[:, 0:PATCH] = jnp.zeros((2 * HALF + rows, PATCH), F32)

        @pl.when(tx == n_tx - 1)
        def _(ref=ref):
            ref[:, PATCH + cols :] = jnp.zeros((2 * HALF + rows, PATCH), F32)

    for index, (dy, dx) in enumerate(DIRECTIONS):
        @pl.when(jnp.logical_not(there(-dy, -dx)))
        def _(index=index):
            around[index] = jnp.zeros((8, PATCH), F32)

    for t in range(n_sec):
        @pl.when(t >= sec)
        def _(t=t):
            meshes[t] = jnp.zeros((8, PATCH), F32)

    span = rows // 4
    spans = [(HALF + span * q, span) for q in range(4)]

    def turned(value, by):
        return pltpu.roll(value, by % PATCH, 1) if by % PATCH else value

    def packed(source, where, side):
        lane = lax.broadcasted_iota(jnp.int32, (where[0][1], PATCH), 1)
        at, first = ((PATCH, 0), (cols, PATCH - HALF))[side]
        value = None
        for q, (r, nr) in enumerate(where):
            part = turned(source[r : r + nr, at : at + PATCH], HALF * q - first)
            value = part if q == 0 else jnp.where(lane >= HALF * q, part, value)
        return value

    def unpack(value, target, where, side):
        at, first = ((PATCH + cols, 0), (0, PATCH - HALF))[side]
        for q, (r, nr) in enumerate(where):
            target[r : r + nr, at : at + PATCH] = turned(value, first - HALF * q)

    def unpack_columns(land, target):
        for side in range(2):
            @pl.when(there(0, 1 - 2 * side))
            def _(side=side):
                unpack(land[side], target, spans, side)

    def eighths(start):
        return [(start + 8 * q, 8) for q in range(4)]

    def unpack_tip(land, target, k):
        dy, dx = CORNERS[k]
        unpack(land[k], target, eighths(HALF + rows if dy < 0 else 0), (dx + 1) // 2)

    def pack_rest(m):
        lane = lax.broadcasted_iota(jnp.int32, (STRIDE, PATCH), 1)
        r = 2 * HALF + m * STRIDE
        left = own[r : r + STRIDE, PATCH : 2 * PATCH]
        right = own[r : r + STRIDE, cols : cols + PATCH]
        own_rest[m, 0:STRIDE] = jnp.where(lane < PATCH - HALF, right, left)
        own_rest[m, STRIDE : STRIDE + HALF] = jnp.where(
            lane[:HALF] < STRIDE, turned(left[:HALF], -HALF), turned(left[HALF:], HALF)
        )
        left = own[r : r + STRIDE, 2 * PATCH : 3 * PATCH]
        right = own[r : r + STRIDE, 3 * PATCH : 4 * PATCH]
        lane = lane[:HALF]
        low = jnp.where(lane < HALF, left[:HALF], turned(left[HALF:], HALF))
        high = jnp.where(lane < PATCH - HALF, turned(right[:HALF], -HALF), right[HALF:])
        own_rest[m, STRIDE + HALF : STRIDE + 2 * HALF] = jnp.where(lane < STRIDE, low, high)

    def unpack_rest(m):
        lane = lax.broadcasted_iota(jnp.int32, (HALF, PATCH), 1)
        for h in range(2):
            r = HALF + m * STRIDE + h * HALF
            q, start = r // span, r % span
            border = [nxt_pack[side, start : start + HALF] for side in range(2)]
            main = nxt_rest[m, h * HALF : (h + 1) * HALF]
            half = turned(nxt_rest[m, STRIDE : STRIDE + HALF], HALF if h == 0 else -HALF)
            left = jnp.where(lane < PATCH - HALF, half, main)
            left = jnp.where(lane < HALF, turned(border[0], -HALF * q), left)
            right = jnp.where(lane < PATCH - HALF, main, turned(border[1], PATCH - HALF - HALF * q))
            nxt[HALF + r : 2 * HALF + r, PATCH : 2 * PATCH] = left
            nxt[HALF + r : 2 * HALF + r, cols : cols + PATCH] = right

    def unpack_edges(m):
        strip = nxt_rest[m, STRIDE + HALF : STRIDE + 2 * HALF]
        edges[0] = jnp.concatenate([strip, turned(strip, -HALF)], axis=0)
        edges[1] = jnp.concatenate([turned(strip, HALF), strip], axis=0)

    def at_band(k, do):
        for m in range(bands):
            @pl.when(mirrored(k) == m)
            def _(m=m):
                do(m)

    tile.wait()
    stats[...] = jnp.ones_like(stats)
    for side in range(2):
        own_pack[side] = packed(own, spans, side)
    for k, (dy, dx) in enumerate(CORNERS):
        tips[k] = packed(own, eighths(HALF if dy < 0 else rows), (dx + 1) // 2)
    for m in range(bands):
        pack_rest(m)

    tall = 1 + (ty > 0).astype(jnp.int32) + (ty < n_ty - 1).astype(jnp.int32)
    broad = 1 + (tx > 0).astype(jnp.int32) + (tx < n_tx - 1).astype(jnp.int32)
    apart = (crosses(-1) & there(-1, 0)).astype(jnp.int32) + (crosses(1) & there(1, 0)).astype(jnp.int32)
    back = has_before.astype(jnp.int32) * (1 + apart + (tall - 1) * (broad - 1))
    pl.semaphore_wait(barrier, tall * broad - 1 + back + n_sec - 1 - sec)

    banded = [mirrored(m) for m in range(bands)]

    def band_rest(m, last):
        return (banded[m], STRIDE + 2 * HALF if last else STRIDE + HALF)

    def band_inner(m):
        return (pl.multiple_of(HALF + banded[m] * STRIDE, HALF), STRIDE, PATCH, 2 * PATCH)

    pieces = [(0, HALF, 0, cols), (rows - HALF, HALF, 0, cols), None]
    for m in range(bands):
        pieces += [band_rest(m, m == bands - 1), band_inner(m)]

    def piece_copy(p):
        piece = pieces[p]
        if piece is None:
            src, dst = own_pack, nxt_pack
        elif len(piece) == 2:
            m, nr = piece
            src, dst = own_rest.at[m, pl.ds(0, nr)], nxt_rest.at[m, pl.ds(0, nr)]
        else:
            r, nr, c, nc = piece
            src = x_ref.at[pl.ds(r, nr), pl.ds(c, nc)]
            to = HALF + r if isinstance(r, int) else pl.multiple_of(HALF + r, HALF)
            dst = nxt.at[pl.ds(to, nr), pl.ds(PATCH + c, nc)]
        return pltpu.make_async_remote_copy(
            src_ref=src,
            dst_ref=dst,
            send_sem=piece_send.at[p],
            recv_sem=piece_recv.at[p],
            device_id=(sec - 1, ty, tx),
            device_id_type=MESH,
        )

    def arrived(*indices):
        @pl.when(has_next)
        def _():
            for p in indices:
                piece_copy(p).wait_recv()

    def edge(dy):
        return (0, HALF + rows) if dy < 0 else (rows - HALF, 0)

    def row_copy(dy, through, target, send, recv, to_sec):
        r, to = edge(dy)
        if through is None:
            src = x_ref.at[pl.ds(r, HALF)]
        else:
            src = through.at[pl.ds(HALF + r, HALF), pl.ds(PATCH, cols)]
        side = (dy + 1) // 2
        return pltpu.make_async_remote_copy(
            src_ref=src,
            dst_ref=target.at[pl.ds(to, HALF), pl.ds(PATCH, cols)],
            send_sem=send.at[side],
            recv_sem=recv.at[side],
            device_id=(to_sec, ty + dy, tx),
            device_id_type=MESH,
        )

    def column_copy(dx, pack, land, send, recv):
        side = (dx + 1) // 2
        return pltpu.make_async_remote_copy(
            src_ref=pack.at[side],
            dst_ref=land.at[side],
            send_sem=send.at[2 + side],
            recv_sem=recv.at[2 + side],
            device_id=(sec, ty, tx + dx),
            device_id_type=MESH,
        )

    def own_rows(dy):
        return row_copy(dy, None, own, own_send, own_recv, sec)

    def own_columns(dx):
        return column_copy(dx, own_pack, own_land, own_send, own_recv)

    def nxt_rows(dy):
        return row_copy(dy, nxt, nxt, nxt_send, nxt_recv, sec)

    def nxt_straight(dy):
        return row_copy(dy, None, nxt, straight_send, nxt_recv, sec - 1)

    def nxt_columns(dx):
        return column_copy(dx, nxt_pack, nxt_land, nxt_send, nxt_recv)

    def tip_copy(k, section):
        dy, dx = CORNERS[k]
        return pltpu.make_async_remote_copy(
            src_ref=tips.at[k],
            dst_ref=(own_tips, nxt_tips)[section].at[k],
            send_sem=tip_send.at[section, k],
            recv_sem=(own_tip_recv, nxt_tip_recv)[section].at[k],
            device_id=(sec - section, ty + dy, tx + dx),
            device_id_type=MESH,
        )

    def diagonals(sign, do):
        for k, (dy, dx) in enumerate(CORNERS):
            @pl.when(there(sign * dy, sign * dx))
            def _(k=k):
                do(k)

    def up_down(ok, do):
        for dy in (-1, 1):
            @pl.when(ok(dy))
            def _(dy=dy):
                do(dy)

    def sides(sign, do):
        for dx in (-1, 1):
            @pl.when(there(0, sign * dx))
            def _(dx=dx):
                do(dx)

    def handed_on(dy):
        return jnp.logical_not(crosses(dy)) & there(dy, 0)

    up_down(lambda dy: there(dy, 0), lambda dy: own_rows(dy).start())
    sides(1, lambda dx: own_columns(dx).start())
    diagonals(1, lambda k: tip_copy(k, 0).start())

    @pl.when(has_before)
    def _():
        diagonals(1, lambda k: tip_copy(k, 1).start())
        up_down(straight, lambda dy: nxt_straight(dy).start())

        @pl.when(crosses(-1))
        def _():
            piece_copy(1).start()

        @pl.when(jnp.logical_not(crosses(-1)))
        def _():
            piece_copy(0).start()

        piece_copy(2).start()

        @pl.when(crosses(-1))
        def _():
            piece_copy(0).start()

        @pl.when(jnp.logical_not(crosses(-1)))
        def _():
            piece_copy(1).start()

        for p in range(3, len(pieces)):
            piece_copy(p).start()

    load.wait()

    lane = lax.broadcasted_iota(jnp.int32, (STRIDE, PATCH), 1)
    even, odd = lane < PATCH - HALF, lane >= HALF

    order = [node_cols - 2, node_cols - 1, *range(node_cols - 2)]
    part_cols = node_cols // 2
    parts = (range(0, part_cols), range(part_cols, node_cols))
    every = range(node_cols)

    def right_chunk(source, high, low, b, places, ahead=False):
        at = pl.ds(b * STRIDE if isinstance(b, int) else pl.multiple_of(b * STRIDE, STRIDE), STRIDE)
        patches = []
        for j in (order[p] for p in places):
            t = j // 2
            main = source[at, (t + 1) * PATCH : (t + 2) * PATCH]
            beside = t if j % 2 == 0 else t + 2
            if ahead and j in (1, node_cols - 2):
                part = edges[0 if j == 1 else 1]
            else:
                part = source[at, beside * PATCH : (beside + 1) * PATCH]
            patch = jnp.where(even if j % 2 == 0 else odd, main, part)
            patches.append(jnp.concatenate(split(patch), axis=1))
        got = jnp.dot(jnp.concatenate(patches, axis=0), table[0], preferred_element_type=F32)
        got = got[:, :PATCH] + got[:, PATCH:]
        for n, p in enumerate(places):
            hi, lo = split(got[n * STRIDE : (n + 1) * STRIDE])
            high[at, p * PATCH : (p + 1) * PATCH] = hi
            low[at, p * PATCH : (p + 1) * PATCH] = lo

    def left_spectrum(high, low, i, columns):
        at = pl.ds(pl.multiple_of(i * STRIDE, STRIDE), PATCH)
        both = jnp.concatenate([high[at, columns], low[at, columns]], axis=0)
        got = jnp.dot(table[1], both, preferred_element_type=F32)
        return got[:PATCH] + got[PATCH:]


    def hand_on(dy):
        piece_copy((dy + 1) // 2).wait_recv()
        nxt_rows(dy).start()

    up_down(lambda dy: there(-dy, 0), lambda dy: own_rows(dy).wait_recv())
    sides(-1, lambda dx: own_columns(dx).wait_recv())
    diagonals(-1, lambda k: tip_copy(k, 0).wait_recv())
    unpack_columns(own_land, own)
    diagonals(-1, lambda k: unpack_tip(own_tips, own, k))

    @pl.when(has_next)
    def _():
        up_down(handed_on, hand_on)

    @pl.loop(0, node_rows + 1)
    def _(b):
        right_chunk(own, own_hi, own_lo, b, every)

    @pl.when(has_next)
    def _():
        piece_copy(2).wait_recv()
        sides(1, lambda dx: nxt_columns(dx).start())

    @pl.loop(0, node_rows)
    def _(i):
        for c in range(0, wide, 2 * PATCH):
            at = pl.ds(c, 2 * PATCH)
            got = left_spectrum(own_hi, own_lo, i, at)
            spec[i, 0, :, at] = got
            for n in range(2):
                spec[i, 1, :, pl.ds(c + n * PATCH, PATCH)] = pltpu.roll(
                    got[:, n * PATCH : (n + 1) * PATCH], PATCH // 2, 1
                )

    @pl.when(has_next)
    def _():
        for dy in (-1, 1):
            @pl.when(jnp.logical_not(handed_on(dy)))
            def _(dy=dy):
                piece_copy((dy + 1) // 2).wait_recv()

        up_down(lambda dy: there(-dy, 0), lambda dy: nxt_rows(dy).wait_recv())
        diagonals(-1, lambda k: tip_copy(k, 1).wait_recv())
        diagonals(-1, lambda k: unpack_tip(nxt_tips, nxt, k))
        sides(-1, lambda dx: nxt_columns(dx).wait_recv())
        unpack_columns(nxt_land, nxt)

    right_chunk(nxt, nxt_hi, nxt_lo, 0, every)
    right_chunk(nxt, nxt_hi, nxt_lo, node_rows, every)

    lanes = lax.broadcasted_iota(jnp.int32, (8, PATCH), 1)

    def flow_block(indices):
        columns = jnp.zeros((8, PATCH), F32)
        for i in indices:
            total, down, across = (jnp.sum(stats[q, i], axis=1, keepdims=True) for q in range(3))
            inv = 1.0 / total
            columns = jnp.where(lanes == i, down * inv, columns)
            columns = jnp.where(lanes == node_rows + i, across * inv, columns)
        columns = pltpu.roll(jnp.where(has_next, columns, 0.0), node_cols - 2, 0)
        return jnp.transpose(jnp.concatenate([columns] * 16, axis=0))[:8]

    def flow_stage(dy, dx):
        if dy == 0:
            return 2
        return jnp.where(crosses(dy), 1, 0 if dx == 0 else 2)

    def flow_copy(index):
        dy, dx = DIRECTIONS[index]
        return pltpu.make_async_remote_copy(
            src_ref=flows.at[flow_stage(dy, dx)],
            dst_ref=around.at[index],
            send_sem=flow_send.at[index],
            recv_sem=flow_recv.at[index],
            device_id=(sec, ty + dy, tx + dx),
            device_id_type=MESH,
        )

    def flow_each(sign, do, stage=None):
        for index, (dy, dx) in enumerate(DIRECTIONS):
            ok = there(sign * dy, sign * dx)
            if stage is not None:
                ok = ok & (flow_stage(dy, dx) == stage)

            @pl.when(ok)
            def _(index=index):
                do(index)

    def flow_send_stage(stage):
        flows[stage] = flow_block(range(node_rows))
        flow_each(1, lambda k: flow_copy(k).start(), stage)

    @pl.loop(0, 4)
    def _(step):
        @pl.when(step == 0)
        def _():
            arrived(3, 4)
            at_band(0, unpack_rest)

        @pl.when(step == 1)
        def _():
            arrived(5, 6)
            at_band(1, unpack_rest)

        @pl.when(step < 2)
        def _():
            right_chunk(nxt, nxt_hi, nxt_lo, 1 + mirrored(step), every)

        @pl.when(step == 2)
        def _():
            flow_send_stage(1)
            arrived(7)
            at_band(2, unpack_rest)
            at_band(2, unpack_edges)
            right_chunk(nxt, nxt_hi, nxt_lo, 1 + mirrored(2), parts[0], True)

        @pl.when(step == 3)
        def _():
            flow_send_stage(2)
            arrived(8)
            right_chunk(nxt, nxt_hi, nxt_lo, 1 + mirrored(2), parts[1])

        halves = [
            (mirrored(jnp.where(step < 2, step, 2 + h), node_rows), jnp.where(step < 2, h, step - 2))
            for h in range(2)
        ]
        nodes = [slice(n * PATCH, (n + 1) * PATCH) for n in range(node_cols)]
        mine, swapped, other = [], [], []
        for i, g in halves:
            columns = pl.ds(pl.multiple_of(g * part_cols * PATCH, PATCH), part_cols * PATCH)
            other.append(left_spectrum(nxt_hi, nxt_lo, i, columns))
            mine.append(spec[i, 0, :, columns])
            swapped.append(spec[i, 1, :, columns])
        mine, swapped, other = (jnp.concatenate(value, axis=1) for value in (mine, swapped, other))
        prods = jnp.concatenate([product(mine[:, n], swapped[:, n], other[:, n]) for n in nodes], axis=1)
        mixed = jnp.dot(
            table[2], jnp.concatenate(split(prods), axis=0), preferred_element_type=F32
        )
        hi, lo = split(mixed[:PATCH] + mixed[PATCH:])
        stacked = jnp.concatenate(
            [jnp.concatenate([hi[:, n], lo[:, n]], axis=1) for n in nodes], axis=0
        )
        corr = jnp.dot(stacked, table[3], preferred_element_type=F32)
        corr = corr[:, :PATCH] + corr[:, PATCH:]
        found = [moments(corr[n]) for n in nodes]
        for h, (i, g) in enumerate(halves):
            for q in range(3):
                stats[q, i, pl.ds(g * part_cols, part_cols), :] = jnp.concatenate(
                    [f[q] for f in found[h * part_cols : (h + 1) * part_cols]], axis=0
                )

    block = flow_block(range(node_rows))
    flows[0] = block
    flow_each(1, lambda k: flow_copy(k).start(), 0)

    up_down(lambda dy: there(dy, 0), lambda dy: own_rows(dy).wait_send())
    sides(1, lambda dx: own_columns(dx).wait_send())
    diagonals(1, lambda k: tip_copy(k, 0).wait_send())

    @pl.when(has_before)
    def _():
        for p in range(len(pieces)):
            piece_copy(p).wait_send()
        up_down(straight, lambda dy: nxt_straight(dy).wait_send())
        diagonals(1, lambda k: tip_copy(k, 1).wait_send())

    @pl.when(has_next)
    def _():
        up_down(handed_on, lambda dy: nxt_rows(dy).wait_send())
        sides(1, lambda dx: nxt_columns(dx).wait_send())

    flow_each(-1, lambda k: flow_copy(k).wait_recv())

    lines = {}
    for dy in (-1, 0, 1):
        def from_(dx, dy=dy):
            return block if (dy, dx) == (0, 0) else around[DIRECTIONS.index((-dy, -dx))]

        line = jnp.where(lanes < 2 + node_cols, pltpu.roll(from_(0), 2, 1), pltpu.roll(from_(1), 2 + node_cols, 1))
        lines[dy] = jnp.where(lanes < 2, pltpu.roll(from_(-1), PATCH + 2 - node_cols, 1), line)

    subs = lax.broadcasted_iota(jnp.int32, (8, PATCH), 0)
    row_id = ty * node_rows + subs - 2
    col_id = tx * node_cols + lanes - 2
    inside = (
        (row_id >= 0) & (row_id < node_rows * n_ty) & (col_id >= 0) & (col_id < node_cols * n_tx)
    )
    done = []
    for c in range(2):
        base = c * node_rows
        above = pltpu.roll(lines[-1], (8 - (base + node_rows - 2)) % 8, 0)
        here = pltpu.roll(lines[0], (8 + 2 - base) % 8, 0)
        below = pltpu.roll(lines[1], (8 + 2 + node_rows - base) % 8, 0)
        flow = jnp.where(subs < 2, above, jnp.where(subs < 2 + node_rows, here, below))
        done.append(pltpu.roll(relax(flow, inside), PATCH - 2, 1))
    result = jnp.where(
        subs < node_rows, pltpu.roll(done[0], 6, 0), pltpu.roll(done[1], (8 + node_rows - 2) % 8, 0)
    )
    flows[3] = result

    def mesh_copy(d):
        return pltpu.make_async_remote_copy(
            src_ref=flows.at[3],
            dst_ref=meshes.at[sec],
            send_sem=mesh_send.at[d],
            recv_sem=mesh_recv.at[d],
            device_id=(sec + d, ty, tx),
            device_id_type=MESH,
        )

    def mesh_wait(d):
        pltpu.make_async_remote_copy(
            src_ref=flows.at[3],
            dst_ref=meshes.at[sec - d],
            send_sem=mesh_send.at[d],
            recv_sem=mesh_recv.at[d],
            device_id=(sec - d, ty, tx),
            device_id_type=MESH,
        ).wait_recv()

    for d in range(1, n_sec):
        @pl.when(sec + d < n_sec)
        def _(d=d):
            mesh_copy(d).start()
    for d in range(1, n_sec):
        @pl.when(sec - d >= 0)
        def _(d=d):
            mesh_wait(d)

    earlier = meshes[0]
    for t in range(1, n_sec):
        earlier = earlier + meshes[t]
    out_ref[0] = result
    out_ref[1] = earlier

    flow_each(1, lambda k: flow_copy(k).wait_send())
    for d in range(1, n_sec):
        @pl.when(sec + d < n_sec)
        def _(d=d):
            mesh_copy(d).wait_send()


def solution(mesh):
    sizes = tuple(mesh.shape[axis] for axis in ("sec", "ty", "tx"))

    def on_device(images):
        image = images[0]
        rows, cols = image.shape
        node_rows, node_cols = rows // STRIDE, cols // STRIDE
        high = 2 * HALF + rows
        wide = node_cols * PATCH
        around = len(DIRECTIONS)
        bands = (rows - 2 * HALF) // STRIDE
        n_pieces = 3 + 2 * bands
        dma = pltpu.SemaphoreType.DMA
        out = pl.pallas_call(
            functools.partial(kernel, sizes),
            out_shape=jax.ShapeDtypeStruct((2, 8, PATCH), F32),
            in_specs=[pl.BlockSpec(memory_space=pl.ANY)] * 2,
            out_specs=pl.BlockSpec(memory_space=pltpu.VMEM),
            scratch_shapes=[
                pltpu.VMEM((high, cols + 2 * PATCH), F32),
                pltpu.VMEM((high, cols + 2 * PATCH), F32),
                pltpu.VMEM((high, wide), BF16),
                pltpu.VMEM((high, wide), BF16),
                pltpu.VMEM((high, wide), BF16),
                pltpu.VMEM((high, wide), BF16),
                pltpu.VMEM((node_rows, 2, PATCH, wide), F32),
                pltpu.VMEM((4, 2 * PATCH, 2 * PATCH), BF16),
                pltpu.VMEM((3, node_rows, node_cols, PATCH), F32),
                pltpu.VMEM((4, 8, PATCH), F32),
                pltpu.VMEM((around, 8, PATCH), F32),
                pltpu.VMEM((sizes[0], 8, PATCH), F32),
                pltpu.VMEM((2, rows // 4, PATCH), F32),
                pltpu.VMEM((2, rows // 4, PATCH), F32),
                pltpu.VMEM((2, rows // 4, PATCH), F32),
                pltpu.VMEM((2, rows // 4, PATCH), F32),
                pltpu.VMEM((bands, STRIDE + 2 * HALF, PATCH), F32),
                pltpu.VMEM((bands, STRIDE + 2 * HALF, PATCH), F32),
                pltpu.VMEM((2, STRIDE, PATCH), F32),
                pltpu.VMEM((len(CORNERS), 8, PATCH), F32),
                pltpu.VMEM((len(CORNERS), 8, PATCH), F32),
                pltpu.VMEM((len(CORNERS), 8, PATCH), F32),
                dma((2,)),
                dma((n_pieces,)),
                dma((n_pieces,)),
                dma((4,)),
                dma((4,)),
                dma((4,)),
                dma((4,)),
                dma((2,)),
                dma((2, len(CORNERS))),
                dma((len(CORNERS),)),
                dma((len(CORNERS),)),
                dma((around,)),
                dma((around,)),
                dma((sizes[0],)),
                dma((sizes[0],)),
            ],
            compiler_params=pltpu.CompilerParams(
                collective_id=0, has_side_effects=True, vmem_limit_bytes=60 * 1024 * 1024
            ),
        )(image, jnp.asarray(tables()))
        out = out[:, :, :node_cols].reshape(2, 1, 2, node_rows, node_cols)
        return out[0], out[1]

    return jax.shard_map(
        on_device,
        mesh=mesh,
        in_specs=(P("sec", "ty", "tx"),),
        out_specs=(P("sec", None, "ty", "tx"), P("sec", None, "ty", "tx")),
        check_vma=False,
    )
```

```python
import functools

import jax
import jax.numpy as jnp
import ml_dtypes
import numpy as np
from jax import lax
from jax.experimental import pallas as pl
from jax.experimental.pallas import tpu as pltpu
from jax.sharding import PartitionSpec as P

PATCH = 128
STRIDE = 64
HALF = 32
RATE = 0.25

MESH = pl.DeviceIdType.MESH
CORNERS = [(dy, dx) for dy in (-1, 1) for dx in (-1, 1)]
DIRECTIONS = [(dy, dx) for dy in (-1, 0, 1) for dx in (-1, 0, 1) if (dy, dx) != (0, 0)]
F32 = jnp.float32
BF16 = jnp.bfloat16


def split_table(table):
    high = table.astype(ml_dtypes.bfloat16)
    low = (table - high.astype(np.float64)).astype(ml_dtypes.bfloat16)
    return high, low


def tables():
    half = PATCH // 2
    point = np.arange(PATCH)
    angle = 2.0 * np.pi / PATCH
    packed = np.zeros((PATCH, PATCH))
    for k in range(half):
        packed[k] = np.cos(angle * (k * point % PATCH))
        packed[half + k] = np.sin(angle * (k * point % PATCH))
    packed[half] = np.cos(np.pi * point)
    weight = np.full(PATCH, 2.0)
    weight[0] = weight[half] = 1.0
    inverse = packed.T * weight[None, :] / PATCH

    def left(table):
        high, low = split_table(table)
        return np.block([[high, high], [low, low]])

    def right(table):
        high, low = split_table(table)
        return np.block([[high, low], [high, low]])

    scale = np.log2(np.e) / PATCH
    return np.stack(
        [right(packed.T), left(packed), left(inverse), right(inverse.T * scale)]
    ).astype(ml_dtypes.bfloat16)


def split(value):
    high = value.astype(BF16)
    low = (value - high.astype(F32)).astype(BF16)
    return high, low


def product(own, turned, other):
    half = PATCH // 2
    lane = lax.broadcasted_iota(jnp.int32, (half, PATCH), 1)
    row = lax.broadcasted_iota(jnp.int32, (half, PATCH), 0)
    left = lane < half
    alone = (lane == 0) | (lane == half)
    plain = left | alone
    top_row = row[:8] == 0

    def first_row(value, rest):
        head = jnp.where(top_row, value[:8], rest[:8])
        return jnp.concatenate([head, rest[8:]], axis=0)

    none = jnp.zeros((8, PATCH), F32)
    t, u = own[:half], own[half:]
    t2, u2 = other[:half], other[half:]
    rt, ru = turned[:half], turned[half:]
    uu, uru = u * u2, ru * u2
    g = t * t2 + first_row(none, uu)
    h = rt * t2 + first_row(none, uru)
    g2 = first_row(uu, t * u2 - u * t2)
    h2 = first_row(uru, rt * u2 - ru * t2)

    def joined(g, h):
        cross = pltpu.roll(jnp.where(left, h, g), half, 1)
        cross = jnp.where(alone, 0.0, cross)
        return jnp.where(plain, g + cross, h - cross)

    top = joined(g, h)
    head = jnp.where(top_row & (lane[:8] == 0), 0.0, top[:8])
    top = jnp.concatenate([head, top[8:]], axis=0)
    return jnp.concatenate([top, joined(g2, h2)], axis=0)


def moments(scores):
    peak = jnp.max(jnp.max(scores, axis=0, keepdims=True), axis=1, keepdims=True)
    terms = jnp.exp2(scores - peak)
    total = None
    for g in range(PATCH // 8):
        part = terms[8 * g : 8 * g + 8]
        steps = float(g if g < PATCH // 16 else g - PATCH // 8)
        total = part if total is None else total + part
        first = part * steps if g == 0 else first + part * steps
    sub = lax.broadcasted_iota(jnp.int32, (8, PATCH), 0).astype(F32)
    lane = lax.broadcasted_iota(jnp.int32, (8, PATCH), 1)
    lag = jnp.where(lane < PATCH // 2, lane, lane - PATCH).astype(F32)
    return [
        jnp.sum(value, axis=0, keepdims=True)
        for value in (total, first * 8.0 + total * sub, total * lag)
    ]


def relax(flow, inside):
    def lap(value):
        return (
            pltpu.roll(value, 1, 0)
            + pltpu.roll(value, 7, 0)
            + pltpu.roll(value, 1, 1)
            + pltpu.roll(value, PATCH - 1, 1)
            - 4.0 * value
        )

    first = flow + RATE * (lap(flow) + flow - flow)
    first = jnp.where(inside, first, 0.0)
    return first + RATE * (lap(first) + flow - first)


def kernel(
    sizes, x_ref, tables_ref, out_ref, own, nxt, own_hi, own_lo, nxt_hi, nxt_lo, spec, table,
    stats, flows, around, meshes,
    own_pack, own_land, nxt_pack, nxt_land, own_rest, nxt_rest, edges, tips, own_tips, nxt_tips,
    local_sem, piece_send, piece_recv, own_send, own_recv, nxt_send, nxt_recv, straight_send,
    tip_send, own_tip_recv, nxt_tip_recv,
    flow_send, flow_recv, mesh_send, mesh_recv,
):
    n_sec, n_ty, n_tx = sizes
    rows, cols = x_ref.shape
    node_rows, node_cols = rows // STRIDE, cols // STRIDE
    wide = node_cols * PATCH
    sec, ty, tx = lax.axis_index("sec"), lax.axis_index("ty"), lax.axis_index("tx")

    def there(dy, dx):
        ok = jnp.bool_(True)
        if dy:
            ok = (ty + dy >= 0) & (ty + dy < n_ty)
        if dx:
            in_x = (tx + dx >= 0) & (tx + dx < n_tx)
            ok = ok & in_x if dy else in_x
        return ok

    has_next = sec < n_sec - 1
    has_before = sec > 0

    def crosses(dy):
        return (ty % 2 == 1) if dy > 0 else (ty % 2 == 0)

    bands = (rows - 2 * HALF) // STRIDE
    odd_core = ty % 2 == 1

    def mirrored(k, count=bands):
        return jnp.where(odd_core, count - 1 - k, k)

    def straight(dy):
        return crosses(dy) & there(dy, 0)

    barrier = pltpu.get_barrier_semaphore()

    def greet(ok, s, y, x):
        @pl.when(ok)
        def _():
            pl.semaphore_signal(barrier, inc=1, device_id=(s, y, x), device_id_type=MESH)

    for dy, dx in DIRECTIONS:
        greet(there(dy, dx), sec, ty + dy, tx + dx)
    for dy in (-1, 1):
        greet(has_next & straight(dy), sec + 1, ty + dy, tx)
    for dy, dx in CORNERS:
        greet(has_next & there(dy, dx), sec + 1, ty + dy, tx + dx)
    greet(has_next, sec + 1, ty, tx)
    for d in range(1, n_sec):
        greet(sec - d >= 0, sec - d, ty, tx)

    tile = pltpu.make_async_copy(
        x_ref, own.at[pl.ds(HALF, rows), pl.ds(PATCH, cols)], local_sem.at[0]
    )
    tile.start()
    load = pltpu.make_async_copy(tables_ref, table, local_sem.at[1])
    load.start()

    for ref in (own, nxt):
        @pl.when(ty == 0)
        def _(ref=ref):
            ref[0:HALF, :] = jnp.zeros((HALF, cols + 2 * PATCH), F32)

        @pl.when(ty == n_ty - 1)
        def _(ref=ref):
            ref[HALF + rows : 2 * HALF + rows, :] = jnp.zeros((HALF, cols + 2 * PATCH), F32)

        @pl.when(tx == 0)
        def _(ref=ref):
            ref[:, 0:PATCH] = jnp.zeros((2 * HALF + rows, PATCH), F32)

        @pl.when(tx == n_tx - 1)
        def _(ref=ref):
            ref[:, PATCH + cols :] = jnp.zeros((2 * HALF + rows, PATCH), F32)

    for index, (dy, dx) in enumerate(DIRECTIONS):
        @pl.when(jnp.logical_not(there(-dy, -dx)))
        def _(index=index):
            around[index] = jnp.zeros((8, PATCH), F32)

    for t in range(n_sec):
        @pl.when(t >= sec)
        def _(t=t):
            meshes[t] = jnp.zeros((8, PATCH), F32)

    span = rows // 4
    spans = [(HALF + span * q, span) for q in range(4)]

    def turned(value, by):
        return pltpu.roll(value, by % PATCH, 1) if by % PATCH else value

    def packed(source, where, side):
        lane = lax.broadcasted_iota(jnp.int32, (where[0][1], PATCH), 1)
        at, first = ((PATCH, 0), (cols, PATCH - HALF))[side]
        value = None
        for q, (r, nr) in enumerate(where):
            part = turned(source[r : r + nr, at : at + PATCH], HALF * q - first)
            value = part if q == 0 else jnp.where(lane >= HALF * q, part, value)
        return value

    def unpack(value, target, where, side):
        at, first = ((PATCH + cols, 0), (0, PATCH - HALF))[side]
        for q, (r, nr) in enumerate(where):
            target[r : r + nr, at : at + PATCH] = turned(value, first - HALF * q)

    def unpack_columns(land, target):
        for side in range(2):
            @pl.when(there(0, 1 - 2 * side))
            def _(side=side):
                unpack(land[side], target, spans, side)

    def eighths(start):
        return [(start + 8 * q, 8) for q in range(4)]

    def unpack_tip(land, target, k):
        dy, dx = CORNERS[k]
        unpack(land[k], target, eighths(HALF + rows if dy < 0 else 0), (dx + 1) // 2)

    def pack_rest(m):
        lane = lax.broadcasted_iota(jnp.int32, (STRIDE, PATCH), 1)
        r = 2 * HALF + m * STRIDE
        left = own[r : r + STRIDE, PATCH : 2 * PATCH]
        right = own[r : r + STRIDE, cols : cols + PATCH]
        own_rest[m, 0:STRIDE] = jnp.where(lane < PATCH - HALF, right, left)
        own_rest[m, STRIDE : STRIDE + HALF] = jnp.where(
            lane[:HALF] < STRIDE, turned(left[:HALF], -HALF), turned(left[HALF:], HALF)
        )
        left = own[r : r + STRIDE, 2 * PATCH : 3 * PATCH]
        right = own[r : r + STRIDE, 3 * PATCH : 4 * PATCH]
        lane = lane[:HALF]
        low = jnp.where(lane < HALF, left[:HALF], turned(left[HALF:], HALF))
        high = jnp.where(lane < PATCH - HALF, turned(right[:HALF], -HALF), right[HALF:])
        own_rest[m, STRIDE + HALF : STRIDE + 2 * HALF] = jnp.where(lane < STRIDE, low, high)

    def unpack_rest(m):
        lane = lax.broadcasted_iota(jnp.int32, (HALF, PATCH), 1)
        for h in range(2):
            r = HALF + m * STRIDE + h * HALF
            q, start = r // span, r % span
            border = [nxt_pack[side, start : start + HALF] for side in range(2)]
            main = nxt_rest[m, h * HALF : (h + 1) * HALF]
            half = turned(nxt_rest[m, STRIDE : STRIDE + HALF], HALF if h == 0 else -HALF)
            left = jnp.where(lane < PATCH - HALF, half, main)
            left = jnp.where(lane < HALF, turned(border[0], -HALF * q), left)
            right = jnp.where(lane < PATCH - HALF, main, turned(border[1], PATCH - HALF - HALF * q))
            nxt[HALF + r : 2 * HALF + r, PATCH : 2 * PATCH] = left
            nxt[HALF + r : 2 * HALF + r, cols : cols + PATCH] = right

    def unpack_edges(m):
        strip = nxt_rest[m, STRIDE + HALF : STRIDE + 2 * HALF]
        edges[0] = jnp.concatenate([strip, turned(strip, -HALF)], axis=0)
        edges[1] = jnp.concatenate([turned(strip, HALF), strip], axis=0)

    def at_band(k, do):
        for m in range(bands):
            @pl.when(mirrored(k) == m)
            def _(m=m):
                do(m)

    tile.wait()
    stats[...] = jnp.ones_like(stats)
    for side in range(2):
        own_pack[side] = packed(own, spans, side)
    for k, (dy, dx) in enumerate(CORNERS):
        tips[k] = packed(own, eighths(HALF if dy < 0 else rows), (dx + 1) // 2)
    for m in range(bands):
        pack_rest(m)

    tall = 1 + (ty > 0).astype(jnp.int32) + (ty < n_ty - 1).astype(jnp.int32)
    broad = 1 + (tx > 0).astype(jnp.int32) + (tx < n_tx - 1).astype(jnp.int32)
    apart = (crosses(-1) & there(-1, 0)).astype(jnp.int32) + (crosses(1) & there(1, 0)).astype(jnp.int32)
    back = has_before.astype(jnp.int32) * (1 + apart + (tall - 1) * (broad - 1))
    pl.semaphore_wait(barrier, tall * broad - 1 + back + n_sec - 1 - sec)

    banded = [mirrored(m) for m in range(bands)]

    def band_rest(m, last):
        return (banded[m], STRIDE + 2 * HALF if last else STRIDE + HALF)

    def band_inner(m):
        return (pl.multiple_of(HALF + banded[m] * STRIDE, HALF), STRIDE, PATCH, 2 * PATCH)

    pieces = [(0, HALF, 0, cols), (rows - HALF, HALF, 0, cols), None]
    for m in range(bands):
        pieces += [band_rest(m, m == bands - 1), band_inner(m)]

    def piece_copy(p):
        piece = pieces[p]
        if piece is None:
            src, dst = own_pack, nxt_pack
        elif len(piece) == 2:
            m, nr = piece
            src, dst = own_rest.at[m, pl.ds(0, nr)], nxt_rest.at[m, pl.ds(0, nr)]
        else:
            r, nr, c, nc = piece
            src = x_ref.at[pl.ds(r, nr), pl.ds(c, nc)]
            to = HALF + r if isinstance(r, int) else pl.multiple_of(HALF + r, HALF)
            dst = nxt.at[pl.ds(to, nr), pl.ds(PATCH + c, nc)]
        return pltpu.make_async_remote_copy(
            src_ref=src,
            dst_ref=dst,
            send_sem=piece_send.at[p],
            recv_sem=piece_recv.at[p],
            device_id=(sec - 1, ty, tx),
            device_id_type=MESH,
        )

    def arrived(*indices):
        @pl.when(has_next)
        def _():
            for p in indices:
                piece_copy(p).wait_recv()

    def edge(dy):
        return (0, HALF + rows) if dy < 0 else (rows - HALF, 0)

    def row_copy(dy, through, target, send, recv, to_sec):
        r, to = edge(dy)
        if through is None:
            src = x_ref.at[pl.ds(r, HALF)]
        else:
            src = through.at[pl.ds(HALF + r, HALF), pl.ds(PATCH, cols)]
        side = (dy + 1) // 2
        return pltpu.make_async_remote_copy(
            src_ref=src,
            dst_ref=target.at[pl.ds(to, HALF), pl.ds(PATCH, cols)],
            send_sem=send.at[side],
            recv_sem=recv.at[side],
            device_id=(to_sec, ty + dy, tx),
            device_id_type=MESH,
        )

    def column_copy(dx, pack, land, send, recv):
        side = (dx + 1) // 2
        return pltpu.make_async_remote_copy(
            src_ref=pack.at[side],
            dst_ref=land.at[side],
            send_sem=send.at[2 + side],
            recv_sem=recv.at[2 + side],
            device_id=(sec, ty, tx + dx),
            device_id_type=MESH,
        )

    def own_rows(dy):
        return row_copy(dy, None, own, own_send, own_recv, sec)

    def own_columns(dx):
        return column_copy(dx, own_pack, own_land, own_send, own_recv)

    def nxt_rows(dy):
        return row_copy(dy, nxt, nxt, nxt_send, nxt_recv, sec)

    def nxt_straight(dy):
        return row_copy(dy, None, nxt, straight_send, nxt_recv, sec - 1)

    def nxt_columns(dx):
        return column_copy(dx, nxt_pack, nxt_land, nxt_send, nxt_recv)

    def tip_copy(k, section):
        dy, dx = CORNERS[k]
        return pltpu.make_async_remote_copy(
            src_ref=tips.at[k],
            dst_ref=(own_tips, nxt_tips)[section].at[k],
            send_sem=tip_send.at[section, k],
            recv_sem=(own_tip_recv, nxt_tip_recv)[section].at[k],
            device_id=(sec - section, ty + dy, tx + dx),
            device_id_type=MESH,
        )

    def diagonals(sign, do):
        for k, (dy, dx) in enumerate(CORNERS):
            @pl.when(there(sign * dy, sign * dx))
            def _(k=k):
                do(k)

    def up_down(ok, do):
        for dy in (-1, 1):
            @pl.when(ok(dy))
            def _(dy=dy):
                do(dy)

    def sides(sign, do):
        for dx in (-1, 1):
            @pl.when(there(0, sign * dx))
            def _(dx=dx):
                do(dx)

    def handed_on(dy):
        return jnp.logical_not(crosses(dy)) & there(dy, 0)

    up_down(lambda dy: there(dy, 0), lambda dy: own_rows(dy).start())
    sides(1, lambda dx: own_columns(dx).start())
    diagonals(1, lambda k: tip_copy(k, 0).start())

    @pl.when(has_before)
    def _():
        diagonals(1, lambda k: tip_copy(k, 1).start())
        up_down(straight, lambda dy: nxt_straight(dy).start())

        @pl.when(crosses(-1))
        def _():
            piece_copy(1).start()

        @pl.when(jnp.logical_not(crosses(-1)))
        def _():
            piece_copy(0).start()

        piece_copy(2).start()

        @pl.when(crosses(-1))
        def _():
            piece_copy(0).start()

        @pl.when(jnp.logical_not(crosses(-1)))
        def _():
            piece_copy(1).start()

        for p in range(3, len(pieces)):
            piece_copy(p).start()

    load.wait()

    lane = lax.broadcasted_iota(jnp.int32, (STRIDE, PATCH), 1)
    even, odd = lane < PATCH - HALF, lane >= HALF

    order = [node_cols - 2, node_cols - 1, *range(node_cols - 2)]
    part_cols = node_cols // 2
    parts = (range(0, part_cols), range(part_cols, node_cols))
    every = range(node_cols)

    def right_chunk(source, high, low, b, places, ahead=False):
        at = pl.ds(b * STRIDE if isinstance(b, int) else pl.multiple_of(b * STRIDE, STRIDE), STRIDE)
        patches = []
        for j in (order[p] for p in places):
            t = j // 2
            main = source[at, (t + 1) * PATCH : (t + 2) * PATCH]
            beside = t if j % 2 == 0 else t + 2
            if ahead and j in (1, node_cols - 2):
                part = edges[0 if j == 1 else 1]
            else:
                part = source[at, beside * PATCH : (beside + 1) * PATCH]
            patch = jnp.where(even if j % 2 == 0 else odd, main, part)
            patches.append(jnp.concatenate(split(patch), axis=1))
        got = jnp.dot(jnp.concatenate(patches, axis=0), table[0], preferred_element_type=F32)
        got = got[:, :PATCH] + got[:, PATCH:]
        for n, p in enumerate(places):
            hi, lo = split(got[n * STRIDE : (n + 1) * STRIDE])
            high[at, p * PATCH : (p + 1) * PATCH] = hi
            low[at, p * PATCH : (p + 1) * PATCH] = lo

    def left_spectrum(high, low, i, columns):
        at = pl.ds(pl.multiple_of(i * STRIDE, STRIDE), PATCH)
        both = jnp.concatenate([high[at, columns], low[at, columns]], axis=0)
        got = jnp.dot(table[1], both, preferred_element_type=F32)
        return got[:PATCH] + got[PATCH:]


    def hand_on(dy):
        piece_copy((dy + 1) // 2).wait_recv()
        nxt_rows(dy).start()

    up_down(lambda dy: there(-dy, 0), lambda dy: own_rows(dy).wait_recv())
    sides(-1, lambda dx: own_columns(dx).wait_recv())
    diagonals(-1, lambda k: tip_copy(k, 0).wait_recv())
    unpack_columns(own_land, own)
    diagonals(-1, lambda k: unpack_tip(own_tips, own, k))

    @pl.when(has_next)
    def _():
        up_down(handed_on, hand_on)

    @pl.loop(0, node_rows + 1)
    def _(b):
        right_chunk(own, own_hi, own_lo, b, every)

    @pl.when(has_next)
    def _():
        piece_copy(2).wait_recv()
        sides(1, lambda dx: nxt_columns(dx).start())

    @pl.loop(0, node_rows)
    def _(i):
        for c in range(0, wide, 2 * PATCH):
            at = pl.ds(c, 2 * PATCH)
            got = left_spectrum(own_hi, own_lo, i, at)
            spec[i, 0, :, at] = got
            for n in range(2):
                spec[i, 1, :, pl.ds(c + n * PATCH, PATCH)] = pltpu.roll(
                    got[:, n * PATCH : (n + 1) * PATCH], PATCH // 2, 1
                )

    @pl.when(has_next)
    def _():
        for dy in (-1, 1):
            @pl.when(jnp.logical_not(handed_on(dy)))
            def _(dy=dy):
                piece_copy((dy + 1) // 2).wait_recv()

        up_down(lambda dy: there(-dy, 0), lambda dy: nxt_rows(dy).wait_recv())
        diagonals(-1, lambda k: tip_copy(k, 1).wait_recv())
        diagonals(-1, lambda k: unpack_tip(nxt_tips, nxt, k))
        sides(-1, lambda dx: nxt_columns(dx).wait_recv())
        unpack_columns(nxt_land, nxt)

    right_chunk(nxt, nxt_hi, nxt_lo, 0, every)
    right_chunk(nxt, nxt_hi, nxt_lo, node_rows, every)

    lanes = lax.broadcasted_iota(jnp.int32, (8, PATCH), 1)

    def flow_block(indices):
        columns = jnp.zeros((8, PATCH), F32)
        for i in indices:
            total, down, across = (jnp.sum(stats[q, i], axis=1, keepdims=True) for q in range(3))
            inv = 1.0 / total
            columns = jnp.where(lanes == i, down * inv, columns)
            columns = jnp.where(lanes == node_rows + i, across * inv, columns)
        columns = pltpu.roll(jnp.where(has_next, columns, 0.0), node_cols - 2, 0)
        return jnp.transpose(jnp.concatenate([columns] * 16, axis=0))[:8]

    def flow_stage(dy, dx):
        if dy == 0:
            return 2
        return jnp.where(crosses(dy), 1, 0 if dx == 0 else 2)

    def flow_copy(index):
        dy, dx = DIRECTIONS[index]
        return pltpu.make_async_remote_copy(
            src_ref=flows.at[flow_stage(dy, dx)],
            dst_ref=around.at[index],
            send_sem=flow_send.at[index],
            recv_sem=flow_recv.at[index],
            device_id=(sec, ty + dy, tx + dx),
            device_id_type=MESH,
        )

    def flow_each(sign, do, stage=None):
        for index, (dy, dx) in enumerate(DIRECTIONS):
            ok = there(sign * dy, sign * dx)
            if stage is not None:
                ok = ok & (flow_stage(dy, dx) == stage)

            @pl.when(ok)
            def _(index=index):
                do(index)

    def flow_send_stage(stage):
        flows[stage] = flow_block(range(node_rows))
        flow_each(1, lambda k: flow_copy(k).start(), stage)

    @pl.loop(0, 4)
    def _(step):
        @pl.when(step == 0)
        def _():
            arrived(3, 4)
            at_band(0, unpack_rest)

        @pl.when(step == 1)
        def _():
            arrived(5, 6)
            at_band(1, unpack_rest)

        @pl.when(step < 2)
        def _():
            right_chunk(nxt, nxt_hi, nxt_lo, 1 + mirrored(step), every)

        @pl.when(step == 2)
        def _():
            flow_send_stage(1)
            arrived(7)
            at_band(2, unpack_rest)
            at_band(2, unpack_edges)
            right_chunk(nxt, nxt_hi, nxt_lo, 1 + mirrored(2), parts[0], True)

        @pl.when(step == 3)
        def _():
            flow_send_stage(2)
            arrived(8)
            right_chunk(nxt, nxt_hi, nxt_lo, 1 + mirrored(2), parts[1])

        halves = [
            (mirrored(jnp.where(step < 2, step, 2 + h), node_rows), jnp.where(step < 2, h, step - 2))
            for h in range(2)
        ]
        nodes = [slice(n * PATCH, (n + 1) * PATCH) for n in range(node_cols)]
        mine, swapped, other = [], [], []
        for i, g in halves:
            columns = pl.ds(pl.multiple_of(g * part_cols * PATCH, PATCH), part_cols * PATCH)
            other.append(left_spectrum(nxt_hi, nxt_lo, i, columns))
            mine.append(spec[i, 0, :, columns])
            swapped.append(spec[i, 1, :, columns])
        mine, swapped, other = (jnp.concatenate(value, axis=1) for value in (mine, swapped, other))
        prods = jnp.concatenate([product(mine[:, n], swapped[:, n], other[:, n]) for n in nodes], axis=1)
        mixed = jnp.dot(
            table[2], jnp.concatenate(split(prods), axis=0), preferred_element_type=F32
        )
        hi, lo = split(mixed[:PATCH] + mixed[PATCH:])
        stacked = jnp.concatenate(
            [jnp.concatenate([hi[:, n], lo[:, n]], axis=1) for n in nodes], axis=0
        )
        corr = jnp.dot(stacked, table[3], preferred_element_type=F32)
        corr = corr[:, :PATCH] + corr[:, PATCH:]
        found = [moments(corr[n]) for n in nodes]
        for h, (i, g) in enumerate(halves):
            for q in range(3):
                stats[q, i, pl.ds(g * part_cols, part_cols), :] = jnp.concatenate(
                    [f[q] for f in found[h * part_cols : (h + 1) * part_cols]], axis=0
                )

    block = flow_block(range(node_rows))
    flows[0] = block
    flow_each(1, lambda k: flow_copy(k).start(), 0)

    up_down(lambda dy: there(dy, 0), lambda dy: own_rows(dy).wait_send())
    sides(1, lambda dx: own_columns(dx).wait_send())
    diagonals(1, lambda k: tip_copy(k, 0).wait_send())

    @pl.when(has_before)
    def _():
        for p in range(len(pieces)):
            piece_copy(p).wait_send()
        up_down(straight, lambda dy: nxt_straight(dy).wait_send())
        diagonals(1, lambda k: tip_copy(k, 1).wait_send())

    @pl.when(has_next)
    def _():
        up_down(handed_on, lambda dy: nxt_rows(dy).wait_send())
        sides(1, lambda dx: nxt_columns(dx).wait_send())

    flow_each(-1, lambda k: flow_copy(k).wait_recv())

    lines = {}
    for dy in (-1, 0, 1):
        def from_(dx, dy=dy):
            return block if (dy, dx) == (0, 0) else around[DIRECTIONS.index((-dy, -dx))]

        line = jnp.where(lanes < 2 + node_cols, pltpu.roll(from_(0), 2, 1), pltpu.roll(from_(1), 2 + node_cols, 1))
        lines[dy] = jnp.where(lanes < 2, pltpu.roll(from_(-1), PATCH + 2 - node_cols, 1), line)

    subs = lax.broadcasted_iota(jnp.int32, (8, PATCH), 0)
    row_id = ty * node_rows + subs - 2
    col_id = tx * node_cols + lanes - 2
    inside = (
        (row_id >= 0) & (row_id < node_rows * n_ty) & (col_id >= 0) & (col_id < node_cols * n_tx)
    )
    done = []
    for c in range(2):
        base = c * node_rows
        above = pltpu.roll(lines[-1], (8 - (base + node_rows - 2)) % 8, 0)
        here = pltpu.roll(lines[0], (8 + 2 - base) % 8, 0)
        below = pltpu.roll(lines[1], (8 + 2 + node_rows - base) % 8, 0)
        flow = jnp.where(subs < 2, above, jnp.where(subs < 2 + node_rows, here, below))
        done.append(pltpu.roll(relax(flow, inside), PATCH - 2, 1))
    result = jnp.where(
        subs < node_rows, pltpu.roll(done[0], 6, 0), pltpu.roll(done[1], (8 + node_rows - 2) % 8, 0)
    )
    flows[3] = result

    def mesh_copy(d):
        return pltpu.make_async_remote_copy(
            src_ref=flows.at[3],
            dst_ref=meshes.at[sec],
            send_sem=mesh_send.at[d],
            recv_sem=mesh_recv.at[d],
            device_id=(sec + d, ty, tx),
            device_id_type=MESH,
        )

    def mesh_wait(d):
        pltpu.make_async_remote_copy(
            src_ref=flows.at[3],
            dst_ref=meshes.at[sec - d],
            send_sem=mesh_send.at[d],
            recv_sem=mesh_recv.at[d],
            device_id=(sec - d, ty, tx),
            device_id_type=MESH,
        ).wait_recv()

    for d in range(1, n_sec):
        @pl.when(sec + d < n_sec)
        def _(d=d):
            mesh_copy(d).start()
    for d in range(1, n_sec):
        @pl.when(sec - d >= 0)
        def _(d=d):
            mesh_wait(d)

    earlier = meshes[0]
    for t in range(1, n_sec):
        earlier = earlier + meshes[t]
    out_ref[0] = result
    out_ref[1] = earlier

    flow_each(1, lambda k: flow_copy(k).wait_send())
    for d in range(1, n_sec):
        @pl.when(sec + d < n_sec)
        def _(d=d):
            mesh_copy(d).wait_send()


def solution(mesh):
    sizes = tuple(mesh.shape[axis] for axis in ("sec", "ty", "tx"))

    def on_device(images):
        image = images[0]
        rows, cols = image.shape
        node_rows, node_cols = rows // STRIDE, cols // STRIDE
        high = 2 * HALF + rows
        wide = node_cols * PATCH
        around = len(DIRECTIONS)
        bands = (rows - 2 * HALF) // STRIDE
        n_pieces = 3 + 2 * bands
        dma = pltpu.SemaphoreType.DMA
        out = pl.pallas_call(
            functools.partial(kernel, sizes),
            out_shape=jax.ShapeDtypeStruct((2, 8, PATCH), F32),
            in_specs=[pl.BlockSpec(memory_space=pl.ANY)] * 2,
            out_specs=pl.BlockSpec(memory_space=pltpu.VMEM),
            scratch_shapes=[
                pltpu.VMEM((high, cols + 2 * PATCH), F32),
                pltpu.VMEM((high, cols + 2 * PATCH), F32),
                pltpu.VMEM((high, wide), BF16),
                pltpu.VMEM((high, wide), BF16),
                pltpu.VMEM((high, wide), BF16),
                pltpu.VMEM((high, wide), BF16),
                pltpu.VMEM((node_rows, 2, PATCH, wide), F32),
                pltpu.VMEM((4, 2 * PATCH, 2 * PATCH), BF16),
                pltpu.VMEM((3, node_rows, node_cols, PATCH), F32),
                pltpu.VMEM((4, 8, PATCH), F32),
                pltpu.VMEM((around, 8, PATCH), F32),
                pltpu.VMEM((sizes[0], 8, PATCH), F32),
                pltpu.VMEM((2, rows // 4, PATCH), F32),
                pltpu.VMEM((2, rows // 4, PATCH), F32),
                pltpu.VMEM((2, rows // 4, PATCH), F32),
                pltpu.VMEM((2, rows // 4, PATCH), F32),
                pltpu.VMEM((bands, STRIDE + 2 * HALF, PATCH), F32),
                pltpu.VMEM((bands, STRIDE + 2 * HALF, PATCH), F32),
                pltpu.VMEM((2, STRIDE, PATCH), F32),
                pltpu.VMEM((len(CORNERS), 8, PATCH), F32),
                pltpu.VMEM((len(CORNERS), 8, PATCH), F32),
                pltpu.VMEM((len(CORNERS), 8, PATCH), F32),
                dma((2,)),
                dma((n_pieces,)),
                dma((n_pieces,)),
                dma((4,)),
                dma((4,)),
                dma((4,)),
                dma((4,)),
                dma((2,)),
                dma((2, len(CORNERS))),
                dma((len(CORNERS),)),
                dma((len(CORNERS),)),
                dma((around,)),
                dma((around,)),
                dma((sizes[0],)),
                dma((sizes[0],)),
            ],
            compiler_params=pltpu.CompilerParams(
                collective_id=0, has_side_effects=True, vmem_limit_bytes=60 * 1024 * 1024
            ),
        )(image, jnp.asarray(tables()))
        out = out[:, :, :node_cols].reshape(2, 1, 2, node_rows, node_cols)
        return out[0], out[1]

    return jax.shard_map(
        on_device,
        mesh=mesh,
        in_specs=(P("sec", "ty", "tx"),),
        out_specs=(P("sec", None, "ty", "tx"), P("sec", None, "ty", "tx")),
        check_vma=False,
    )
```
